128 devices in a mesh: section: 8 (over y, core), tok: 16 (over x, z).
Axes of the slice: x: 4, y: 4, z: 4, core: 2. Of those that a mesh axis runs over, the one named last changes fastest.
Arguments:
- coords: float32 [8, 3, 3456], P('section', None, 'tok'), may hold values from -6 to 6
- atom_single: bfloat16 [3456, 128], P('tok'), may hold values from -6 to 6
- token_atoms: int32 [384], P('tok'), may hold values from 1 to 24, as said below
- cond_single: bfloat16 [384, 768], P('tok'), may hold values from -6 to 6
- pair_bias: bfloat16 [8, 16, 384, 384], P('section', None, 'tok'), may hold values from -4 to 330
- w_coord: float32 [3, 128], replicated, may hold values from -4 to 4
- w_in: bfloat16 [128, 768], replicated, may hold values from -1.5 to 1.5
- w_ada: bfloat16 [8, 768, 3072], P('section'), may hold values from -0.21875 to 0.21875
- w_qkv: bfloat16 [8, 768, 2304], P('section'), may hold values from -0.21875 to 0.21875
- w_out: bfloat16 [8, 768, 768], P('section'), may hold values from -0.21875 to 0.21875
- w_ff: bfloat16 [8, 768, 3072], P('section'), may hold values from -0.21875 to 0.21875
- w_down: bfloat16 [8, 1536, 768], P('section'), may hold values from -0.15625 to 0.15625
Outputs:
- token_out: bfloat16 [8, 384, 768], P('section', 'tok')
The draws below stay inside these ranges and needn't reach their ends.
Inputs may be any that keep to these rules, and one draw needn't show every extreme that they name: `token_atoms`: the first 192 tokens each have 10 to 24 atoms; the later tokens are single-atom ligand tokens.
All inputs are finite; a program needn't handle non-finite values.
Results may differ from the reference program's by a relative error of at most 0.02.
Values may be sent and summed in bfloat16 or wider, within the bound.
A program may use at most 64 MiB of HBM per device.

```python
import jax
import jax.numpy as jnp
from jax import lax

D = 768
HEADS = 16
HEAD_DIM = 48
FF = 1536
C_ATOM = 128
MOST_ATOMS = 24
TOKENS = 384
ATOMS = 3456
POSES = 8
LAYERS = 8


def draw_token_atoms(key, part):
    key = jax.random.fold_in(key, 5)
    half = TOKENS // 2
    pairs = half // 2
    spread = MOST_ATOMS - 17
    offsets = jax.random.randint(key, (pairs,), -spread, spread + 1)
    offsets = offsets.at[0].set(spread)
    residues = jnp.stack([17 + offsets, 17 - offsets], axis=1).reshape(half)
    singles = jnp.ones((half,), jnp.int32)
    return jnp.concatenate([residues.astype(jnp.int32), singles]).astype(jnp.int32)


def draw_pair_bias(key, part):
    key = jax.random.fold_in(key, 11)
    shape = (LAYERS, HEADS, TOKENS, TOKENS)
    base = jax.random.normal(key, shape, jnp.float32)
    return jnp.clip(base, -4.0, 4.0).astype(jnp.bfloat16)


def block_scale(stream_key, dims, split, low, high):
    def one(dim, parts):
        steps = jax.random.uniform(jax.random.fold_in(jax.random.fold_in(stream_key, 6), dim), (parts,), jnp.float32, low / len(split), high / len(split))
        return jnp.repeat(jnp.exp(steps), dims[dim] // parts).reshape((-1,) + (1,) * (len(dims) - dim - 1))

    level = one(*split[0])
    for cut in split[1:]:
        level = level * one(*cut)
    return level


def noise(key, extent, scale, most, pieces=(), held_as=jnp.bfloat16):
    entries = scale * jax.random.normal(key, extent, jnp.float32)
    if pieces:
        entries = entries * block_scale(key, extent, pieces, -0.22, 0.18)
    return jnp.clip(entries, -most, most).astype(held_as)


def setup_inputs(seed: int = 0) -> dict:
    seeds = jax.random.split(jax.random.key(seed), 13)
    coords = noise(seeds[0], (POSES, 3, ATOMS), 1.0, 6.0, ((0, 8), (2, 16)), jnp.float32)
    atom_single = noise(seeds[1], (ATOMS, C_ATOM), 1.0, 6.0, ((0, 16),))
    token_atoms = draw_token_atoms(jax.random.fold_in(seeds[12], 71), 0)
    cond_single = noise(seeds[3], (TOKENS, D), 1.0, 6.0, ((0, 16),))
    pair_bias = draw_pair_bias(jax.random.fold_in(seeds[12], 71), 0)
    w_coord = noise(seeds[5], (3, C_ATOM), 1.0, 4.0, (), jnp.float32)
    w_in = noise(seeds[6], (C_ATOM, D), (C_ATOM // 9) ** -0.5, 1.5)
    w_ada = noise(seeds[7], (LAYERS, D, 4 * D), D ** -0.5, 0.21875, ((0, 8),))
    w_qkv = noise(seeds[8], (LAYERS, D, 3 * D), D ** -0.5, 0.21875, ((0, 8),))
    w_out = noise(seeds[9], (LAYERS, D, D), D ** -0.5, 0.21875, ((0, 8),))
    w_ff = noise(seeds[10], (LAYERS, D, 2 * FF), D ** -0.5, 0.21875, ((0, 8),))
    w_down = noise(seeds[11], (LAYERS, FF, D), FF ** -0.5, 0.15625, ((0, 8),))
    return {"coords": coords, "atom_single": atom_single, "token_atoms": token_atoms, "cond_single": cond_single, "pair_bias": pair_bias, "w_coord": w_coord, "w_in": w_in, "w_ada": w_ada, "w_qkv": w_qkv, "w_out": w_out, "w_ff": w_ff, "w_down": w_down}


def layer_norm(values):
    centre = values - lax.optimization_barrier(jnp.mean(values, axis=-1, keepdims=True))
    return centre * lax.rsqrt(lax.optimization_barrier(jnp.mean(centre * centre, axis=-1, keepdims=True)) + 1e-05)

def token_layer(state, conditioning, bias, weight_qkv, weight_out, weight_ff, weight_down):
    width = state.shape[-1]
    scale_attn = conditioning[:, :width]
    shift_attn = conditioning[:, width:2 * width]
    scale_trans = conditioning[:, 2 * width:3 * width]
    shift_trans = conditioning[:, 3 * width:]
    normed = (layer_norm(state) * jax.nn.sigmoid(scale_attn) + shift_attn).astype(jnp.bfloat16)
    projected = jnp.dot(normed, weight_qkv, preferred_element_type=jnp.float32).astype(jnp.bfloat16)
    queries = projected[:, :width].reshape(-1, HEADS, HEAD_DIM).astype(jnp.float32)
    keys_all = projected[:, width:2 * width].reshape(-1, HEADS, HEAD_DIM).astype(jnp.float32)
    values_all = projected[:, 2 * width:].reshape(-1, HEADS, HEAD_DIM).astype(jnp.float32)
    scores = jnp.einsum('ihd,jhd->hij', queries, keys_all) * HEAD_DIM ** (-0.5) + bias.astype(jnp.float32)
    probs = jax.nn.softmax(scores, axis=-1).astype(jnp.bfloat16)
    attended = jnp.einsum('hij,jhd->ihd', probs.astype(jnp.float32), values_all)
    attended = attended.reshape(-1, width).astype(jnp.bfloat16)
    state = state + jnp.dot(attended, weight_out, preferred_element_type=jnp.float32)
    normed_t = (layer_norm(state) * jax.nn.sigmoid(scale_trans) + shift_trans).astype(jnp.bfloat16)
    gate_up = jnp.dot(normed_t, weight_ff, preferred_element_type=jnp.float32)
    hidden = (jax.nn.silu(gate_up[:, :FF]) * gate_up[:, FF:]).astype(jnp.bfloat16)
    return state + jnp.dot(hidden, weight_down, preferred_element_type=jnp.float32)

def reference(coords, atom_single, token_atoms, cond_single, pair_bias, w_coord, w_in, w_ada, w_qkv, w_out, w_ff, w_down):
    atom_token = jnp.repeat(jnp.arange(TOKENS, dtype=jnp.int32), token_atoms, total_repeat_length=ATOMS).astype(jnp.int32)
    counts_float = token_atoms.astype(jnp.float32)[:, None]
    conditions = [jnp.dot(cond_single, w_ada[layer_index], preferred_element_type=jnp.float32) for layer_index in range(LAYERS)]
    results_list = []
    for pose_index in range(POSES):
        points = coords[pose_index]
        atom_act = atom_single.astype(jnp.float32) + points[0][:, None] * w_coord[0][None, :] + points[1][:, None] * w_coord[1][None, :] + points[2][:, None] * w_coord[2][None, :]
        atom_act = jax.nn.relu(atom_act).astype(jnp.bfloat16)
        pooled = jax.ops.segment_sum(atom_act.astype(jnp.float32), atom_token, num_segments=TOKENS)
        averaged = (pooled / counts_float).astype(jnp.bfloat16)
        state = jnp.dot(averaged, w_in, preferred_element_type=jnp.float32)
        for layer_index in range(LAYERS):
            state = token_layer(state, conditions[layer_index], pair_bias[layer_index], w_qkv[layer_index], w_out[layer_index], w_ff[layer_index], w_down[layer_index])
        results_list.append(layer_norm(state).astype(jnp.bfloat16))
    return jnp.stack(results_list)
```

```python
import jax
import jax.numpy as jnp
from jax import lax
from jax.experimental import pallas as pl
from jax.experimental.pallas import tpu as pltpu
from jax.sharding import PartitionSpec as P

HEADS = 16
HEAD_DIM = 48
FF = 1536
D = 768
POSES = 8
TOK_DEVS = 16
SECTIONS = 8
ROWS = 192
TOK_DEV = 24
ATOM_DEV = 216
ATOM_PAD = 224
COND_PAD = 32
KEYS = 384
GROUP = 384
MESH = pl.DeviceIdType.MESH
BF = jnp.bfloat16
F32 = jnp.float32


def chip_of(pose):
    x = pose // 2
    return 4 * x + 2 * (pose % 2) + x % 2


def normalise(v):
    centre = v - jnp.mean(v, axis=-1, keepdims=True)
    return centre * lax.rsqrt(jnp.mean(centre * centre, axis=-1, keepdims=True) + 1e-05)


def landed(ref, sem):
    pltpu.make_async_copy(ref, ref, sem).wait()


def kernel(
    coords_ref, atom_ref, count_ref, cond_ref, bias_ref, wcoord_ref, win_ref,
    wada_ref, wqkv_ref, wout_ref, wff_ref, wdown_ref,
    out_ref,
    c_src, a_src, d_src, c_all, a_all, n_all, d_all, b_all,
    wada_v, wqkv_v, wout_v, wff_v, wdown_v,
    cond, cond_tx, x, xin, xtx, norm, q, kv, att, hid, fin_tx, fin,
    c_send, c_recv, a_send, a_recv, n_send, n_recv, d_send, d_recv, b_send, b_recv,
    w_send, w_recv, ada_sem, m_send, m_recv, kv_send, kv_recv, x_send, x_recv, f_send, f_recv,
):
    s = lax.axis_index("section")
    t = lax.axis_index("tok")
    plane = s // 2
    core = lax.rem(s, 2)
    sibling = s + 1 - 2 * core
    cx, cz = t // 4, lax.rem(t, 4)
    active = lax.rem(cx + cz, 2) == 0
    pose = 2 * cx + cz // 2
    half = t // 8

    weights = ((wqkv_ref, wqkv_v), (wout_ref, wout_v), (wff_ref, wff_v), (wdown_ref, wdown_v))

    @pl.when(active)
    def _():
        pltpu.make_async_copy(wada_ref, wada_v, ada_sem).start()
        for k, (src, dst) in enumerate(weights):
            pltpu.make_async_copy(src, dst.at[core], w_recv.at[core, k]).start()

    barrier = pltpu.get_barrier_semaphore()

    def greet(section, tok):
        pl.semaphore_signal(barrier, inc=1, device_id=(section, tok), device_id_type=MESH)

    @pl.when(active)
    def _():
        @pl.loop(0, TOK_DEVS)
        def _(j):
            @pl.when(j != t)
            def _():
                greet(s, j)

        @pl.loop(0, 8)
        def _(j):
            greet(sibling, 8 * core + j)

        greet(sibling, t)

        @pl.when((s == 0) & (pose != 0))
        def _():
            @pl.loop(0, TOK_DEVS)
            def _(j):
                greet(pose, j)

        @pl.when((s == 1) & (pose != 1))
        def _():
            greet(pose, TOK_DEVS - 1)

        @pl.when(plane > 0)
        def _():
            greet(s - 2, t)

    fin_section, fin_tok = 6 + half, chip_of(s)
    fin_self = (fin_section == s) & (fin_tok == t)

    @pl.when(jnp.logical_not(fin_self))
    def _():
        greet(fin_section, fin_tok)

    c_src[...] = jnp.zeros_like(c_src)
    c_src[0:3, 0:ATOM_DEV] = coords_ref[0]
    a_src[...] = jnp.concatenate(
        [atom_ref[...].astype(F32), jnp.zeros((ATOM_PAD - ATOM_DEV, 128), F32)], axis=0
    ).astype(BF)
    d_src[...] = jnp.concatenate(
        [cond_ref[...].astype(F32), jnp.zeros((COND_PAD - TOK_DEV, D), F32)], axis=0
    ).astype(BF)

    one = lambda flag: flag.astype(jnp.int32)
    last = t == TOK_DEVS - 1
    expected = 8 - one(active)
    expected += 8 * one(half != core)
    expected += one(s != 0) + one(last & (s != 1))
    expected += one(active) + one(active & (plane < 3))
    fin_here = active & (plane == 3)
    fin_own = fin_here & (pose == s) & (half == core)
    expected += 8 * one(fin_here) - one(fin_own)
    pl.semaphore_wait(barrier, expected)

    def send(src, dst, send_sem, recv_sem, section, tok):
        own = (section == s) & (tok == t)

        @pl.when(own)
        def _():
            pltpu.make_async_copy(src, dst, recv_sem).start()

        @pl.when(jnp.logical_not(own))
        def _():
            pltpu.make_async_remote_copy(
                src_ref=src, dst_ref=dst, send_sem=send_sem, recv_sem=recv_sem,
                device_id=(section, tok), device_id_type=MESH,
            ).start()

    def sent(src, send_sem, section, tok):
        @pl.when(jnp.logical_not((section == s) & (tok == t)))
        def _():
            landed(src, send_sem)

    send(c_src, c_all.at[t], c_send.at[0], c_recv.at[t], 0, chip_of(s))

    @pl.when(last)
    def _():
        send(c_src, c_all.at[t], c_send.at[1], c_recv.at[t], 1, chip_of(s))

    @pl.when((s == 0) | ((s == 1) & last))
    def _():
        @pl.loop(0, POSES)
        def _(p):
            send(a_src, a_all.at[t], a_send.at[p], a_recv.at[t], s, chip_of(p))

    @pl.when((s == 0) & (t < 8))
    def _():
        @pl.loop(0, POSES)
        def _(p):
            send(count_ref, n_all.at[t], n_send.at[p], n_recv.at[t], s, chip_of(p))

    @pl.loop(0, POSES)
    def _(p):
        send(d_src, d_all.at[t], d_send.at[p], d_recv.at[t], s, chip_of(p))

    @pl.loop(0, POSES)
    def _(p):
        send(bias_ref, b_all.at[core, t - 8 * half], b_send.at[p], b_recv.at[core, t - 8 * half],
             2 * plane + half, chip_of(p))

    @pl.when(active)
    def _():
        for k, (src, dst) in enumerate(weights):
            pltpu.make_async_remote_copy(
                src_ref=src, dst_ref=dst.at[core], send_sem=w_send.at[k],
                recv_sem=w_recv.at[core, k], device_id=(sibling, t), device_id_type=MESH,
            ).start()

    def act_of(points, single):
        moved = lax.dot_general(
            points, wcoord_ref[...], (((0,), (0,)), ((), ())),
            precision=lax.Precision.HIGHEST, preferred_element_type=F32,
        )
        return jnp.maximum(single.astype(F32) + moved[:ATOM_PAD], 0.0)

    def enter_first():
        @pl.loop(0, 8)
        def _(j):
            landed(n_all.at[j], n_recv.at[j])

        counts = jnp.concatenate([n_all[j] for j in range(8)], axis=0)
        before = (
            lax.broadcasted_iota(jnp.int32, (ROWS, ROWS), 1)
            < lax.broadcasted_iota(jnp.int32, (ROWS, ROWS), 0)
        ).astype(F32).astype(BF)
        starts = jnp.dot(before, counts.astype(BF), preferred_element_type=F32)
        ends = starts + counts
        lower = jnp.concatenate([starts, starts], axis=1)[:, :ATOM_PAD]
        upper = jnp.concatenate([ends, ends], axis=1)[:, :ATOM_PAD]
        lane = lax.broadcasted_iota(jnp.int32, (ROWS, ATOM_PAD), 1)

        def block(j, pooled):
            landed(c_all.at[j], c_recv.at[j])
            landed(a_all.at[j], a_recv.at[j])
            place = (lane + j * ATOM_DEV).astype(F32)
            inside = (place >= lower) & (place < upper) & (lane < ATOM_DEV)
            member = jnp.where(inside, 1.0, 0.0).astype(BF)
            act = act_of(c_all[j], a_all[j]).astype(BF)
            return pooled + jnp.dot(member, act, preferred_element_type=F32)

        pooled = lax.fori_loop(0, TOK_DEVS, block, jnp.zeros((ROWS, 128), F32))
        averaged = (pooled / counts).astype(BF)
        x[...] = jnp.dot(averaged, win_ref[...], preferred_element_type=F32)

    def enter_second():
        j = TOK_DEVS - 1
        landed(c_all.at[j], c_recv.at[j])
        landed(a_all.at[j], a_recv.at[j])
        act = act_of(c_all[j], a_all[j])[ATOM_DEV - ROWS : ATOM_DEV]
        x[...] = jnp.dot(act.astype(BF), win_ref[...], preferred_element_type=F32)

    def conditions():
        @pl.loop(0, TOK_DEVS)
        def _(j):
            landed(d_all.at[j], d_recv.at[j])

        landed(wada_ref, ada_sem)

        def rows_for(which, store):
            rows = d_all[pl.ds(8 * which, 8)].reshape(8 * COND_PAD, D)
            for k in range(4):
                full = jnp.dot(
                    rows, wada_v[:, D * k : D * (k + 1)], preferred_element_type=F32
                )
                value = full.reshape(8, COND_PAD, D)[:, :TOK_DEV].reshape(ROWS, D)
                store(k, jax.nn.sigmoid(value) if k % 2 == 0 else value)

        def to_send(k, value):
            cond_tx[k] = value

        def to_keep(k, value):
            cond[core, k] = value

        rows_for(1 - core, to_send)
        pltpu.make_async_remote_copy(
            src_ref=cond_tx, dst_ref=cond.at[core], send_sem=m_send, recv_sem=m_recv,
            device_id=(sibling, t), device_id_type=MESH,
        ).start()
        rows_for(core, to_keep)

    own_rows = pl.ds(pl.multiple_of(core * ROWS, ROWS), ROWS)
    other_rows = pl.ds(pl.multiple_of((1 - core) * ROWS, ROWS), ROWS)

    def layer(lp):
        @pl.when(lp != core)
        def _():
            landed(cond.at[lp], m_recv)

        norm[...] = (normalise(x[...]) * cond[lp, 0] + cond[lp, 1]).astype(BF)
        landed(wqkv_v.at[lp], w_recv.at[lp, 0])

        def project(column, width):
            return jnp.dot(
                norm[...], wqkv_v[lp, :, column : column + width], preferred_element_type=F32
            ).astype(BF)

        for part in range(2):
            for j in range(3):
                kv[lp, part, own_rows, 256 * j : 256 * (j + 1)] = project(
                    D * (part + 1) + 256 * j, 256
                )
            pltpu.make_async_remote_copy(
                src_ref=kv.at[lp, part, own_rows], dst_ref=kv.at[lp, part, own_rows],
                send_sem=kv_send.at[lp, part], recv_sem=kv_recv.at[lp, part],
                device_id=(sibling, t), device_id_type=MESH,
            ).start()
        for j in range(3):
            q[:, 256 * j : 256 * (j + 1)] = project(256 * j, 256)

        @pl.loop(0, 8)
        def _(j):
            landed(b_all.at[lp, j], b_recv.at[lp, j])

        for part in range(2):
            landed(kv.at[lp, part, other_rows], kv_recv.at[lp, part])

        @pl.loop(0, 2)
        def _(g):
            blocks = [None, None, None]
            for pair in range(4):
                bias = b_all[lp, :, pl.ds(pl.multiple_of(192 * g + 48 * pair, 48), 48), :].astype(F32)
                for e in range(2):
                    low = HEAD_DIM * (2 * pair + e)
                    high = low + HEAD_DIM
                    first, stop = low // 128, (high + 127) // 128
                    width = 128 * (stop - first)
                    lanes = pl.ds(pl.multiple_of(g * GROUP + 128 * first, 128), width)
                    lane = lax.broadcasted_iota(jnp.int32, (1, width), 1) + 128 * first
                    mask = jnp.where((lane >= low) & (lane < high), 1.0, 0.0).astype(BF)
                    scores = lax.dot_general(
                        q[:, lanes] * mask, kv[lp, 0, :, lanes], (((1,), (1,)), ((), ())),
                        preferred_element_type=F32,
                    )
                    scores = scores * HEAD_DIM ** (-0.5) + bias[
                        :, TOK_DEV * e : TOK_DEV * (e + 1)
                    ].reshape(ROWS, KEYS)
                    top = jnp.max(scores, axis=-1, keepdims=True)
                    weight = jnp.exp(scores - top)
                    total = jnp.sum(weight, axis=-1, keepdims=True)
                    out = jnp.dot(
                        weight.astype(BF), kv[lp, 1, :, lanes], preferred_element_type=F32
                    ) / total
                    for b in range(first, stop):
                        piece = out[:, 128 * (b - first) : 128 * (b - first + 1)]
                        if blocks[b] is None:
                            blocks[b] = piece
                        else:
                            at = lax.broadcasted_iota(jnp.int32, (ROWS, 128), 1) + 128 * b
                            blocks[b] = jnp.where(at >= low, piece, blocks[b])
            for b in range(3):
                att[:, pl.ds(pl.multiple_of(g * GROUP + 128 * b, 128), 128)] = blocks[b].astype(BF)

        for part in range(2):
            landed(kv.at[lp, part, own_rows], kv_send.at[lp, part])

        landed(wout_v.at[lp], w_recv.at[lp, 1])
        for j in range(3):
            cols = slice(256 * j, 256 * (j + 1))
            x[:, cols] = x[:, cols] + jnp.dot(
                att[...], wout_v[lp, :, cols], preferred_element_type=F32
            )
        norm[...] = (normalise(x[...]) * cond[lp, 2] + cond[lp, 3]).astype(BF)
        landed(wff_v.at[lp], w_recv.at[lp, 2])
        for j in range(6):
            gate = jnp.dot(
                norm[...], wff_v[lp, :, 256 * j : 256 * (j + 1)], preferred_element_type=F32
            )
            up = jnp.dot(
                norm[...], wff_v[lp, :, FF + 256 * j : FF + 256 * (j + 1)],
                preferred_element_type=F32,
            )
            hid[:, 256 * j : 256 * (j + 1)] = (jax.nn.silu(gate) * up).astype(BF)
        landed(wdown_v.at[lp], w_recv.at[lp, 3])
        for j in range(3):
            cols = slice(256 * j, 256 * (j + 1))
            x[:, cols] = x[:, cols] + jnp.dot(
                hid[...], wdown_v[lp, :, cols], preferred_element_type=F32
            )

    @pl.when(active)
    def _():
        conditions()

        @pl.when(s == 0)
        def _():
            enter_first()

        @pl.when(s == 1)
        def _():
            enter_second()

        @pl.when(plane > 0)
        def _():
            landed(xin, x_recv)
            x[...] = xin[...].astype(F32)

        @pl.loop(0, 2)
        def _(lp):
            layer(lp)

        @pl.when(plane < 3)
        def _():
            xtx[...] = x[...].astype(BF)
            pltpu.make_async_remote_copy(
                src_ref=xtx, dst_ref=xin, send_sem=x_send, recv_sem=x_recv,
                device_id=(s + 2, t), device_id_type=MESH,
            ).start()

        @pl.when(plane == 3)
        def _():
            done = normalise(x[...]).reshape(8, TOK_DEV, D)
            fin_tx[...] = jnp.concatenate(
                [done, jnp.zeros((8, COND_PAD - TOK_DEV, D), F32)], axis=1
            ).astype(BF)

            @pl.loop(0, 8)
            def _(j):
                send(fin_tx.at[j], fin, f_send.at[j], f_recv, pose, 8 * core + j)

    landed(fin, f_recv)
    out_ref[...] = fin[...]

    sent(c_src, c_send.at[0], 0, chip_of(s))

    @pl.when(last)
    def _():
        sent(c_src, c_send.at[1], 1, chip_of(s))

    @pl.when((s == 0) | ((s == 1) & last))
    def _():
        @pl.loop(0, POSES)
        def _(p):
            sent(a_src, a_send.at[p], s, chip_of(p))

    @pl.when((s == 0) & (t < 8))
    def _():
        @pl.loop(0, POSES)
        def _(p):
            sent(count_ref, n_send.at[p], s, chip_of(p))

    @pl.loop(0, POSES)
    def _(p):
        sent(d_src, d_send.at[p], s, chip_of(p))
        sent(bias_ref, b_send.at[p], 2 * plane + half, chip_of(p))

    @pl.when(active)
    def _():
        for k, (src, dst) in enumerate(weights):
            landed(src, w_send.at[k])
        landed(cond_tx, m_send)

        @pl.when(plane < 3)
        def _():
            landed(xtx, x_send)

        @pl.when(plane == 3)
        def _():
            @pl.loop(0, 8)
            def _(j):
                sent(fin_tx.at[j], f_send.at[j], pose, 8 * core + j)


def body(
    coords, atom_single, token_atoms, cond_single, pair_bias, w_coord, w_in,
    w_ada, w_qkv, w_out, w_ff, w_down,
):
    counts = jnp.broadcast_to(token_atoms.astype(F32)[:, None], (TOK_DEV, 128))
    bias = pair_bias[0].reshape(HEADS * TOK_DEV, KEYS)
    w_coord_rows = jnp.concatenate([w_coord, jnp.zeros((5, 128), F32)], axis=0)
    vmem = pl.BlockSpec(memory_space=pltpu.VMEM)
    hbm = pl.BlockSpec(memory_space=pl.ANY)
    dma = pltpu.SemaphoreType.DMA
    rows = pl.pallas_call(
        kernel,
        out_shape=jax.ShapeDtypeStruct((COND_PAD, D), BF),
        in_specs=[vmem, vmem, vmem, vmem, hbm, vmem, vmem, hbm, hbm, hbm, hbm, hbm],
        out_specs=vmem,
        scratch_shapes=[
            pltpu.VMEM((8, 256), F32),
            pltpu.VMEM((ATOM_PAD, 128), BF),
            pltpu.VMEM((COND_PAD, D), BF),
            pltpu.VMEM((TOK_DEVS, 8, 256), F32),
            pltpu.VMEM((TOK_DEVS, ATOM_PAD, 128), BF),
            pltpu.VMEM((8, TOK_DEV, 128), F32),
            pltpu.VMEM((TOK_DEVS, COND_PAD, D), BF),
            pltpu.VMEM((2, 8, HEADS * TOK_DEV, KEYS), BF),
            pltpu.VMEM((D, 4 * D), BF),
            pltpu.VMEM((2, D, 3 * D), BF),
            pltpu.VMEM((2, D, D), BF),
            pltpu.VMEM((2, D, 2 * FF), BF),
            pltpu.VMEM((2, FF, D), BF),
            pltpu.VMEM((2, 4, ROWS, D), F32),
            pltpu.VMEM((4, ROWS, D), F32),
            pltpu.VMEM((ROWS, D), F32),
            pltpu.VMEM((ROWS, D), BF),
            pltpu.VMEM((ROWS, D), BF),
            pltpu.VMEM((ROWS, D), BF),
            pltpu.VMEM((ROWS, D), BF),
            pltpu.VMEM((2, 2, KEYS, D), BF),
            pltpu.VMEM((ROWS, D), BF),
            pltpu.VMEM((ROWS, FF), BF),
            pltpu.VMEM((8, COND_PAD, D), BF),
            pltpu.VMEM((COND_PAD, D), BF),
            dma((2,)), dma((TOK_DEVS,)),
            dma((POSES,)), dma((TOK_DEVS,)),
            dma((POSES,)), dma((8,)),
            dma((POSES,)), dma((TOK_DEVS,)),
            dma((POSES,)), dma((2, 8)),
            dma((4,)), dma((2, 4)),
            dma,
            dma, dma,
            dma((2, 2)), dma((2, 2)),
            dma, dma,
            dma((8,)), dma,
        ],
        compiler_params=pltpu.CompilerParams(
            collective_id=0, has_side_effects=True, vmem_limit_bytes=60 << 20
        ),
    )(
        coords, atom_single, counts, cond_single, bias, w_coord_rows, w_in,
        w_ada[0], w_qkv[0], w_out[0], w_ff[0], w_down[0],
    )
    return rows[None, :TOK_DEV]


def solution(mesh):
    return jax.shard_map(
        body,
        mesh=mesh,
        in_specs=(
            P("section", None, "tok"),
            P("tok", None),
            P("tok"),
            P("tok", None),
            P("section", None, "tok", None),
            P(),
            P(),
            P("section", None, None),
            P("section", None, None),
            P("section", None, None),
            P("section", None, None),
            P("section", None, None),
        ),
        out_specs=P("section", "tok", None),
        check_vma=False,
    )
```

```python
import jax
import jax.numpy as jnp
from jax import lax
from jax.experimental import pallas as pl
from jax.experimental.pallas import tpu as pltpu
from jax.sharding import PartitionSpec as P

HEADS = 16
HEAD_DIM = 48
FF = 1536
D = 768
POSES = 8
TOK_DEVS = 16
SECTIONS = 8
ROWS = 192
TOK_DEV = 24
ATOM_DEV = 216
ATOM_PAD = 224
COND_PAD = 32
KEYS = 384
GROUP = 384
MESH = pl.DeviceIdType.MESH
BF = jnp.bfloat16
F32 = jnp.float32


def chip_of(pose):
    x = pose // 2
    return 4 * x + 2 * (pose % 2) + x % 2


def normalise(v):
    centre = v - jnp.mean(v, axis=-1, keepdims=True)
    return centre * lax.rsqrt(jnp.mean(centre * centre, axis=-1, keepdims=True) + 1e-05)


def landed(ref, sem):
    pltpu.make_async_copy(ref, ref, sem).wait()


def kernel(
    coords_ref, atom_ref, count_ref, cond_ref, bias_ref, wcoord_ref, win_ref,
    wada_ref, wqkv_ref, wout_ref, wff_ref, wdown_ref,
    out_ref,
    c_src, a_src, d_src, wc, c_all, a_all, d_all, b_all, relay,
    wada_v, wqkv_v, wout_v, wff_v, wdown_v,
    cond, cond_tx, x, xin, xtx, norm, q, kv, att, hid, fin_tx, fin,
    c_send, c_recv, a_send, a_recv, d_send, d_recv, r_send, r_recv, b_send, b_recv, go,
    w_send, w_recv, ada_sem, m_send, m_recv, kv_send, kv_recv, x_send, x_recv, f_send, f_recv,
):
    s = lax.axis_index("section")
    t = lax.axis_index("tok")
    plane = s // 2
    core = lax.rem(s, 2)
    sibling = s + 1 - 2 * core
    cx, cz = t // 4, lax.rem(t, 4)
    active = lax.rem(cx + cz, 2) == 0
    pose = 2 * cx + cz // 2
    half = t // 8

    weights = ((wqkv_ref, wqkv_v), (wout_ref, wout_v), (wff_ref, wff_v), (wdown_ref, wdown_v))

    @pl.when(active)
    def _():
        pltpu.make_async_copy(wada_ref, wada_v, ada_sem).start()
        for k, (src, dst) in enumerate(weights):
            pltpu.make_async_copy(src, dst.at[core], w_recv.at[core, k]).start()

    barrier = pltpu.get_barrier_semaphore()

    def greet(section, tok):
        pl.semaphore_signal(barrier, inc=1, device_id=(section, tok), device_id_type=MESH)

    @pl.when(active)
    def _():
        @pl.loop(0, TOK_DEVS)
        def _(j):
            @pl.when(j != t)
            def _():
                greet(s, j)

        @pl.loop(0, TOK_DEVS)
        def _(j):
            greet(sibling, j)

        @pl.when((s == 0) & (pose != 0))
        def _():
            @pl.loop(0, TOK_DEVS)
            def _(j):
                greet(pose, j)

        @pl.when((s == 1) & (pose != 1))
        def _():
            greet(pose, TOK_DEVS - 1)

        @pl.when(plane > 0)
        def _():
            greet(s - 2, t)

    greet(sibling, t)

    @pl.loop(1, 4)
    def _(k):
        greet(s, 4 * lax.rem(cx + k, 4) + cz)
        greet(s, 4 * cx + lax.rem(cz + k, 4))

    fin_section, fin_tok = 6 + half, chip_of(s)
    fin_self = (fin_section == s) & (fin_tok == t)

    @pl.when(jnp.logical_not(fin_self))
    def _():
        greet(fin_section, fin_tok)

    c_src[...] = jnp.zeros_like(c_src)
    c_src[0:3, 0:ATOM_DEV] = coords_ref[...].reshape(3, ATOM_DEV)
    c_src[3:4, 0:TOK_DEV] = count_ref[...].astype(F32)
    wc[...] = jnp.zeros_like(wc)
    wc[0:3] = wcoord_ref[...]
    a_src[...] = jnp.concatenate(
        [atom_ref[...].astype(F32), jnp.zeros((ATOM_PAD - ATOM_DEV, 128), F32)], axis=0
    ).astype(BF)
    d_src[...] = jnp.concatenate(
        [cond_ref[...].astype(F32), jnp.zeros((COND_PAD - TOK_DEV, D), F32)], axis=0
    ).astype(BF)

    one = lambda flag: flag.astype(jnp.int32)
    last = t == TOK_DEVS - 1
    expected = 8 - one(active)
    expected += 8 + 1 + 6
    expected += one(s != 0) + one(last & (s != 1))
    expected += one(active & (plane < 3))
    fin_here = active & (plane == 3)
    fin_own = fin_here & (pose == s) & (half == core)
    expected += 8 * one(fin_here) - one(fin_own)
    pl.semaphore_wait(barrier, expected)

    def send(src, dst, send_sem, recv_sem, section, tok):
        own = (section == s) & (tok == t)

        @pl.when(own)
        def _():
            pltpu.make_async_copy(src, dst, recv_sem).start()

        @pl.when(jnp.logical_not(own))
        def _():
            pltpu.make_async_remote_copy(
                src_ref=src, dst_ref=dst, send_sem=send_sem, recv_sem=recv_sem,
                device_id=(section, tok), device_id_type=MESH,
            ).start()

    def sent(src, send_sem, section, tok):
        @pl.when(jnp.logical_not((section == s) & (tok == t)))
        def _():
            landed(src, send_sem)

    send(c_src, c_all.at[t], c_send.at[0], c_recv.at[t], 0, chip_of(s))

    @pl.when(last)
    def _():
        send(c_src, c_all.at[t], c_send.at[1], c_recv.at[t], 1, chip_of(s))

    @pl.when((s == 0) | ((s == 1) & last))
    def _():
        @pl.loop(0, POSES)
        def _(p):
            send(a_src, a_all.at[t], a_send.at[p], a_recv.at[t], s, chip_of(p))

    @pl.loop(0, POSES)
    def _(p):
        send(d_src, d_all.at[t], d_send.at[p], d_recv.at[t], s, chip_of(p))

    def legs(part, at, k):
        if part == 0:
            return 4 * lax.rem(cx + k, 4) + cz
        return 4 * cx + lax.rem(cz + k, 4)

    def half_of(part):
        return bias_ref.at[pl.ds(ROWS * part, ROWS)]

    def forward(part, at, source, act):
        origin = 4 * at + cz if part == 0 else 4 * cx + at
        block = lax.rem(origin, 8)
        for e in range(2):
            if part == 0:
                tok = 4 * cx + lax.rem(cx, 2) + 2 * e
            else:
                tok = 4 * (lax.rem(cz, 2) + 2 * e) + cz
            act(source, b_all.at[core, block, pl.ds(ROWS * part, ROWS)], b_send.at[part, at, e],
                b_recv.at[core, block, part], 2 * plane + origin // 8, tok)

    def bias_out():
        for part in range(2):
            here = cx if part == 0 else cz

            @pl.loop(1, 4)
            def _(k):
                pltpu.make_async_remote_copy(
                    src_ref=half_of(part), dst_ref=relay.at[part, here],
                    send_sem=r_send.at[part, k], recv_sem=r_recv.at[part, here],
                    device_id=(s, legs(part, here, k)), device_id_type=MESH,
                ).start()

        for part in range(2):
            forward(part, cx if part == 0 else cz, half_of(part), send)

    def bias_on():
        @pl.loop(1, 4)
        def _(k):
            for part in range(2):
                at = lax.rem((cx if part == 0 else cz) + k, 4)
                landed(relay.at[part, at], r_recv.at[part, at])
                forward(part, at, relay.at[part, at], send)

    def bias_gone():
        def gone(source, target, send_sem, recv_sem, section, tok):
            sent(source, send_sem, section, tok)

        for part in range(2):
            @pl.loop(0, 4)
            def _(k):
                at = lax.rem((cx if part == 0 else cz) + k, 4)

                @pl.when(k > 0)
                def _():
                    landed(half_of(part), r_send.at[part, k])

                forward(part, at, half_of(part), gone)

    @pl.when(active)
    def _():
        for k, (src, dst) in enumerate(weights):
            pltpu.make_async_remote_copy(
                src_ref=src, dst_ref=dst.at[core], send_sem=w_send.at[k],
                recv_sem=w_recv.at[core, k], device_id=(sibling, t), device_id_type=MESH,
            ).start()

    @pl.when(core == 0)
    def _():
        bias_out()
        bias_on()

    @pl.when((core == 0) & jnp.logical_not(active))
    def _():
        bias_gone()
        pl.semaphore_signal(go, inc=1, device_id=(sibling, t), device_id_type=MESH)

    @pl.when((core == 1) & jnp.logical_not(active))
    def _():
        pl.semaphore_wait(go, 1)
        bias_out()
        bias_on()
        bias_gone()

    def act_of(points, single):
        moved = lax.dot_general(
            points, wc[...], (((0,), (0,)), ((), ())),
            precision=lax.Precision.HIGHEST, preferred_element_type=F32,
        )
        return jnp.maximum(single.astype(F32) + moved[:ATOM_PAD], 0.0)

    def enter_first():
        @pl.loop(0, TOK_DEVS)
        def _(j):
            landed(c_all.at[j], c_recv.at[j])

        lane8 = lax.broadcasted_iota(jnp.int32, (TOK_DEV, 128), 1)
        place8 = lax.broadcasted_iota(jnp.int32, (TOK_DEV, 128), 0)
        count_blocks, start_blocks = [], []
        total = jnp.zeros((TOK_DEV, 1), F32)
        for j in range(8):
            row = jnp.broadcast_to(c_all[j, 3:4, 0:128], (TOK_DEV, 128))
            mine = jnp.where(lane8 == place8, row, 0.0)
            ahead = jnp.where(lane8 < place8, row, 0.0)
            count_blocks.append(jnp.sum(mine, axis=1, keepdims=True))
            start_blocks.append(total + jnp.sum(ahead, axis=1, keepdims=True))
            total = total + jnp.sum(row, axis=1, keepdims=True)
        counts = jnp.broadcast_to(jnp.concatenate(count_blocks, axis=0), (ROWS, 128))
        starts = jnp.broadcast_to(jnp.concatenate(start_blocks, axis=0), (ROWS, 128))
        ends = starts + counts
        lower = jnp.concatenate([starts, starts], axis=1)[:, :ATOM_PAD]
        upper = jnp.concatenate([ends, ends], axis=1)[:, :ATOM_PAD]
        lane = lax.broadcasted_iota(jnp.int32, (ROWS, ATOM_PAD), 1)

        def block(j, pooled):
            landed(a_all.at[j], a_recv.at[j])
            place = (lane + j * ATOM_DEV).astype(F32)
            inside = (place >= lower) & (place < upper) & (lane < ATOM_DEV)
            member = jnp.where(inside, 1.0, 0.0).astype(BF)
            act = act_of(c_all[j], a_all[j]).astype(BF)
            return pooled + jnp.dot(member, act, preferred_element_type=F32)

        pooled = lax.fori_loop(0, TOK_DEVS, block, jnp.zeros((ROWS, 128), F32))
        averaged = (pooled / counts).astype(BF)
        x[...] = jnp.dot(averaged, win_ref[...], preferred_element_type=F32)

    def enter_second():
        j = TOK_DEVS - 1
        landed(c_all.at[j], c_recv.at[j])
        landed(a_all.at[j], a_recv.at[j])
        act = act_of(c_all[j], a_all[j])[ATOM_DEV - ROWS : ATOM_DEV]
        x[...] = jnp.dot(act.astype(BF), win_ref[...], preferred_element_type=F32)

    def conditions():
        @pl.loop(0, TOK_DEVS)
        def _(j):
            landed(d_all.at[j], d_recv.at[j])

        landed(wada_ref, ada_sem)

        def rows_for(which, store):
            rows = d_all[pl.ds(8 * which, 8)].reshape(8 * COND_PAD, D)
            for k in range(4):
                full = jnp.dot(
                    rows, wada_v[:, D * k : D * (k + 1)], preferred_element_type=F32
                )
                value = full.reshape(8, COND_PAD, D)[:, :TOK_DEV].reshape(ROWS, D)
                store(k, jax.nn.sigmoid(value) if k % 2 == 0 else value)

        def to_send(k, value):
            cond_tx[k] = value

        def to_keep(k, value):
            cond[core, k] = value

        rows_for(1 - core, to_send)
        pltpu.make_async_remote_copy(
            src_ref=cond_tx, dst_ref=cond.at[core], send_sem=m_send, recv_sem=m_recv,
            device_id=(sibling, t), device_id_type=MESH,
        ).start()
        rows_for(core, to_keep)

    own_rows = pl.ds(pl.multiple_of(core * ROWS, ROWS), ROWS)
    other_rows = pl.ds(pl.multiple_of((1 - core) * ROWS, ROWS), ROWS)

    def layer(lp):
        @pl.when(lp != core)
        def _():
            landed(cond.at[lp], m_recv)

        norm[...] = (normalise(x[...]) * cond[lp, 0] + cond[lp, 1]).astype(BF)
        landed(wqkv_v.at[lp], w_recv.at[lp, 0])

        def project(column, width):
            return jnp.dot(
                norm[...], wqkv_v[lp, :, column : column + width], preferred_element_type=F32
            ).astype(BF)

        for part in range(2):
            for j in range(3):
                kv[lp, part, own_rows, 256 * j : 256 * (j + 1)] = project(
                    D * (part + 1) + 256 * j, 256
                )
            pltpu.make_async_remote_copy(
                src_ref=kv.at[lp, part, own_rows], dst_ref=kv.at[lp, part, own_rows],
                send_sem=kv_send.at[lp, part], recv_sem=kv_recv.at[lp, part],
                device_id=(sibling, t), device_id_type=MESH,
            ).start()
        for j in range(3):
            q[:, 256 * j : 256 * (j + 1)] = project(256 * j, 256)

        @pl.loop(0, 16)
        def _(j):
            block = b_all.at[lp, j // 2, pl.ds(ROWS * lax.rem(j, 2), ROWS)]
            landed(block, b_recv.at[lp, j // 2, lax.rem(j, 2)])

        @pl.when((lp == 0) & (core == 1))
        def _():
            bias_out()

        for part in range(2):
            landed(kv.at[lp, part, other_rows], kv_recv.at[lp, part])

        @pl.loop(0, 2)
        def _(g):
            blocks = [None, None, None]
            for pair in range(4):
                bias = b_all[lp, :, pl.ds(pl.multiple_of(192 * g + 48 * pair, 48), 48), :].astype(F32)
                for e in range(2):
                    low = HEAD_DIM * (2 * pair + e)
                    high = low + HEAD_DIM
                    first, stop = low // 128, (high + 127) // 128
                    width = 128 * (stop - first)
                    lanes = pl.ds(pl.multiple_of(g * GROUP + 128 * first, 128), width)
                    lane = lax.broadcasted_iota(jnp.int32, (1, width), 1) + 128 * first
                    mask = jnp.where((lane >= low) & (lane < high), 1.0, 0.0).astype(BF)
                    scores = lax.dot_general(
                        q[:, lanes] * mask, kv[lp, 0, :, lanes], (((1,), (1,)), ((), ())),
                        preferred_element_type=F32,
                    )
                    scores = scores * HEAD_DIM ** (-0.5) + bias[
                        :, TOK_DEV * e : TOK_DEV * (e + 1)
                    ].reshape(ROWS, KEYS)
                    top = jnp.max(scores, axis=-1, keepdims=True)
                    weight = jnp.exp(scores - top)
                    total = jnp.sum(weight, axis=-1, keepdims=True)
                    out = jnp.dot(
                        weight.astype(BF), kv[lp, 1, :, lanes], preferred_element_type=F32
                    ) / total
                    for b in range(first, stop):
                        piece = out[:, 128 * (b - first) : 128 * (b - first + 1)]
                        if blocks[b] is None:
                            blocks[b] = piece
                        else:
                            at = lax.broadcasted_iota(jnp.int32, (ROWS, 128), 1) + 128 * b
                            blocks[b] = jnp.where(at >= low, piece, blocks[b])
            for b in range(3):
                att[:, pl.ds(pl.multiple_of(g * GROUP + 128 * b, 128), 128)] = blocks[b].astype(BF)

        @pl.when((lp == 0) & (core == 1))
        def _():
            bias_on()

        for part in range(2):
            landed(kv.at[lp, part, own_rows], kv_send.at[lp, part])

        landed(wout_v.at[lp], w_recv.at[lp, 1])
        for j in range(3):
            cols = slice(256 * j, 256 * (j + 1))
            x[:, cols] = x[:, cols] + jnp.dot(
                att[...], wout_v[lp, :, cols], preferred_element_type=F32
            )
        norm[...] = (normalise(x[...]) * cond[lp, 2] + cond[lp, 3]).astype(BF)
        landed(wff_v.at[lp], w_recv.at[lp, 2])
        for j in range(6):
            gate = jnp.dot(
                norm[...], wff_v[lp, :, 256 * j : 256 * (j + 1)], preferred_element_type=F32
            )
            up = jnp.dot(
                norm[...], wff_v[lp, :, FF + 256 * j : FF + 256 * (j + 1)],
                preferred_element_type=F32,
            )
            hid[:, 256 * j : 256 * (j + 1)] = (jax.nn.silu(gate) * up).astype(BF)
        landed(wdown_v.at[lp], w_recv.at[lp, 3])
        for j in range(3):
            cols = slice(256 * j, 256 * (j + 1))
            x[:, cols] = x[:, cols] + jnp.dot(
                hid[...], wdown_v[lp, :, cols], preferred_element_type=F32
            )

    @pl.when(active)
    def _():
        conditions()

        @pl.when(s == 0)
        def _():
            enter_first()

        @pl.when(s == 1)
        def _():
            enter_second()

        @pl.when(plane > 0)
        def _():
            landed(xin, x_recv)
            x[...] = xin[...].astype(F32)

        @pl.loop(0, 2)
        def _(lp):
            layer(lp)

        @pl.when(plane < 3)
        def _():
            xtx[...] = x[...].astype(BF)
            pltpu.make_async_remote_copy(
                src_ref=xtx, dst_ref=xin, send_sem=x_send, recv_sem=x_recv,
                device_id=(s + 2, t), device_id_type=MESH,
            ).start()

        @pl.when(plane == 3)
        def _():
            done = normalise(x[...]).reshape(8, TOK_DEV, D)
            fin_tx[...] = jnp.concatenate(
                [done, jnp.zeros((8, COND_PAD - TOK_DEV, D), F32)], axis=1
            ).astype(BF)

            @pl.loop(0, 8)
            def _(j):
                send(fin_tx.at[j], fin, f_send.at[j], f_recv, pose, 8 * core + j)

    landed(fin, f_recv)
    out_ref[...] = fin[...].astype(F32)[:TOK_DEV].astype(BF)

    sent(c_src, c_send.at[0], 0, chip_of(s))

    @pl.when(last)
    def _():
        sent(c_src, c_send.at[1], 1, chip_of(s))

    @pl.when((s == 0) | ((s == 1) & last))
    def _():
        @pl.loop(0, POSES)
        def _(p):
            sent(a_src, a_send.at[p], s, chip_of(p))

    @pl.loop(0, POSES)
    def _(p):
        sent(d_src, d_send.at[p], s, chip_of(p))

    @pl.when(active)
    def _():
        for k, (src, dst) in enumerate(weights):
            landed(src, w_send.at[k])
        landed(cond_tx, m_send)
        bias_gone()

        @pl.when(plane < 3)
        def _():
            landed(xtx, x_send)

        @pl.when(plane == 3)
        def _():
            @pl.loop(0, 8)
            def _(j):
                sent(fin_tx.at[j], f_send.at[j], pose, 8 * core + j)


def body(
    coords, atom_single, token_atoms, cond_single, pair_bias, w_coord, w_in,
    w_ada, w_qkv, w_out, w_ff, w_down,
):
    counts = token_atoms.reshape(1, TOK_DEV)
    points = jnp.transpose(coords, (1, 0, 2))
    bias = pair_bias[0].reshape(HEADS * TOK_DEV, KEYS)
    vmem = pl.BlockSpec(memory_space=pltpu.VMEM)
    hbm = pl.BlockSpec(memory_space=pl.ANY)
    dma = pltpu.SemaphoreType.DMA
    rows = pl.pallas_call(
        kernel,
        out_shape=jax.ShapeDtypeStruct((TOK_DEV, D), BF),
        in_specs=[vmem, vmem, vmem, vmem, hbm, vmem, vmem, hbm, hbm, hbm, hbm, hbm],
        out_specs=vmem,
        scratch_shapes=[
            pltpu.VMEM((8, 256), F32),
            pltpu.VMEM((ATOM_PAD, 128), BF),
            pltpu.VMEM((COND_PAD, D), BF),
            pltpu.VMEM((8, 128), F32),
            pltpu.VMEM((TOK_DEVS, 8, 256), F32),
            pltpu.VMEM((TOK_DEVS, ATOM_PAD, 128), BF),
            pltpu.VMEM((TOK_DEVS, COND_PAD, D), BF),
            pltpu.VMEM((2, 8, HEADS * TOK_DEV, KEYS), BF),
            pltpu.VMEM((2, 4, ROWS, KEYS), BF),
            pltpu.VMEM((D, 4 * D), BF),
            pltpu.VMEM((2, D, 3 * D), BF),
            pltpu.VMEM((2, D, D), BF),
            pltpu.VMEM((2, D, 2 * FF), BF),
            pltpu.VMEM((2, FF, D), BF),
            pltpu.VMEM((2, 4, ROWS, D), F32),
            pltpu.VMEM((4, ROWS, D), F32),
            pltpu.VMEM((ROWS, D), F32),
            pltpu.VMEM((ROWS, D), BF),
            pltpu.VMEM((ROWS, D), BF),
            pltpu.VMEM((ROWS, D), BF),
            pltpu.VMEM((ROWS, D), BF),
            pltpu.VMEM((2, 2, KEYS, D), BF),
            pltpu.VMEM((ROWS, D), BF),
            pltpu.VMEM((ROWS, FF), BF),
            pltpu.VMEM((8, COND_PAD, D), BF),
            pltpu.VMEM((COND_PAD, D), BF),
            dma((2,)), dma((TOK_DEVS,)),
            dma((POSES,)), dma((TOK_DEVS,)),
            dma((POSES,)), dma((TOK_DEVS,)),
            dma((2, 4)), dma((2, 4)),
            dma((2, 4, 2)), dma((2, 8, 2)),
            pltpu.SemaphoreType.REGULAR,
            dma((4,)), dma((2, 4)),
            dma,
            dma, dma,
            dma((2, 2)), dma((2, 2)),
            dma, dma,
            dma((8,)), dma,
        ],
        compiler_params=pltpu.CompilerParams(
            collective_id=0, has_side_effects=True, vmem_limit_bytes=60 << 20
        ),
    )(
        points, atom_single, counts, cond_single, bias, w_coord, w_in,
        w_ada[0], w_qkv[0], w_out[0], w_ff[0], w_down[0],
    )
    return rows[None]


def solution(mesh):
    return jax.shard_map(
        body,
        mesh=mesh,
        in_specs=(
            P("section", None, "tok"),
            P("tok", None),
            P("tok"),
            P("tok", None),
            P("section", None, "tok", None),
            P(),
            P(),
            P("section", None, None),
            P("section", None, None),
            P("section", None, None),
            P("section", None, None),
            P("section", None, None),
        ),
        out_specs=P("section", "tok", None),
        check_vma=False,
    )
```

```python
import jax
import jax.numpy as jnp
from jax import lax
from jax.experimental import pallas as pl
from jax.experimental.pallas import tpu as pltpu
from jax.sharding import PartitionSpec as P

HEADS = 16
HEAD_DIM = 48
FF = 1536
D = 768
POSES = 8
TOK_DEVS = 16
SECTIONS = 8
ROWS = 192
TOK_DEV = 24
ATOM_DEV = 216
ATOM_PAD = 224
COND_PAD = 32
KEYS = 384
GROUP = 384
MESH = pl.DeviceIdType.MESH
BF = jnp.bfloat16
F32 = jnp.float32


def chip_of(pose):
    x = pose // 2
    return 4 * x + 2 * (pose % 2) + x % 2


def normalise(v):
    centre = v - jnp.mean(v, axis=-1, keepdims=True)
    return centre * lax.rsqrt(jnp.mean(centre * centre, axis=-1, keepdims=True) + 1e-05)


def landed(ref, sem):
    pltpu.make_async_copy(ref, ref, sem).wait()


def kernel(
    coords_ref, atom_ref, count_ref, cond_ref, bias_ref, wcoord_ref, win_ref,
    wada_ref, wqkv_ref, wout_ref, wff_ref, wdown_ref,
    out_ref,
    c_src, a_src, d_src, wc, c_all, a_all, d_all, b_all, relay,
    wada_v, wqkv_v, wout_v, wff_v, wdown_v,
    cond, cond_tx, x, xin, xtx, norm, q, kv, att, hid, fin_tx, fin,
    spread, scores, probs, inverse,
    c_send, c_recv, a_send, a_recv, d_send, d_recv, r_send, r_recv, b_send, b_recv, go,
    w_send, w_recv, ada_sem, m_send, m_recv, kv_send, kv_recv, x_send, x_recv, f_send, f_recv,
):
    s = lax.axis_index("section")
    t = lax.axis_index("tok")
    plane = s // 2
    core = lax.rem(s, 2)
    sibling = s + 1 - 2 * core
    cx, cz = t // 4, lax.rem(t, 4)
    active = lax.rem(cx + cz, 2) == 0
    pose = 2 * cx + cz // 2
    half = t // 8

    weights = ((wqkv_ref, wqkv_v), (wout_ref, wout_v), (wff_ref, wff_v), (wdown_ref, wdown_v))

    @pl.when(active)
    def _():
        pltpu.make_async_copy(wada_ref, wada_v, ada_sem).start()
        for k, (src, dst) in enumerate(weights):
            pltpu.make_async_copy(src, dst.at[core], w_recv.at[core, k]).start()

    barrier = pltpu.get_barrier_semaphore()

    def greet(section, tok):
        pl.semaphore_signal(barrier, inc=1, device_id=(section, tok), device_id_type=MESH)

    @pl.when(active)
    def _():
        @pl.loop(0, TOK_DEVS)
        def _(j):
            @pl.when(j != t)
            def _():
                greet(s, j)

        @pl.loop(0, TOK_DEVS)
        def _(j):
            greet(sibling, j)

        @pl.when((s == 0) & (pose != 0))
        def _():
            @pl.loop(0, TOK_DEVS)
            def _(j):
                greet(pose, j)

        @pl.when((s == 1) & (pose != 1))
        def _():
            greet(pose, TOK_DEVS - 1)

        @pl.when(plane > 0)
        def _():
            greet(s - 2, t)

    greet(sibling, t)

    @pl.loop(1, 4)
    def _(k):
        greet(s, 4 * lax.rem(cx + k, 4) + cz)
        greet(s, 4 * cx + lax.rem(cz + k, 4))

    fin_section, fin_tok = 6 + half, chip_of(s)
    fin_self = (fin_section == s) & (fin_tok == t)

    @pl.when(jnp.logical_not(fin_self))
    def _():
        greet(fin_section, fin_tok)

    c_src[...] = jnp.zeros_like(c_src)
    c_src[0:3, 0:ATOM_DEV] = coords_ref[...].reshape(3, ATOM_DEV)
    c_src[3:4, 0:TOK_DEV] = count_ref[...].astype(F32)
    wc[...] = jnp.zeros_like(wc)
    wc[0:3] = wcoord_ref[...]
    a_src[...] = jnp.concatenate(
        [atom_ref[...].astype(F32), jnp.zeros((ATOM_PAD - ATOM_DEV, 128), F32)], axis=0
    ).astype(BF)
    d_src[...] = jnp.concatenate(
        [cond_ref[...].astype(F32), jnp.zeros((COND_PAD - TOK_DEV, D), F32)], axis=0
    ).astype(BF)

    one = lambda flag: flag.astype(jnp.int32)
    last = t == TOK_DEVS - 1
    expected = 8 - one(active)
    expected += 8 + 1 + 6
    expected += one(s != 0) + one(last & (s != 1))
    expected += one(active & (plane < 3))
    fin_here = active & (plane == 3)
    fin_own = fin_here & (pose == s) & (half == core)
    expected += 8 * one(fin_here) - one(fin_own)
    pl.semaphore_wait(barrier, expected)

    def send(src, dst, send_sem, recv_sem, section, tok):
        own = (section == s) & (tok == t)

        @pl.when(own)
        def _():
            pltpu.make_async_copy(src, dst, recv_sem).start()

        @pl.when(jnp.logical_not(own))
        def _():
            pltpu.make_async_remote_copy(
                src_ref=src, dst_ref=dst, send_sem=send_sem, recv_sem=recv_sem,
                device_id=(section, tok), device_id_type=MESH,
            ).start()

    def sent(src, send_sem, section, tok):
        @pl.when(jnp.logical_not((section == s) & (tok == t)))
        def _():
            landed(src, send_sem)

    send(c_src, c_all.at[t], c_send.at[0], c_recv.at[t], 0, chip_of(s))

    @pl.when(last)
    def _():
        send(c_src, c_all.at[t], c_send.at[1], c_recv.at[t], 1, chip_of(s))

    @pl.when((s == 0) | ((s == 1) & last))
    def _():
        @pl.loop(0, POSES)
        def _(p):
            send(a_src, a_all.at[t], a_send.at[p], a_recv.at[t], s, chip_of(p))

    @pl.loop(0, POSES)
    def _(p):
        send(d_src, d_all.at[t], d_send.at[p], d_recv.at[t], s, chip_of(p))

    def legs(part, at, k):
        if part == 0:
            return 4 * lax.rem(cx + k, 4) + cz
        return 4 * cx + lax.rem(cz + k, 4)

    def half_of(part):
        return bias_ref.at[pl.ds(ROWS * part, ROWS)]

    def forward(part, at, source, act):
        origin = 4 * at + cz if part == 0 else 4 * cx + at
        block = lax.rem(origin, 8)
        for e in range(2):
            if part == 0:
                tok = 4 * cx + lax.rem(cx, 2) + 2 * e
            else:
                tok = 4 * (lax.rem(cz, 2) + 2 * e) + cz
            act(source, b_all.at[core, block, pl.ds(ROWS * part, ROWS)], b_send.at[part, at, e],
                b_recv.at[core, block, part], 2 * plane + origin // 8, tok)

    def bias_out():
        for part in range(2):
            here = cx if part == 0 else cz

            @pl.loop(1, 4)
            def _(k):
                pltpu.make_async_remote_copy(
                    src_ref=half_of(part), dst_ref=relay.at[part, here],
                    send_sem=r_send.at[part, k], recv_sem=r_recv.at[part, here],
                    device_id=(s, legs(part, here, k)), device_id_type=MESH,
                ).start()

    def bias_on():
        for part in range(2):
            forward(part, cx if part == 0 else cz, half_of(part), send)

        @pl.loop(1, 4)
        def _(k):
            for part in range(2):
                at = lax.rem((cx if part == 0 else cz) + k, 4)
                landed(relay.at[part, at], r_recv.at[part, at])
                forward(part, at, relay.at[part, at], send)

    def bias_gone():
        def gone(source, target, send_sem, recv_sem, section, tok):
            sent(source, send_sem, section, tok)

        for part in range(2):
            @pl.loop(0, 4)
            def _(k):
                at = lax.rem((cx if part == 0 else cz) + k, 4)

                @pl.when(k > 0)
                def _():
                    landed(half_of(part), r_send.at[part, k])

                forward(part, at, half_of(part), gone)

    @pl.when(active)
    def _():
        for k, (src, dst) in enumerate(weights):
            pltpu.make_async_remote_copy(
                src_ref=src, dst_ref=dst.at[core], send_sem=w_send.at[k],
                recv_sem=w_recv.at[core, k], device_id=(sibling, t), device_id_type=MESH,
            ).start()

    bias_out()

    @pl.when(core == 0)
    def _():
        bias_on()

    @pl.when((core == 0) & jnp.logical_not(active))
    def _():
        bias_gone()
        pl.semaphore_signal(go, inc=1, device_id=(sibling, t), device_id_type=MESH)

    @pl.when((core == 1) & jnp.logical_not(active))
    def _():
        pl.semaphore_wait(go, 1)
        bias_on()
        bias_gone()

    def act_of(points, single):
        moved = lax.dot_general(
            points, wc[...], (((0,), (0,)), ((), ())),
            precision=lax.Precision.HIGHEST, preferred_element_type=F32,
        )
        return jnp.maximum(single.astype(F32) + moved[:ATOM_PAD], 0.0)

    def enter_first():
        @pl.loop(0, TOK_DEVS)
        def _(j):
            landed(c_all.at[j], c_recv.at[j])

        lane8 = lax.broadcasted_iota(jnp.int32, (TOK_DEV, 128), 1)
        place8 = lax.broadcasted_iota(jnp.int32, (TOK_DEV, 128), 0)
        count_blocks, start_blocks = [], []
        total = jnp.zeros((TOK_DEV, 1), F32)
        for j in range(8):
            row = jnp.broadcast_to(c_all[j, 3:4, 0:128], (TOK_DEV, 128))
            mine = jnp.where(lane8 == place8, row, 0.0)
            ahead = jnp.where(lane8 < place8, row, 0.0)
            count_blocks.append(jnp.sum(mine, axis=1, keepdims=True))
            start_blocks.append(total + jnp.sum(ahead, axis=1, keepdims=True))
            total = total + jnp.sum(row, axis=1, keepdims=True)
        counts = jnp.broadcast_to(jnp.concatenate(count_blocks, axis=0), (ROWS, 128))
        starts = jnp.broadcast_to(jnp.concatenate(start_blocks, axis=0), (ROWS, 128))
        ends = starts + counts
        lower = jnp.concatenate([starts, starts], axis=1)[:, :ATOM_PAD]
        upper = jnp.concatenate([ends, ends], axis=1)[:, :ATOM_PAD]
        lane = lax.broadcasted_iota(jnp.int32, (ROWS, ATOM_PAD), 1)

        def block(j, pooled):
            landed(a_all.at[j], a_recv.at[j])
            place = (lane + j * ATOM_DEV).astype(F32)
            inside = (place >= lower) & (place < upper) & (lane < ATOM_DEV)
            member = jnp.where(inside, 1.0, 0.0).astype(BF)
            act = act_of(c_all[j], a_all[j]).astype(BF)
            return pooled + jnp.dot(member, act, preferred_element_type=F32)

        pooled = lax.fori_loop(0, TOK_DEVS, block, jnp.zeros((ROWS, 128), F32))
        averaged = (pooled / counts).astype(BF)
        x[...] = jnp.dot(averaged, win_ref[...], preferred_element_type=F32)

    def enter_second():
        j = TOK_DEVS - 1
        landed(c_all.at[j], c_recv.at[j])
        landed(a_all.at[j], a_recv.at[j])
        act = act_of(c_all[j], a_all[j])[ATOM_DEV - ROWS : ATOM_DEV]
        x[...] = jnp.dot(act.astype(BF), win_ref[...], preferred_element_type=F32)

    def conditions():
        @pl.loop(0, TOK_DEVS)
        def _(j):
            landed(d_all.at[j], d_recv.at[j])

        landed(wada_ref, ada_sem)

        def rows_for(which, store):
            rows = d_all[pl.ds(8 * which, 8)].reshape(8 * COND_PAD, D)
            for k in range(4):
                full = jnp.dot(
                    rows, wada_v[:, D * k : D * (k + 1)], preferred_element_type=F32
                )
                value = full.reshape(8, COND_PAD, D)[:, :TOK_DEV].reshape(ROWS, D)
                store(k, jax.nn.sigmoid(value) if k % 2 == 0 else value)

        def to_send(k, value):
            cond_tx[k] = value

        def to_keep(k, value):
            cond[core, k] = value

        rows_for(1 - core, to_send)
        pltpu.make_async_remote_copy(
            src_ref=cond_tx, dst_ref=cond.at[core], send_sem=m_send, recv_sem=m_recv,
            device_id=(sibling, t), device_id_type=MESH,
        ).start()
        rows_for(core, to_keep)

    own_rows = pl.ds(pl.multiple_of(core * ROWS, ROWS), ROWS)
    other_rows = pl.ds(pl.multiple_of((1 - core) * ROWS, ROWS), ROWS)

    def layer(lp):
        @pl.when(lp != core)
        def _():
            landed(cond.at[lp], m_recv)

        norm[...] = (normalise(x[...]) * cond[lp, 0] + cond[lp, 1]).astype(BF)
        landed(wqkv_v.at[lp], w_recv.at[lp, 0])

        def project(column, width):
            return jnp.dot(
                norm[...], wqkv_v[lp, :, column : column + width], preferred_element_type=F32
            ).astype(BF)

        for part in range(2):
            for j in range(3):
                kv[lp, part, own_rows, 256 * j : 256 * (j + 1)] = project(
                    D * (part + 1) + 256 * j, 256
                )
            pltpu.make_async_remote_copy(
                src_ref=kv.at[lp, part, own_rows], dst_ref=kv.at[lp, part, own_rows],
                send_sem=kv_send.at[lp, part], recv_sem=kv_recv.at[lp, part],
                device_id=(sibling, t), device_id_type=MESH,
            ).start()
        for j in range(3):
            q[:, 256 * j : 256 * (j + 1)] = project(256 * j, 256)

        @pl.loop(0, 16)
        def _(j):
            block = b_all.at[lp, j // 2, pl.ds(ROWS * lax.rem(j, 2), ROWS)]
            landed(block, b_recv.at[lp, j // 2, lax.rem(j, 2)])

        for part in range(2):
            landed(kv.at[lp, part, other_rows], kv_recv.at[lp, part])

        for w in range(3):
            lanes = slice(256 * w, 256 * (w + 1))
            window = q[:, lanes]
            lane = lax.broadcasted_iota(jnp.int32, (1, 256), 1) + 256 * w
            for k in range(6):
                low = HEAD_DIM * (5 * w + k)
                mask = jnp.where((lane >= low) & (lane < low + HEAD_DIM), 1.0, 0.0).astype(BF)
                spread[ROWS * k : ROWS * (k + 1)] = window * mask
            scores[w] = lax.dot_general(
                spread[...], kv[lp, 0, :, lanes], (((1,), (1,)), ((), ())),
                preferred_element_type=F32,
            )

        for pair in range(8):
            bias = b_all[lp, :, 48 * pair : 48 * (pair + 1), :].astype(F32)
            for e in range(2):
                head = 2 * pair + e
                w = min(head // 5, 2)
                k = head - 5 * w
                raw = scores[w, ROWS * k : ROWS * (k + 1)]
                if k == 0 and w > 0:
                    raw = raw + scores[w - 1, 5 * ROWS : 6 * ROWS]
                logits = raw * HEAD_DIM ** (-0.5) + bias[
                    :, TOK_DEV * e : TOK_DEV * (e + 1)
                ].reshape(ROWS, KEYS)
                top = jnp.max(logits, axis=-1, keepdims=True)
                weight = jnp.exp(logits - top)
                total = jnp.sum(weight, axis=-1, keepdims=True)
                inverse[head] = jnp.broadcast_to(1.0 / total, (ROWS, 128))
                probs[ROWS * head : ROWS * (head + 1)] = weight.astype(BF)

        for w in range(3):
            lanes = slice(256 * w, 256 * (w + 1))
            out = jnp.dot(
                probs[ROWS * 5 * w : ROWS * (5 * w + 6)], kv[lp, 1, :, lanes],
                preferred_element_type=F32,
            )
            lane = lax.broadcasted_iota(jnp.int32, (1, 256), 1) + 256 * w
            whole = jnp.zeros((ROWS, 256), F32)
            for k in range(6):
                low = HEAD_DIM * (5 * w + k)
                factor = inverse[5 * w + k]
                piece = out[ROWS * k : ROWS * (k + 1)] * jnp.concatenate([factor, factor], axis=1)
                whole = jnp.where(lane >= low, piece, whole)
            att[:, lanes] = whole.astype(BF)

        for part in range(2):
            landed(kv.at[lp, part, own_rows], kv_send.at[lp, part])

        landed(wout_v.at[lp], w_recv.at[lp, 1])
        for j in range(3):
            cols = slice(256 * j, 256 * (j + 1))
            x[:, cols] = x[:, cols] + jnp.dot(
                att[...], wout_v[lp, :, cols], preferred_element_type=F32
            )
        norm[...] = (normalise(x[...]) * cond[lp, 2] + cond[lp, 3]).astype(BF)
        landed(wff_v.at[lp], w_recv.at[lp, 2])
        for j in range(6):
            gate = jnp.dot(
                norm[...], wff_v[lp, :, 256 * j : 256 * (j + 1)], preferred_element_type=F32
            )
            up = jnp.dot(
                norm[...], wff_v[lp, :, FF + 256 * j : FF + 256 * (j + 1)],
                preferred_element_type=F32,
            )
            hid[:, 256 * j : 256 * (j + 1)] = (jax.nn.silu(gate) * up).astype(BF)
        landed(wdown_v.at[lp], w_recv.at[lp, 3])
        for j in range(3):
            cols = slice(256 * j, 256 * (j + 1))
            x[:, cols] = x[:, cols] + jnp.dot(
                hid[...], wdown_v[lp, :, cols], preferred_element_type=F32
            )

    @pl.when(active)
    def _():
        conditions()

        @pl.when(core == 1)
        def _():
            bias_on()

        @pl.when(s == 0)
        def _():
            enter_first()

        @pl.when(s == 1)
        def _():
            enter_second()

        @pl.when(plane > 0)
        def _():
            landed(xin, x_recv)
            x[...] = xin[...].astype(F32)

        @pl.loop(0, 2)
        def _(lp):
            layer(lp)

        @pl.when(plane < 3)
        def _():
            xtx[...] = x[...].astype(BF)
            pltpu.make_async_remote_copy(
                src_ref=xtx, dst_ref=xin, send_sem=x_send, recv_sem=x_recv,
                device_id=(s + 2, t), device_id_type=MESH,
            ).start()

        @pl.when(plane == 3)
        def _():
            done = normalise(x[...]).reshape(8, TOK_DEV, D)
            fin_tx[...] = jnp.concatenate(
                [done, jnp.zeros((8, COND_PAD - TOK_DEV, D), F32)], axis=1
            ).astype(BF)

            @pl.loop(0, 8)
            def _(j):
                send(fin_tx.at[j], fin, f_send.at[j], f_recv, pose, 8 * core + j)

    landed(fin, f_recv)
    out_ref[...] = fin[...].astype(F32)[:TOK_DEV].astype(BF)

    sent(c_src, c_send.at[0], 0, chip_of(s))

    @pl.when(last)
    def _():
        sent(c_src, c_send.at[1], 1, chip_of(s))

    @pl.when((s == 0) | ((s == 1) & last))
    def _():
        @pl.loop(0, POSES)
        def _(p):
            sent(a_src, a_send.at[p], s, chip_of(p))

    @pl.loop(0, POSES)
    def _(p):
        sent(d_src, d_send.at[p], s, chip_of(p))

    @pl.when(active)
    def _():
        for k, (src, dst) in enumerate(weights):
            landed(src, w_send.at[k])
        landed(cond_tx, m_send)
        bias_gone()

        @pl.when(plane < 3)
        def _():
            landed(xtx, x_send)

        @pl.when(plane == 3)
        def _():
            @pl.loop(0, 8)
            def _(j):
                sent(fin_tx.at[j], f_send.at[j], pose, 8 * core + j)


def body(
    coords, atom_single, token_atoms, cond_single, pair_bias, w_coord, w_in,
    w_ada, w_qkv, w_out, w_ff, w_down,
):
    counts = token_atoms.reshape(1, TOK_DEV)
    points = jnp.transpose(coords, (1, 0, 2))
    bias = pair_bias[0].reshape(HEADS * TOK_DEV, KEYS)
    vmem = pl.BlockSpec(memory_space=pltpu.VMEM)
    hbm = pl.BlockSpec(memory_space=pl.ANY)
    dma = pltpu.SemaphoreType.DMA
    rows = pl.pallas_call(
        kernel,
        out_shape=jax.ShapeDtypeStruct((TOK_DEV, D), BF),
        in_specs=[vmem, vmem, vmem, vmem, hbm, vmem, vmem, hbm, hbm, hbm, hbm, hbm],
        out_specs=vmem,
        scratch_shapes=[
            pltpu.VMEM((8, 256), F32),
            pltpu.VMEM((ATOM_PAD, 128), BF),
            pltpu.VMEM((COND_PAD, D), BF),
            pltpu.VMEM((8, 128), F32),
            pltpu.VMEM((TOK_DEVS, 8, 256), F32),
            pltpu.VMEM((TOK_DEVS, ATOM_PAD, 128), BF),
            pltpu.VMEM((TOK_DEVS, COND_PAD, D), BF),
            pltpu.VMEM((2, 8, HEADS * TOK_DEV, KEYS), BF),
            pltpu.VMEM((2, 4, ROWS, KEYS), BF),
            pltpu.VMEM((D, 4 * D), BF),
            pltpu.VMEM((2, D, 3 * D), BF),
            pltpu.VMEM((2, D, D), BF),
            pltpu.VMEM((2, D, 2 * FF), BF),
            pltpu.VMEM((2, FF, D), BF),
            pltpu.VMEM((2, 4, ROWS, D), F32),
            pltpu.VMEM((4, ROWS, D), F32),
            pltpu.VMEM((ROWS, D), F32),
            pltpu.VMEM((ROWS, D), BF),
            pltpu.VMEM((ROWS, D), BF),
            pltpu.VMEM((ROWS, D), BF),
            pltpu.VMEM((ROWS, D), BF),
            pltpu.VMEM((2, 2, KEYS, D), BF),
            pltpu.VMEM((ROWS, D), BF),
            pltpu.VMEM((ROWS, FF), BF),
            pltpu.VMEM((8, COND_PAD, D), BF),
            pltpu.VMEM((COND_PAD, D), BF),
            pltpu.VMEM((6 * ROWS, 256), BF),
            pltpu.VMEM((3, 6 * ROWS, KEYS), F32),
            pltpu.VMEM((HEADS * ROWS, KEYS), BF),
            pltpu.VMEM((HEADS, ROWS, 128), F32),
            dma((2,)), dma((TOK_DEVS,)),
            dma((POSES,)), dma((TOK_DEVS,)),
            dma((POSES,)), dma((TOK_DEVS,)),
            dma((2, 4)), dma((2, 4)),
            dma((2, 4, 2)), dma((2, 8, 2)),
            pltpu.SemaphoreType.REGULAR,
            dma((4,)), dma((2, 4)),
            dma,
            dma, dma,
            dma((2, 2)), dma((2, 2)),
            dma, dma,
            dma((8,)), dma,
        ],
        compiler_params=pltpu.CompilerParams(
            collective_id=0, has_side_effects=True, vmem_limit_bytes=60 << 20
        ),
    )(
        points, atom_single, counts, cond_single, bias, w_coord, w_in,
        w_ada[0], w_qkv[0], w_out[0], w_ff[0], w_down[0],
    )
    return rows[None]


def solution(mesh):
    return jax.shard_map(
        body,
        mesh=mesh,
        in_specs=(
            P("section", None, "tok"),
            P("tok", None),
            P("tok"),
            P("tok", None),
            P("section", None, "tok", None),
            P(),
            P(),
            P("section", None, None),
            P("section", None, None),
            P("section", None, None),
            P("section", None, None),
            P("section", None, None),
        ),
        out_specs=P("section", "tok", None),
        check_vma=False,
    )
```

```python
import jax
import jax.numpy as jnp
from jax import lax
from jax.experimental import pallas as pl
from jax.experimental.pallas import tpu as pltpu
from jax.sharding import PartitionSpec as P

HEADS = 16
HEAD_DIM = 48
FF = 1536
D = 768
POSES = 8
TOK_DEVS = 16
SECTIONS = 8
ROWS = 192
TOK_DEV = 24
ATOM_DEV = 216
ATOM_PAD = 224
COND_PAD = 32
KEYS = 384
QUARTER = 96
MESH = pl.DeviceIdType.MESH
BF = jnp.bfloat16
F32 = jnp.float32


def chip_of(pose):
    x = pose // 2
    return 4 * x + 2 * (pose % 2) + x % 2


def normalise(v):
    centre = v - jnp.mean(v, axis=-1, keepdims=True)
    return centre * lax.rsqrt(jnp.mean(centre * centre, axis=-1, keepdims=True) + 1e-05)


def landed(ref, sem):
    pltpu.make_async_copy(ref, ref, sem).wait()


def kernel(
    coords_ref, atom_ref, count_ref, cond_ref, bias_ref, wcoord_ref, win_ref,
    wada_ref, wqkv_ref, wout_ref, wff_ref, wdown_ref,
    out_ref,
    c_src, a_src, d_src, wc, c_all, a_all, d_all, b_all, relay,
    wada_v, wqkv_v, wout_v, wff_v, wdown_v,
    cond, cond_tx, x, xin, xtx, norm, q, kv, att, hid, fin_tx, fin,
    spread, scores, probs, inverse,
    c_send, c_recv, a_send, a_recv, d_send, d_recv, r_send, r_recv, b_send, b_recv, go,
    w_send, w_recv, ada_sem, m_send, m_recv, kv_send, kv_recv, x_send, x_recv, f_send, f_recv,
):
    s = lax.axis_index("section")
    t = lax.axis_index("tok")
    plane = s // 2
    core = lax.rem(s, 2)
    sibling = s + 1 - 2 * core
    cx, cz = t // 4, lax.rem(t, 4)
    active = lax.rem(cx + cz, 2) == 0
    pose = 2 * cx + cz // 2
    half = t // 8

    weights = ((wqkv_ref, wqkv_v), (wout_ref, wout_v), (wff_ref, wff_v), (wdown_ref, wdown_v))

    @pl.when(active)
    def _():
        pltpu.make_async_copy(wada_ref, wada_v, ada_sem).start()
        for k, (src, dst) in enumerate(weights):
            pltpu.make_async_copy(src, dst.at[core], w_recv.at[core, k]).start()

    barrier = pltpu.get_barrier_semaphore()

    def greet(section, tok):
        pl.semaphore_signal(barrier, inc=1, device_id=(section, tok), device_id_type=MESH)

    @pl.loop(1, TOK_DEVS)
    def _(j):
        greet(s, lax.rem(t + j, TOK_DEVS))

    def beside(k):
        step = 1 + 2 * lax.rem(k, 2)
        return jnp.where(
            k < 2, 4 * lax.rem(cx + step, 4) + cz, 4 * cx + lax.rem(cz + step, 4)
        )

    @pl.when(active)
    def _():
        @pl.loop(0, 4)
        def _(k):
            greet(sibling, beside(k))

        @pl.when((s == 0) & (pose != 0))
        def _():
            @pl.loop(0, TOK_DEVS)
            def _(j):
                greet(pose, j)

        @pl.when((s == 1) & (pose != 1))
        def _():
            greet(pose, TOK_DEVS - 1)

        @pl.when(plane > 0)
        def _():
            greet(s - 2, t)

    greet(sibling, t)

    fin_section, fin_tok = 6 + half, chip_of(s)
    fin_self = (fin_section == s) & (fin_tok == t)

    @pl.when(jnp.logical_not(fin_self))
    def _():
        greet(fin_section, fin_tok)

    c_src[...] = jnp.zeros_like(c_src)
    c_src[0:3, 0:ATOM_DEV] = coords_ref[...].reshape(3, ATOM_DEV)
    c_src[3:4, 0:TOK_DEV] = count_ref[...].astype(F32)
    wc[...] = jnp.zeros_like(wc)
    wc[0:3] = wcoord_ref[...]
    a_src[...] = jnp.concatenate(
        [atom_ref[...].astype(F32), jnp.zeros((ATOM_PAD - ATOM_DEV, 128), F32)], axis=0
    ).astype(BF)
    d_src[...] = jnp.concatenate(
        [cond_ref[...].astype(F32), jnp.zeros((COND_PAD - TOK_DEV, D), F32)], axis=0
    ).astype(BF)

    one = lambda flag: flag.astype(jnp.int32)
    last = t == TOK_DEVS - 1
    expected = 15 + 1 + 4 * (1 - one(active))
    expected += one(s != 0) + one(last & (s != 1))
    expected += one(active & (plane < 3))
    fin_here = active & (plane == 3)
    fin_own = fin_here & (pose == s) & (half == core)
    expected += 8 * one(fin_here) - one(fin_own)
    pl.semaphore_wait(barrier, expected)

    def send(src, dst, send_sem, recv_sem, section, tok):
        own = (section == s) & (tok == t)

        @pl.when(own)
        def _():
            pltpu.make_async_copy(src, dst, recv_sem).start()

        @pl.when(jnp.logical_not(own))
        def _():
            pltpu.make_async_remote_copy(
                src_ref=src, dst_ref=dst, send_sem=send_sem, recv_sem=recv_sem,
                device_id=(section, tok), device_id_type=MESH,
            ).start()

    def sent(src, send_sem, section, tok):
        @pl.when(jnp.logical_not((section == s) & (tok == t)))
        def _():
            landed(src, send_sem)

    send(c_src, c_all.at[t], c_send.at[0], c_recv.at[t], 0, chip_of(s))

    @pl.when(last)
    def _():
        send(c_src, c_all.at[t], c_send.at[1], c_recv.at[t], 1, chip_of(s))

    @pl.when((s == 0) | ((s == 1) & last))
    def _():
        @pl.loop(0, POSES)
        def _(p):
            send(a_src, a_all.at[t], a_send.at[p], a_recv.at[t], s, chip_of(p))

    @pl.loop(0, POSES)
    def _(p):
        send(d_src, d_all.at[t], d_send.at[p], d_recv.at[t], s, chip_of(p))

    quarter = 2 * lax.rem(cx, 2) + lax.rem(cz + 2 * (cx // 2), 4) // 2

    def bias_part(k):
        return bias_ref.at[pl.ds(pl.multiple_of(QUARTER * k, QUARTER), QUARTER)]

    def relay_chip(k, e):
        first = k // 2
        return 4 * (first + 2 * e) + lax.rem(2 * lax.rem(k, 2) + 1 - first + 2 * e, 4)

    def bias_out():
        @pl.loop(0, 8)
        def _(j):
            k, e = lax.rem(j, 4), j // 4
            send(bias_part(k), relay.at[t], r_send.at[j], r_recv.at[t], s, relay_chip(k, e))

    def bias_out_gone():
        @pl.loop(0, 8)
        def _(j):
            k, e = lax.rem(j, 4), j // 4
            sent(bias_part(k), r_send.at[j], s, relay_chip(k, e))

    def bias_on():
        @pl.loop(0, 4)
        def _(g):
            @pl.loop(0, 4)
            def _(j):
                landed(relay.at[4 * g + j], r_recv.at[4 * g + j])

            @pl.loop(0, 4)
            def _(k):
                pltpu.make_async_remote_copy(
                    src_ref=relay.at[pl.ds(4 * g, 4)],
                    dst_ref=b_all.at[
                        core, pl.ds(4 * lax.rem(g, 2), 4),
                        pl.ds(pl.multiple_of(QUARTER * quarter, QUARTER), QUARTER),
                    ],
                    send_sem=b_send.at[g, k], recv_sem=b_recv.at[core, lax.rem(g, 2), quarter],
                    device_id=(2 * plane + g // 2, beside(k)), device_id_type=MESH,
                ).start()

    def bias_gone():
        @pl.loop(0, 4)
        def _(g):
            @pl.loop(0, 4)
            def _(k):
                landed(relay.at[pl.ds(4 * g, 4)], b_send.at[g, k])

    def tell():
        pl.semaphore_signal(go, inc=1, device_id=(sibling, t), device_id_type=MESH)

    @pl.when(active)
    def _():
        for k, (src, dst) in enumerate(weights):
            pltpu.make_async_remote_copy(
                src_ref=src, dst_ref=dst.at[core], send_sem=w_send.at[k],
                recv_sem=w_recv.at[core, k], device_id=(sibling, t), device_id_type=MESH,
            ).start()

    @pl.when(core == 0)
    def _():
        bias_out()

    @pl.when((core == 0) & jnp.logical_not(active))
    def _():
        bias_out_gone()
        tell()
        bias_on()
        bias_gone()
        tell()

    @pl.when((core == 1) & jnp.logical_not(active))
    def _():
        pl.semaphore_wait(go, 1)
        bias_out()
        pl.semaphore_wait(go, 1)
        bias_on()
        bias_out_gone()
        bias_gone()

    def act_of(points, single):
        moved = lax.dot_general(
            points, wc[...], (((0,), (0,)), ((), ())),
            precision=lax.Precision.HIGHEST, preferred_element_type=F32,
        )
        return jnp.maximum(single.astype(F32) + moved[:ATOM_PAD], 0.0)

    def enter_first():
        @pl.loop(0, TOK_DEVS)
        def _(j):
            landed(c_all.at[j], c_recv.at[j])

        lane8 = lax.broadcasted_iota(jnp.int32, (TOK_DEV, 128), 1)
        place8 = lax.broadcasted_iota(jnp.int32, (TOK_DEV, 128), 0)
        count_blocks, start_blocks = [], []
        total = jnp.zeros((TOK_DEV, 1), F32)
        for j in range(8):
            row = jnp.broadcast_to(c_all[j, 3:4, 0:128], (TOK_DEV, 128))
            mine = jnp.where(lane8 == place8, row, 0.0)
            ahead = jnp.where(lane8 < place8, row, 0.0)
            count_blocks.append(jnp.sum(mine, axis=1, keepdims=True))
            start_blocks.append(total + jnp.sum(ahead, axis=1, keepdims=True))
            total = total + jnp.sum(row, axis=1, keepdims=True)
        counts = jnp.broadcast_to(jnp.concatenate(count_blocks, axis=0), (ROWS, 128))
        starts = jnp.broadcast_to(jnp.concatenate(start_blocks, axis=0), (ROWS, 128))
        ends = starts + counts
        lower = jnp.concatenate([starts, starts], axis=1)[:, :ATOM_PAD]
        upper = jnp.concatenate([ends, ends], axis=1)[:, :ATOM_PAD]
        lane = lax.broadcasted_iota(jnp.int32, (ROWS, ATOM_PAD), 1)

        @pl.loop(0, TOK_DEVS)
        def _(j):
            landed(a_all.at[j], a_recv.at[j])

        pooled = jnp.zeros((ROWS, 128), F32)
        for j in range(TOK_DEVS):
            place = (lane + j * ATOM_DEV).astype(F32)
            inside = (place >= lower) & (place < upper) & (lane < ATOM_DEV)
            member = jnp.where(inside, 1.0, 0.0).astype(BF)
            act = act_of(c_all[j], a_all[j]).astype(BF)
            pooled = pooled + jnp.dot(member, act, preferred_element_type=F32)
        averaged = (pooled / counts).astype(BF)
        x[...] = jnp.dot(averaged, win_ref[...], preferred_element_type=F32)

    def enter_second():
        j = TOK_DEVS - 1
        landed(c_all.at[j], c_recv.at[j])
        landed(a_all.at[j], a_recv.at[j])
        act = act_of(c_all[j], a_all[j])[ATOM_DEV - ROWS : ATOM_DEV]
        x[...] = jnp.dot(act.astype(BF), win_ref[...], preferred_element_type=F32)

    def conditions():
        @pl.loop(0, TOK_DEVS)
        def _(j):
            landed(d_all.at[j], d_recv.at[j])

        landed(wada_ref, ada_sem)

        def rows_for(which, store):
            rows = d_all[pl.ds(8 * which, 8)].reshape(8 * COND_PAD, D)
            for k in range(4):
                full = jnp.dot(
                    rows, wada_v[:, D * k : D * (k + 1)], preferred_element_type=F32
                )
                value = full.reshape(8, COND_PAD, D)[:, :TOK_DEV].reshape(ROWS, D)
                store(k, jax.nn.sigmoid(value) if k % 2 == 0 else value)

        def to_send(k, value):
            cond_tx[k] = value

        def to_keep(k, value):
            cond[core, k] = value

        rows_for(1 - core, to_send)
        pltpu.make_async_remote_copy(
            src_ref=cond_tx, dst_ref=cond.at[core], send_sem=m_send, recv_sem=m_recv,
            device_id=(sibling, t), device_id_type=MESH,
        ).start()
        rows_for(core, to_keep)

    own_rows = pl.ds(pl.multiple_of(core * ROWS, ROWS), ROWS)
    other_rows = pl.ds(pl.multiple_of((1 - core) * ROWS, ROWS), ROWS)

    def layer(lp):
        @pl.when(lp != core)
        def _():
            landed(cond.at[lp], m_recv)

        norm[...] = (normalise(x[...]) * cond[lp, 0] + cond[lp, 1]).astype(BF)
        landed(wqkv_v.at[lp], w_recv.at[lp, 0])

        def project(column, width):
            return jnp.dot(
                norm[...], wqkv_v[lp, :, column : column + width], preferred_element_type=F32
            ).astype(BF)

        for part in range(2):
            for j in range(3):
                kv[lp, part, own_rows, 256 * j : 256 * (j + 1)] = project(
                    D * (part + 1) + 256 * j, 256
                )
            pltpu.make_async_remote_copy(
                src_ref=kv.at[lp, part, own_rows], dst_ref=kv.at[lp, part, own_rows],
                send_sem=kv_send.at[lp, part], recv_sem=kv_recv.at[lp, part],
                device_id=(sibling, t), device_id_type=MESH,
            ).start()
        for j in range(3):
            q[:, 256 * j : 256 * (j + 1)] = project(256 * j, 256)

        @pl.loop(0, 8)
        def _(j):
            g, k = j // 4, lax.rem(j, 4)
            block = b_all.at[
                lp, pl.ds(4 * g, 4), pl.ds(pl.multiple_of(QUARTER * k, QUARTER), QUARTER)
            ]
            landed(block, b_recv.at[lp, g, k])

        for part in range(2):
            landed(kv.at[lp, part, other_rows], kv_recv.at[lp, part])

        for w in range(3):
            lanes = slice(256 * w, 256 * (w + 1))
            window = q[:, lanes]
            lane = lax.broadcasted_iota(jnp.int32, (1, 256), 1) + 256 * w
            for k in range(6):
                low = HEAD_DIM * (5 * w + k)
                mask = jnp.where((lane >= low) & (lane < low + HEAD_DIM), 1.0, 0.0).astype(BF)
                spread[ROWS * k : ROWS * (k + 1)] = window * mask
            scores[w] = lax.dot_general(
                spread[...], kv[lp, 0, :, lanes], (((1,), (1,)), ((), ())),
                preferred_element_type=F32,
            )

        for pair in range(8):
            bias = b_all[lp, :, 48 * pair : 48 * (pair + 1), :].astype(F32)
            for e in range(2):
                head = 2 * pair + e
                w = min(head // 5, 2)
                k = head - 5 * w
                raw = scores[w, ROWS * k : ROWS * (k + 1)]
                if k == 0 and w > 0:
                    raw = raw + scores[w - 1, 5 * ROWS : 6 * ROWS]
                logits = raw * HEAD_DIM ** (-0.5) + bias[
                    :, TOK_DEV * e : TOK_DEV * (e + 1)
                ].reshape(ROWS, KEYS)
                top = jnp.max(logits, axis=-1, keepdims=True)
                weight = jnp.exp(logits - top)
                total = jnp.sum(weight, axis=-1, keepdims=True)
                inverse[head] = jnp.broadcast_to(1.0 / total, (ROWS, 128))
                probs[ROWS * head : ROWS * (head + 1)] = weight.astype(BF)

        for w in range(3):
            lanes = slice(256 * w, 256 * (w + 1))
            out = jnp.dot(
                probs[ROWS * 5 * w : ROWS * (5 * w + 6)], kv[lp, 1, :, lanes],
                preferred_element_type=F32,
            )
            lane = lax.broadcasted_iota(jnp.int32, (1, 256), 1) + 256 * w
            whole = jnp.zeros((ROWS, 256), F32)
            for k in range(6):
                low = HEAD_DIM * (5 * w + k)
                factor = inverse[5 * w + k]
                piece = out[ROWS * k : ROWS * (k + 1)] * jnp.concatenate([factor, factor], axis=1)
                whole = jnp.where(lane >= low, piece, whole)
            att[:, lanes] = whole.astype(BF)

        for part in range(2):
            landed(kv.at[lp, part, own_rows], kv_send.at[lp, part])

        landed(wout_v.at[lp], w_recv.at[lp, 1])
        for j in range(3):
            cols = slice(256 * j, 256 * (j + 1))
            x[:, cols] = x[:, cols] + jnp.dot(
                att[...], wout_v[lp, :, cols], preferred_element_type=F32
            )
        norm[...] = (normalise(x[...]) * cond[lp, 2] + cond[lp, 3]).astype(BF)
        landed(wff_v.at[lp], w_recv.at[lp, 2])
        for j in range(6):
            gate = jnp.dot(
                norm[...], wff_v[lp, :, 256 * j : 256 * (j + 1)], preferred_element_type=F32
            )
            up = jnp.dot(
                norm[...], wff_v[lp, :, FF + 256 * j : FF + 256 * (j + 1)],
                preferred_element_type=F32,
            )
            hid[:, 256 * j : 256 * (j + 1)] = (jax.nn.silu(gate) * up).astype(BF)
        landed(wdown_v.at[lp], w_recv.at[lp, 3])
        for j in range(3):
            cols = slice(256 * j, 256 * (j + 1))
            x[:, cols] = x[:, cols] + jnp.dot(
                hid[...], wdown_v[lp, :, cols], preferred_element_type=F32
            )

    @pl.when(active)
    def _():
        conditions()

        @pl.when(core == 1)
        def _():
            bias_out()

        @pl.when(s == 0)
        def _():
            enter_first()

        @pl.when(s == 1)
        def _():
            enter_second()

        @pl.when(plane > 0)
        def _():
            landed(xin, x_recv)
            x[...] = xin[...].astype(F32)

        @pl.loop(0, 2)
        def _(lp):
            layer(lp)

        @pl.when(plane < 3)
        def _():
            xtx[...] = x[...].astype(BF)
            pltpu.make_async_remote_copy(
                src_ref=xtx, dst_ref=xin, send_sem=x_send, recv_sem=x_recv,
                device_id=(s + 2, t), device_id_type=MESH,
            ).start()

        @pl.when(plane == 3)
        def _():
            done = normalise(x[...]).reshape(8, TOK_DEV, D)
            fin_tx[...] = jnp.concatenate(
                [done, jnp.zeros((8, COND_PAD - TOK_DEV, D), F32)], axis=1
            ).astype(BF)

            @pl.loop(0, 8)
            def _(j):
                send(fin_tx.at[j], fin, f_send.at[j], f_recv, pose, 8 * core + j)

    landed(fin, f_recv)
    out_ref[...] = fin[...].astype(F32)[:TOK_DEV].astype(BF)

    sent(c_src, c_send.at[0], 0, chip_of(s))

    @pl.when(last)
    def _():
        sent(c_src, c_send.at[1], 1, chip_of(s))

    @pl.when((s == 0) | ((s == 1) & last))
    def _():
        @pl.loop(0, POSES)
        def _(p):
            sent(a_src, a_send.at[p], s, chip_of(p))

    @pl.loop(0, POSES)
    def _(p):
        sent(d_src, d_send.at[p], s, chip_of(p))

    @pl.when(active)
    def _():
        for k, (src, dst) in enumerate(weights):
            landed(src, w_send.at[k])
        landed(cond_tx, m_send)
        bias_out_gone()

        @pl.when(plane < 3)
        def _():
            landed(xtx, x_send)

        @pl.when(plane == 3)
        def _():
            @pl.loop(0, 8)
            def _(j):
                sent(fin_tx.at[j], f_send.at[j], pose, 8 * core + j)


def body(
    coords, atom_single, token_atoms, cond_single, pair_bias, w_coord, w_in,
    w_ada, w_qkv, w_out, w_ff, w_down,
):
    counts = token_atoms.reshape(1, TOK_DEV)
    points = jnp.transpose(coords, (1, 0, 2))
    bias = pair_bias[0].reshape(HEADS * TOK_DEV, KEYS)
    vmem = pl.BlockSpec(memory_space=pltpu.VMEM)
    hbm = pl.BlockSpec(memory_space=pl.ANY)
    dma = pltpu.SemaphoreType.DMA
    rows = pl.pallas_call(
        kernel,
        out_shape=jax.ShapeDtypeStruct((TOK_DEV, D), BF),
        in_specs=[vmem, vmem, vmem, vmem, hbm, vmem, vmem, hbm, hbm, hbm, hbm, hbm],
        out_specs=vmem,
        scratch_shapes=[
            pltpu.VMEM((8, 256), F32),
            pltpu.VMEM((ATOM_PAD, 128), BF),
            pltpu.VMEM((COND_PAD, D), BF),
            pltpu.VMEM((8, 128), F32),
            pltpu.VMEM((TOK_DEVS, 8, 256), F32),
            pltpu.VMEM((TOK_DEVS, ATOM_PAD, 128), BF),
            pltpu.VMEM((TOK_DEVS, COND_PAD, D), BF),
            pltpu.VMEM((2, 8, HEADS * TOK_DEV, KEYS), BF),
            pltpu.VMEM((TOK_DEVS, QUARTER, KEYS), BF),
            pltpu.VMEM((D, 4 * D), BF),
            pltpu.VMEM((2, D, 3 * D), BF),
            pltpu.VMEM((2, D, D), BF),
            pltpu.VMEM((2, D, 2 * FF), BF),
            pltpu.VMEM((2, FF, D), BF),
            pltpu.VMEM((2, 4, ROWS, D), F32),
            pltpu.VMEM((4, ROWS, D), F32),
            pltpu.VMEM((ROWS, D), F32),
            pltpu.VMEM((ROWS, D), BF),
            pltpu.VMEM((ROWS, D), BF),
            pltpu.VMEM((ROWS, D), BF),
            pltpu.VMEM((ROWS, D), BF),
            pltpu.VMEM((2, 2, KEYS, D), BF),
            pltpu.VMEM((ROWS, D), BF),
            pltpu.VMEM((ROWS, FF), BF),
            pltpu.VMEM((8, COND_PAD, D), BF),
            pltpu.VMEM((COND_PAD, D), BF),
            pltpu.VMEM((6 * ROWS, 256), BF),
            pltpu.VMEM((3, 6 * ROWS, KEYS), F32),
            pltpu.VMEM((HEADS * ROWS, KEYS), BF),
            pltpu.VMEM((HEADS, ROWS, 128), F32),
            dma((2,)), dma((TOK_DEVS,)),
            dma((POSES,)), dma((TOK_DEVS,)),
            dma((POSES,)), dma((TOK_DEVS,)),
            dma((8,)), dma((TOK_DEVS,)),
            dma((4, 4)), dma((2, 2, 4)),
            pltpu.SemaphoreType.REGULAR,
            dma((4,)), dma((2, 4)),
            dma,
            dma, dma,
            dma((2, 2)), dma((2, 2)),
            dma, dma,
            dma((8,)), dma,
        ],
        compiler_params=pltpu.CompilerParams(
            collective_id=0, has_side_effects=True, vmem_limit_bytes=60 << 20
        ),
    )(
        points, atom_single, counts, cond_single, bias, w_coord, w_in,
        w_ada[0], w_qkv[0], w_out[0], w_ff[0], w_down[0],
    )
    return rows[None]


def solution(mesh):
    return jax.shard_map(
        body,
        mesh=mesh,
        in_specs=(
            P("section", None, "tok"),
            P("tok", None),
            P("tok"),
            P("tok", None),
            P("section", None, "tok", None),
            P(),
            P(),
            P("section", None, None),
            P("section", None, None),
            P("section", None, None),
            P("section", None, None),
            P("section", None, None),
        ),
        out_specs=P("section", "tok", None),
        check_vma=False,
    )
```

```python
import jax
import jax.numpy as jnp
from jax import lax
from jax.experimental import pallas as pl
from jax.experimental.pallas import tpu as pltpu
from jax.sharding import PartitionSpec as P

HEADS = 16
HEAD_DIM = 48
FF = 1536
D = 768
POSES = 8
TOK_DEVS = 16
SECTIONS = 8
ROWS = 192
TOK_DEV = 24
ATOM_DEV = 216
ATOM_PAD = 224
COND_PAD = 32
KEYS = 384
QUARTER = 96
MESH = pl.DeviceIdType.MESH
BF = jnp.bfloat16
F32 = jnp.float32


def chip_of(pose):
    x = pose // 2
    return 4 * x + 2 * (pose % 2) + x % 2


def normalise(v):
    centre = v - jnp.mean(v, axis=-1, keepdims=True)
    return centre * lax.rsqrt(jnp.mean(centre * centre, axis=-1, keepdims=True) + 1e-05)


def landed(ref, sem):
    pltpu.make_async_copy(ref, ref, sem).wait()


def kernel(
    coords_ref, atom_ref, count_ref, cond_ref, bias_ref, wcoord_ref, win_ref,
    wada_ref, wqkv_ref, wout_ref, wff_ref, wdown_ref,
    out_ref,
    c_src, a_src, d_src, wc, c_all, a_all, d_all, b_all, relay,
    wada_v, wqkv_v, wout_v, wff_v, wdown_v,
    cond, cond_tx, x, xin, xtx, norm, q, kv, att, hid, fin_tx, fin,
    spread, scores, probs, inverse,
    c_send, c_recv, a_send, a_recv, d_send, d_recv, r_send, r_recv, b_send, b_recv, go,
    w_send, w_recv, ada_sem, p_send, p_recv, m_send, m_recv, kv_send, kv_recv, x_send, x_recv, f_send, f_recv,
):
    s = lax.axis_index("section")
    t = lax.axis_index("tok")
    plane = s // 2
    core = lax.rem(s, 2)
    sibling = s + 1 - 2 * core
    cx, cz = t // 4, lax.rem(t, 4)
    active = lax.rem(cx + cz, 2) == 0
    pose = 2 * cx + cz // 2
    half = t // 8

    weights = ((wqkv_ref, wqkv_v), (wout_ref, wout_v), (wff_ref, wff_v), (wdown_ref, wdown_v))

    @pl.when(active)
    def _():
        pltpu.make_async_copy(wada_ref, wada_v, ada_sem).start()
        for k, (src, dst) in enumerate(weights):
            pltpu.make_async_copy(src, dst.at[core], w_recv.at[core, k]).start()

    barrier = pltpu.get_barrier_semaphore()

    def greet(section, tok):
        pl.semaphore_signal(barrier, inc=1, device_id=(section, tok), device_id_type=MESH)

    @pl.loop(1, TOK_DEVS)
    def _(j):
        greet(s, lax.rem(t + j, TOK_DEVS))

    def beside(k):
        step = 1 + 2 * lax.rem(k, 2)
        return jnp.where(
            k < 2, 4 * lax.rem(cx + step, 4) + cz, 4 * cx + lax.rem(cz + step, 4)
        )

    @pl.when(active)
    def _():
        @pl.loop(0, 4)
        def _(k):
            greet(sibling, beside(k))

        @pl.when((s == 0) & (pose != 0))
        def _():
            @pl.loop(0, TOK_DEVS)
            def _(j):
                greet(pose, j)

        @pl.when((s == 1) & (pose != 1))
        def _():
            greet(pose, TOK_DEVS - 1)

        @pl.when(plane > 0)
        def _():
            greet(s - 2, t)

    greet(sibling, t)

    fin_section, fin_tok = 6 + half, chip_of(s)
    fin_self = (fin_section == s) & (fin_tok == t)

    @pl.when(jnp.logical_not(fin_self))
    def _():
        greet(fin_section, fin_tok)

    c_src[...] = jnp.zeros_like(c_src)
    c_src[0:3, 0:ATOM_DEV] = coords_ref[...].reshape(3, ATOM_DEV)
    c_src[3:4, 0:TOK_DEV] = count_ref[...].astype(F32)
    wc[...] = jnp.zeros_like(wc)
    wc[0:3] = wcoord_ref[...]
    a_src[...] = jnp.concatenate(
        [atom_ref[...].astype(F32), jnp.zeros((ATOM_PAD - ATOM_DEV, 128), F32)], axis=0
    ).astype(BF)
    single = cond_ref[...].astype(F32)
    d_src[...] = jnp.concatenate([single[:, :KEYS], single[:, KEYS:]], axis=0).astype(BF)

    one = lambda flag: flag.astype(jnp.int32)
    last = t == TOK_DEVS - 1
    expected = 15 + 1 + 4 * (1 - one(active))
    expected += one(s != 0) + one(last & (s != 1))
    expected += one(active & (plane < 3))
    fin_here = active & (plane == 3)
    fin_own = fin_here & (pose == s) & (half == core)
    expected += 8 * one(fin_here) - one(fin_own)
    pl.semaphore_wait(barrier, expected)

    def send(src, dst, send_sem, recv_sem, section, tok):
        own = (section == s) & (tok == t)

        @pl.when(own)
        def _():
            pltpu.make_async_copy(src, dst, recv_sem).start()

        @pl.when(jnp.logical_not(own))
        def _():
            pltpu.make_async_remote_copy(
                src_ref=src, dst_ref=dst, send_sem=send_sem, recv_sem=recv_sem,
                device_id=(section, tok), device_id_type=MESH,
            ).start()

    def sent(src, send_sem, section, tok):
        @pl.when(jnp.logical_not((section == s) & (tok == t)))
        def _():
            landed(src, send_sem)

    send(c_src, c_all.at[t], c_send.at[0], c_recv.at[t], 0, chip_of(s))

    @pl.when(last)
    def _():
        send(c_src, c_all.at[t], c_send.at[1], c_recv.at[t], 1, chip_of(s))

    quarter = 2 * lax.rem(cx, 2) + lax.rem(cz + 2 * (cx // 2), 4) // 2

    def bias_part(k):
        return bias_ref.at[pl.ds(pl.multiple_of(QUARTER * k, QUARTER), QUARTER)]

    def relay_chip(k, e):
        first = k // 2
        return 4 * (first + 2 * e) + lax.rem(2 * lax.rem(k, 2) + 1 - first + 2 * e, 4)

    def bias_out():
        @pl.loop(0, 8)
        def _(j):
            k, e = lax.rem(j, 4), j // 4
            send(bias_part(k), relay.at[t], r_send.at[j], r_recv.at[t], s, relay_chip(k, e))

    def bias_out_gone():
        @pl.loop(0, 8)
        def _(j):
            k, e = lax.rem(j, 4), j // 4
            sent(bias_part(k), r_send.at[j], s, relay_chip(k, e))

    def bias_on():
        @pl.loop(0, TOK_DEVS)
        def _(j):
            origin = lax.rem(t + j, TOK_DEVS)
            landed(relay.at[origin], r_recv.at[origin])

            @pl.loop(0, 4)
            def _(k):
                pltpu.make_async_remote_copy(
                    src_ref=relay.at[origin],
                    dst_ref=b_all.at[
                        core, lax.rem(origin, 8),
                        pl.ds(pl.multiple_of(QUARTER * quarter, QUARTER), QUARTER),
                    ],
                    send_sem=b_send.at[j, k], recv_sem=b_recv.at[core],
                    device_id=(2 * plane + origin // 8, beside(k)), device_id_type=MESH,
                ).start()

    def bias_gone(low, high):
        @pl.loop(low, high)
        def _(j):
            @pl.loop(0, 4)
            def _(k):
                landed(relay.at[0], b_send.at[j, k])

    def tell():
        pl.semaphore_signal(go, inc=1, device_id=(sibling, t), device_id_type=MESH)

    @pl.when(core == 0)
    def _():
        bias_out()

    @pl.when((s == 0) | ((s == 1) & last))
    def _():
        @pl.loop(0, POSES)
        def _(p):
            send(a_src, a_all.at[t], a_send.at[p], a_recv.at[t], s, chip_of(p))

    @pl.when(core == 1)
    def _():
        @pl.loop(0, POSES)
        def _(p):
            send(d_src, d_all.at[t], d_send.at[p], d_recv.at[t], s, chip_of(p))

    @pl.when(active)
    def _():
        for k, (src, dst) in enumerate(weights):
            pltpu.make_async_remote_copy(
                src_ref=src, dst_ref=dst.at[core], send_sem=w_send.at[k],
                recv_sem=w_recv.at[core, k], device_id=(sibling, t), device_id_type=MESH,
            ).start()

    @pl.when(core == 0)
    def _():
        bias_out_gone()
        tell()

    @pl.when(core == 1)
    def _():
        pl.semaphore_wait(go, 1)
        bias_out()

    @pl.when((core == 0) & jnp.logical_not(active))
    def _():
        bias_on()
        bias_gone(0, 12)
        tell()
        bias_gone(12, 16)

    @pl.when((core == 1) & jnp.logical_not(active))
    def _():
        pl.semaphore_wait(go, 1)
        bias_on()
        bias_out_gone()
        bias_gone(0, 16)

    def act_of(points, single):
        moved = lax.dot_general(
            points, wc[...], (((0,), (0,)), ((), ())),
            precision=lax.Precision.HIGHEST, preferred_element_type=F32,
        )
        return jnp.maximum(single.astype(F32) + moved[:ATOM_PAD], 0.0)

    def enter_first():
        @pl.loop(0, TOK_DEVS)
        def _(j):
            landed(c_all.at[j], c_recv.at[j])

        lane8 = lax.broadcasted_iota(jnp.int32, (TOK_DEV, 128), 1)
        place8 = lax.broadcasted_iota(jnp.int32, (TOK_DEV, 128), 0)
        count_blocks, start_blocks = [], []
        total = jnp.zeros((TOK_DEV, 1), F32)
        for j in range(8):
            row = jnp.broadcast_to(c_all[j, 3:4, 0:128], (TOK_DEV, 128))
            mine = jnp.where(lane8 == place8, row, 0.0)
            ahead = jnp.where(lane8 < place8, row, 0.0)
            count_blocks.append(jnp.sum(mine, axis=1, keepdims=True))
            start_blocks.append(total + jnp.sum(ahead, axis=1, keepdims=True))
            total = total + jnp.sum(row, axis=1, keepdims=True)
        counts = jnp.broadcast_to(jnp.concatenate(count_blocks, axis=0), (ROWS, 128))
        starts = jnp.broadcast_to(jnp.concatenate(start_blocks, axis=0), (ROWS, 128))
        ends = starts + counts
        lower = jnp.concatenate([starts, starts], axis=1)[:, :ATOM_PAD]
        upper = jnp.concatenate([ends, ends], axis=1)[:, :ATOM_PAD]
        lane = lax.broadcasted_iota(jnp.int32, (ROWS, ATOM_PAD), 1)

        @pl.loop(0, TOK_DEVS)
        def _(j):
            landed(a_all.at[j], a_recv.at[j])

        pooled = jnp.zeros((ROWS, 128), F32)
        for j in range(TOK_DEVS):
            place = (lane + j * ATOM_DEV).astype(F32)
            inside = (place >= lower) & (place < upper) & (lane < ATOM_DEV)
            member = jnp.where(inside, 1.0, 0.0).astype(BF)
            act = act_of(c_all[j], a_all[j]).astype(BF)
            pooled = pooled + jnp.dot(member, act, preferred_element_type=F32)
        averaged = (pooled / counts).astype(BF)
        x[...] = jnp.dot(averaged, win_ref[...], preferred_element_type=F32)

    def enter_second():
        j = TOK_DEVS - 1
        landed(c_all.at[j], c_recv.at[j])
        landed(a_all.at[j], a_recv.at[j])
        act = act_of(c_all[j], a_all[j])[ATOM_DEV - ROWS : ATOM_DEV]
        x[...] = jnp.dot(act.astype(BF), win_ref[...], preferred_element_type=F32)

    def conditions():
        @pl.when(core == 1)
        def _():
            @pl.loop(0, TOK_DEVS)
            def _(j):
                landed(d_all.at[j], d_recv.at[j])

            pltpu.make_async_remote_copy(
                src_ref=d_all, dst_ref=d_all, send_sem=p_send, recv_sem=p_recv,
                device_id=(sibling, t), device_id_type=MESH,
            ).start()

        @pl.when(core == 0)
        def _():
            landed(d_all, p_recv)

        landed(wada_ref, ada_sem)

        def rows_for(which, store):
            blocks = d_all[pl.ds(8 * which, 8)].astype(F32)
            norm[...] = jnp.concatenate(
                [blocks[:, :TOK_DEV].reshape(ROWS, KEYS), blocks[:, TOK_DEV:].reshape(ROWS, KEYS)],
                axis=1,
            ).astype(BF)
            for k in range(4):
                value = jnp.dot(
                    norm[...], wada_v[:, D * k : D * (k + 1)], preferred_element_type=F32
                )
                store(k, jax.nn.sigmoid(value) if k % 2 == 0 else value)

        def to_send(k, value):
            cond_tx[k] = value

        def to_keep(k, value):
            cond[core, k] = value

        rows_for(1 - core, to_send)
        pltpu.make_async_remote_copy(
            src_ref=cond_tx, dst_ref=cond.at[core], send_sem=m_send, recv_sem=m_recv,
            device_id=(sibling, t), device_id_type=MESH,
        ).start()
        rows_for(core, to_keep)

    own_rows = pl.ds(pl.multiple_of(core * ROWS, ROWS), ROWS)
    other_rows = pl.ds(pl.multiple_of((1 - core) * ROWS, ROWS), ROWS)

    def layer(lp):
        @pl.when(lp != core)
        def _():
            landed(cond.at[lp], m_recv)

        norm[...] = (normalise(x[...]) * cond[lp, 0] + cond[lp, 1]).astype(BF)
        landed(wqkv_v.at[lp], w_recv.at[lp, 0])

        def project(column, width):
            return jnp.dot(
                norm[...], wqkv_v[lp, :, column : column + width], preferred_element_type=F32
            ).astype(BF)

        def tile(part, j, rows):
            return kv.at[lp, part, j, rows]

        for part in range(2):
            for j in range(3):
                kv[lp, part, j, own_rows, :] = project(D * (part + 1) + 256 * j, 256)
            pltpu.make_async_remote_copy(
                src_ref=kv.at[lp, part, :, own_rows], dst_ref=kv.at[lp, part, :, own_rows],
                send_sem=kv_send.at[lp, part, 0], recv_sem=kv_recv.at[lp, part, 0],
                device_id=(sibling, t), device_id_type=MESH,
            ).start()
        for j in range(3):
            q[:, 256 * j : 256 * (j + 1)] = project(256 * j, 256)

        def score(w):
            window = q[:, 256 * w : 256 * (w + 1)]
            lane = lax.broadcasted_iota(jnp.int32, (1, 256), 1) + 256 * w
            for k in range(6):
                low = HEAD_DIM * (5 * w + k)
                mask = jnp.where((lane >= low) & (lane < low + HEAD_DIM), 1.0, 0.0).astype(BF)
                spread[w, ROWS * k : ROWS * (k + 1)] = window * mask
            scores[w] = lax.dot_general(
                spread[w], kv[lp, 0, w], (((1,), (1,)), ((), ())), preferred_element_type=F32
            )

        def soften(head):
            pair, e = head // 2, head % 2
            bias = b_all[lp, :, 48 * pair : 48 * (pair + 1), :].astype(F32)
            w = min(head // 5, 2)
            k = head - 5 * w
            raw = scores[w, ROWS * k : ROWS * (k + 1)]
            if k == 0 and w > 0:
                raw = raw + scores[w - 1, 5 * ROWS : 6 * ROWS]
            logits = raw * HEAD_DIM ** (-0.5) + bias[
                :, TOK_DEV * e : TOK_DEV * (e + 1)
            ].reshape(ROWS, KEYS)
            top = jnp.max(logits, axis=-1, keepdims=True)
            weight = jnp.exp(logits - top)
            total = jnp.sum(weight, axis=-1, keepdims=True)
            inverse[head] = jnp.broadcast_to(1.0 / total, (ROWS, 128))
            probs[ROWS * head : ROWS * (head + 1)] = weight.astype(BF)

        def gather(w):
            out = jnp.dot(
                probs[ROWS * 5 * w : ROWS * (5 * w + 6)], kv[lp, 1, w], preferred_element_type=F32
            )
            lane = lax.broadcasted_iota(jnp.int32, (1, 256), 1) + 256 * w
            whole = jnp.zeros((ROWS, 256), F32)
            for k in range(6):
                low = HEAD_DIM * (5 * w + k)
                factor = inverse[5 * w + k]
                piece = out[ROWS * k : ROWS * (k + 1)] * jnp.concatenate([factor, factor], axis=1)
                whole = jnp.where(lane >= low, piece, whole)
            att[:, 256 * w : 256 * (w + 1)] = whole.astype(BF)

        landed(kv.at[lp, 0, :, other_rows], kv_recv.at[lp, 0, 0])
        score(0)
        score(1)
        score(2)
        landed(kv.at[lp, 1, :, other_rows], kv_recv.at[lp, 1, 0])

        landed(b_all.at[lp], b_recv.at[lp])
        for head in range(0, 6):
            soften(head)
        gather(0)
        for head in range(6, 11):
            soften(head)
        gather(1)
        for head in range(11, 16):
            soften(head)
        gather(2)

        for part in range(2):
            landed(kv.at[lp, part, :, own_rows], kv_send.at[lp, part, 0])

        landed(wout_v.at[lp], w_recv.at[lp, 1])
        for j in range(3):
            cols = slice(256 * j, 256 * (j + 1))
            x[:, cols] = x[:, cols] + jnp.dot(
                att[...], wout_v[lp, :, cols], preferred_element_type=F32
            )
        norm[...] = (normalise(x[...]) * cond[lp, 2] + cond[lp, 3]).astype(BF)
        landed(wff_v.at[lp], w_recv.at[lp, 2])
        for j in range(6):
            gate = jnp.dot(
                norm[...], wff_v[lp, :, 256 * j : 256 * (j + 1)], preferred_element_type=F32
            )
            up = jnp.dot(
                norm[...], wff_v[lp, :, FF + 256 * j : FF + 256 * (j + 1)],
                preferred_element_type=F32,
            )
            hid[:, 256 * j : 256 * (j + 1)] = (jax.nn.silu(gate) * up).astype(BF)
        landed(wdown_v.at[lp], w_recv.at[lp, 3])
        for j in range(3):
            cols = slice(256 * j, 256 * (j + 1))
            x[:, cols] = x[:, cols] + jnp.dot(
                hid[...], wdown_v[lp, :, cols], preferred_element_type=F32
            )

    @pl.when(active)
    def _():
        conditions()

        @pl.when(s == 0)
        def _():
            enter_first()

        @pl.when(s == 1)
        def _():
            enter_second()

        @pl.when(plane > 0)
        def _():
            landed(xin, x_recv)
            x[...] = xin[...].astype(F32)

        @pl.loop(0, 2)
        def _(lp):
            layer(lp)

        @pl.when(plane < 3)
        def _():
            xtx[...] = x[...].astype(BF)
            pltpu.make_async_remote_copy(
                src_ref=xtx, dst_ref=xin, send_sem=x_send, recv_sem=x_recv,
                device_id=(s + 2, t), device_id_type=MESH,
            ).start()

        @pl.when(plane == 3)
        def _():
            done = normalise(x[...]).reshape(8, TOK_DEV, D)
            fin_tx[...] = jnp.concatenate(
                [done, jnp.zeros((8, COND_PAD - TOK_DEV, D), F32)], axis=1
            ).astype(BF)

            @pl.loop(0, 8)
            def _(j):
                send(fin_tx.at[j], fin, f_send.at[j], f_recv, pose, 8 * core + j)

    landed(fin, f_recv)
    out_ref[...] = fin[...].astype(F32)[:TOK_DEV].astype(BF)

    sent(c_src, c_send.at[0], 0, chip_of(s))

    @pl.when(last)
    def _():
        sent(c_src, c_send.at[1], 1, chip_of(s))

    @pl.when((s == 0) | ((s == 1) & last))
    def _():
        @pl.loop(0, POSES)
        def _(p):
            sent(a_src, a_send.at[p], s, chip_of(p))

    @pl.when(core == 1)
    def _():
        @pl.loop(0, POSES)
        def _(p):
            sent(d_src, d_send.at[p], s, chip_of(p))

    @pl.when(active)
    def _():
        for k, (src, dst) in enumerate(weights):
            landed(src, w_send.at[k])
        landed(cond_tx, m_send)

        @pl.when(core == 1)
        def _():
            landed(d_all, p_send)
            bias_out_gone()


        @pl.when(plane < 3)
        def _():
            landed(xtx, x_send)

        @pl.when(plane == 3)
        def _():
            @pl.loop(0, 8)
            def _(j):
                sent(fin_tx.at[j], f_send.at[j], pose, 8 * core + j)


def body(
    coords, atom_single, token_atoms, cond_single, pair_bias, w_coord, w_in,
    w_ada, w_qkv, w_out, w_ff, w_down,
):
    counts = token_atoms.reshape(1, TOK_DEV)
    points = jnp.transpose(coords, (1, 0, 2))
    bias = pair_bias[0].reshape(HEADS * TOK_DEV, KEYS)
    vmem = pl.BlockSpec(memory_space=pltpu.VMEM)
    hbm = pl.BlockSpec(memory_space=pl.ANY)
    dma = pltpu.SemaphoreType.DMA
    rows = pl.pallas_call(
        kernel,
        out_shape=jax.ShapeDtypeStruct((TOK_DEV, D), BF),
        in_specs=[vmem, vmem, vmem, vmem, hbm, vmem, vmem, hbm, hbm, hbm, hbm, hbm],
        out_specs=vmem,
        scratch_shapes=[
            pltpu.VMEM((8, 256), F32),
            pltpu.VMEM((ATOM_PAD, 128), BF),
            pltpu.VMEM((2 * TOK_DEV, KEYS), BF),
            pltpu.VMEM((8, 128), F32),
            pltpu.VMEM((TOK_DEVS, 8, 256), F32),
            pltpu.VMEM((TOK_DEVS, ATOM_PAD, 128), BF),
            pltpu.VMEM((TOK_DEVS, 2 * TOK_DEV, KEYS), BF),
            pltpu.VMEM((2, 8, HEADS * TOK_DEV, KEYS), BF),
            pltpu.VMEM((TOK_DEVS, QUARTER, KEYS), BF),
            pltpu.VMEM((D, 4 * D), BF),
            pltpu.VMEM((2, D, 3 * D), BF),
            pltpu.VMEM((2, D, D), BF),
            pltpu.VMEM((2, D, 2 * FF), BF),
            pltpu.VMEM((2, FF, D), BF),
            pltpu.VMEM((2, 4, ROWS, D), F32),
            pltpu.VMEM((4, ROWS, D), F32),
            pltpu.VMEM((ROWS, D), F32),
            pltpu.VMEM((ROWS, D), BF),
            pltpu.VMEM((ROWS, D), BF),
            pltpu.VMEM((ROWS, D), BF),
            pltpu.VMEM((ROWS, D), BF),
            pltpu.VMEM((2, 2, 3, KEYS, 256), BF),
            pltpu.VMEM((ROWS, D), BF),
            pltpu.VMEM((ROWS, FF), BF),
            pltpu.VMEM((8, COND_PAD, D), BF),
            pltpu.VMEM((COND_PAD, D), BF),
            pltpu.VMEM((3, 6 * ROWS, 256), BF),
            pltpu.VMEM((3, 6 * ROWS, KEYS), F32),
            pltpu.VMEM((HEADS * ROWS, KEYS), BF),
            pltpu.VMEM((HEADS, ROWS, 128), F32),
            dma((2,)), dma((TOK_DEVS,)),
            dma((POSES,)), dma((TOK_DEVS,)),
            dma((POSES,)), dma((TOK_DEVS,)),
            dma((8,)), dma((TOK_DEVS,)),
            dma((TOK_DEVS, 4)), dma((2,)),
            pltpu.SemaphoreType.REGULAR,
            dma((4,)), dma((2, 4)),
            dma,
            dma, dma,
            dma, dma,
            dma((2, 2, 3)), dma((2, 2, 3)),
            dma, dma,
            dma((8,)), dma,
        ],
        compiler_params=pltpu.CompilerParams(
            collective_id=0, has_side_effects=True, vmem_limit_bytes=60 << 20
        ),
    )(
        points, atom_single, counts, cond_single, bias, w_coord, w_in,
        w_ada[0], w_qkv[0], w_out[0], w_ff[0], w_down[0],
    )
    return rows[None]


def solution(mesh):
    return jax.shard_map(
        body,
        mesh=mesh,
        in_specs=(
            P("section", None, "tok"),
            P("tok", None),
            P("tok"),
            P("tok", None),
            P("section", None, "tok", None),
            P(),
            P(),
            P("section", None, None),
            P("section", None, None),
            P("section", None, None),
            P("section", None, None),
            P("section", None, None),
        ),
        out_specs=P("section", "tok", None),
        check_vma=False,
    )
```

```python
import jax
import jax.numpy as jnp
from jax import lax
from jax.experimental import pallas as pl
from jax.experimental.pallas import tpu as pltpu
from jax.sharding import PartitionSpec as P

HEADS = 16
HEAD_DIM = 48
FF = 1536
D = 768
POSES = 8
TOK_DEVS = 16
SECTIONS = 8
ROWS = 192
TOK_DEV = 24
ATOM_DEV = 216
ATOM_PAD = 224
COND_PAD = 32
KEYS = 384
QUARTER = 96
MESH = pl.DeviceIdType.MESH
BF = jnp.bfloat16
F32 = jnp.float32


def chip_of(pose):
    x = pose // 2
    return 4 * x + 2 * (pose % 2) + x % 2


def normalise(v):
    centre = v - jnp.mean(v, axis=-1, keepdims=True)
    return centre * lax.rsqrt(jnp.mean(centre * centre, axis=-1, keepdims=True) + 1e-05)


def landed(ref, sem):
    pltpu.make_async_copy(ref, ref, sem).wait()


def kernel(
    coords_in, atom_ref, count_in, cond_ref, bias_in, wcoord_in, win_in,
    wada_ref, wqkv_ref, wout_ref, wff_ref, wdown_ref,
    out_ref,
    coords_ref, count_ref, wcoord_ref, win_ref, fetch,
    c_src, a_src, d_src, wc, c_all, a_all, d_all, b_all, relay,
    wada_v, wqkv_v, wout_v, wff_v, wdown_v, bias_v, bias_t,
    cond, cond_tx, x, xin, xtx, norm, q, kv, att, hid, fin_tx, fin,
    spread, scores, probs, inverse,
    c_send, c_recv, a_send, a_recv, d_send, d_recv, r_send, r_recv, b_send, b_recv, go,
    w_send, w_recv, ada_sem, p_send, p_recv, m_send, m_recv, kv_send, kv_recv, x_send, x_recv, f_send, f_recv,
):
    s = lax.axis_index("section")
    t = lax.axis_index("tok")
    plane = s // 2
    core = lax.rem(s, 2)
    sibling = s + 1 - 2 * core
    cx, cz = t // 4, lax.rem(t, 4)
    active = lax.rem(cx + cz, 2) == 0
    pose = 2 * cx + cz // 2
    half = t // 8

    fetched = (
        (coords_in, coords_ref), (count_in, count_ref),
        (wcoord_in, wcoord_ref), (win_in, win_ref), (bias_in, bias_v),
    )
    for k, (src, dst) in enumerate(fetched):
        pltpu.make_async_copy(src, dst, fetch.at[k]).start()

    weights = ((wqkv_ref, wqkv_v), (wout_ref, wout_v), (wff_ref, wff_v), (wdown_ref, wdown_v))

    @pl.when(active)
    def _():
        pltpu.make_async_copy(wada_ref, wada_v, ada_sem).start()
        for k, (src, dst) in enumerate(weights):
            pltpu.make_async_copy(src, dst.at[core], w_recv.at[core, k]).start()

    barrier = pltpu.get_barrier_semaphore()

    def greet(section, tok):
        pl.semaphore_signal(barrier, inc=1, device_id=(section, tok), device_id_type=MESH)

    @pl.loop(1, TOK_DEVS)
    def _(j):
        greet(s, lax.rem(t + j, TOK_DEVS))

    def beside(k):
        step = 1 + 2 * lax.rem(k, 2)
        return jnp.where(
            k < 2, 4 * lax.rem(cx + step, 4) + cz, 4 * cx + lax.rem(cz + step, 4)
        )

    @pl.when(active)
    def _():
        @pl.loop(0, 4)
        def _(k):
            greet(sibling, beside(k))

        @pl.when((s == 0) & (pose != 0))
        def _():
            @pl.loop(0, TOK_DEVS)
            def _(j):
                greet(pose, j)

        @pl.when((s == 1) & (pose != 1))
        def _():
            greet(pose, TOK_DEVS - 1)

        @pl.when(plane > 0)
        def _():
            greet(s - 2, t)

    greet(sibling, t)

    fin_section, fin_tok = 6 + half, chip_of(s)
    fin_self = (fin_section == s) & (fin_tok == t)

    @pl.when(jnp.logical_not(fin_self))
    def _():
        greet(fin_section, fin_tok)

    for k, (src, dst) in enumerate(fetched):
        pltpu.make_async_copy(src, dst, fetch.at[k]).wait()

    @pl.when(half == 0)
    def _():
        bias_t[...] = bias_v[...]

    @pl.when(half == 1)
    def _():
        straight = bias_v[...].astype(F32)
        bias_t[...] = jnp.concatenate([straight[:, ROWS:], straight[:, :ROWS]], axis=1).astype(BF)

    c_src[...] = jnp.zeros_like(c_src)
    c_src[0:3, 0:ATOM_DEV] = coords_ref[...].reshape(3, ATOM_DEV)
    c_src[3:4, 0:TOK_DEV] = count_ref[...].astype(F32)
    wc[...] = jnp.zeros_like(wc)
    wc[0:3] = wcoord_ref[...]
    a_src[...] = jnp.concatenate(
        [atom_ref[...].astype(F32), jnp.zeros((ATOM_PAD - ATOM_DEV, 128), F32)], axis=0
    ).astype(BF)
    single = cond_ref[...].astype(F32)
    d_src[...] = jnp.concatenate([single[:, :KEYS], single[:, KEYS:]], axis=0).astype(BF)

    one = lambda flag: flag.astype(jnp.int32)
    last = t == TOK_DEVS - 1
    expected = 15 + 1 + 4 * (1 - one(active))
    expected += one(s != 0) + one(last & (s != 1))
    expected += one(active & (plane < 3))
    fin_here = active & (plane == 3)
    fin_own = fin_here & (pose == s) & (half == core)
    expected += 8 * one(fin_here) - one(fin_own)
    pl.semaphore_wait(barrier, expected)

    def send(src, dst, send_sem, recv_sem, section, tok):
        own = (section == s) & (tok == t)

        @pl.when(own)
        def _():
            pltpu.make_async_copy(src, dst, recv_sem).start()

        @pl.when(jnp.logical_not(own))
        def _():
            pltpu.make_async_remote_copy(
                src_ref=src, dst_ref=dst, send_sem=send_sem, recv_sem=recv_sem,
                device_id=(section, tok), device_id_type=MESH,
            ).start()

    def sent(src, send_sem, section, tok):
        @pl.when(jnp.logical_not((section == s) & (tok == t)))
        def _():
            landed(src, send_sem)

    send(c_src, c_all.at[t], c_send.at[0], c_recv.at[t], 0, chip_of(s))

    @pl.when(last)
    def _():
        send(c_src, c_all.at[t], c_send.at[1], c_recv.at[t], 1, chip_of(s))

    quarter = 2 * lax.rem(cx, 2) + lax.rem(cz + 2 * (cx // 2), 4) // 2

    def bias_part(k):
        return bias_t.at[pl.ds(pl.multiple_of(QUARTER * k, QUARTER), QUARTER)]

    def relay_chip(k, e):
        first = k // 2
        return 4 * (first + 2 * e) + lax.rem(2 * lax.rem(k, 2) + 1 - first + 2 * e, 4)

    def bias_out():
        @pl.loop(0, 8)
        def _(j):
            k, e = lax.rem(j, 4), j // 4
            send(bias_part(k), relay.at[t], r_send.at[j], r_recv.at[t], s, relay_chip(k, e))

    def bias_out_gone():
        @pl.loop(0, 8)
        def _(j):
            k, e = lax.rem(j, 4), j // 4
            sent(bias_part(k), r_send.at[j], s, relay_chip(k, e))

    def bias_on():
        @pl.loop(0, 8)
        def _(j):
            pair = lax.rem(t // 2 + j, 8)
            for e in range(2):
                landed(relay.at[2 * pair + e], r_recv.at[2 * pair + e])

            @pl.loop(0, 4)
            def _(k):
                pltpu.make_async_remote_copy(
                    src_ref=relay.at[pl.ds(2 * pair, 2)],
                    dst_ref=b_all.at[
                        core, pl.ds(2 * lax.rem(pair, 4), 2),
                        pl.ds(pl.multiple_of(QUARTER * quarter, QUARTER), QUARTER),
                    ],
                    send_sem=b_send.at[j, k], recv_sem=b_recv.at[core],
                    device_id=(2 * plane + pair // 4, beside(k)), device_id_type=MESH,
                ).start()

    def bias_gone(low, high):
        @pl.loop(low, high)
        def _(j):
            @pl.loop(0, 4)
            def _(k):
                landed(relay.at[pl.ds(0, 2)], b_send.at[j, k])

    def tell():
        pl.semaphore_signal(go, inc=1, device_id=(sibling, t), device_id_type=MESH)

    @pl.when(core == 0)
    def _():
        bias_out()

    @pl.when((s == 0) | ((s == 1) & last))
    def _():
        @pl.loop(0, POSES)
        def _(p):
            send(a_src, a_all.at[t], a_send.at[p], a_recv.at[t], s, chip_of(p))

    @pl.when(core == 1)
    def _():
        @pl.loop(0, POSES)
        def _(p):
            send(d_src, d_all.at[t], d_send.at[p], d_recv.at[t], s, chip_of(p))

    @pl.when(active)
    def _():
        for k, (src, dst) in enumerate(weights):
            pltpu.make_async_remote_copy(
                src_ref=src, dst_ref=dst.at[core], send_sem=w_send.at[k],
                recv_sem=w_recv.at[core, k], device_id=(sibling, t), device_id_type=MESH,
            ).start()

    @pl.when(core == 0)
    def _():
        bias_out_gone()
        tell()

    @pl.when(core == 1)
    def _():
        pl.semaphore_wait(go, 1)
        bias_out()

    @pl.when((core == 0) & jnp.logical_not(active))
    def _():
        bias_on()
        bias_gone(0, 6)
        tell()
        bias_gone(6, 8)

    @pl.when((core == 1) & jnp.logical_not(active))
    def _():
        pl.semaphore_wait(go, 1)
        bias_on()
        bias_out_gone()
        bias_gone(0, 8)

    def act_of(points, single):
        moved = lax.dot_general(
            points, wc[...], (((0,), (0,)), ((), ())),
            precision=lax.Precision.HIGHEST, preferred_element_type=F32,
        )
        return jnp.maximum(single.astype(F32) + moved[:ATOM_PAD], 0.0)

    def enter_first():
        @pl.loop(0, TOK_DEVS)
        def _(j):
            landed(c_all.at[j], c_recv.at[j])

        lane8 = lax.broadcasted_iota(jnp.int32, (TOK_DEV, 128), 1)
        place8 = lax.broadcasted_iota(jnp.int32, (TOK_DEV, 128), 0)
        count_blocks, start_blocks = [], []
        total = jnp.zeros((TOK_DEV, 1), F32)
        for j in range(8):
            row = jnp.broadcast_to(c_all[j, 3:4, 0:128], (TOK_DEV, 128))
            mine = jnp.where(lane8 == place8, row, 0.0)
            ahead = jnp.where(lane8 < place8, row, 0.0)
            count_blocks.append(jnp.sum(mine, axis=1, keepdims=True))
            start_blocks.append(total + jnp.sum(ahead, axis=1, keepdims=True))
            total = total + jnp.sum(row, axis=1, keepdims=True)
        counts = jnp.broadcast_to(jnp.concatenate(count_blocks, axis=0), (ROWS, 128))
        starts = jnp.broadcast_to(jnp.concatenate(start_blocks, axis=0), (ROWS, 128))
        ends = starts + counts
        lower = jnp.concatenate([starts, starts], axis=1)[:, :ATOM_PAD]
        upper = jnp.concatenate([ends, ends], axis=1)[:, :ATOM_PAD]
        lane = lax.broadcasted_iota(jnp.int32, (ROWS, ATOM_PAD), 1)

        @pl.loop(0, TOK_DEVS)
        def _(j):
            landed(a_all.at[j], a_recv.at[j])

        pooled = jnp.zeros((ROWS, 128), F32)
        for j in range(TOK_DEVS):
            place = (lane + j * ATOM_DEV).astype(F32)
            inside = (place >= lower) & (place < upper) & (lane < ATOM_DEV)
            member = jnp.where(inside, 1.0, 0.0).astype(BF)
            act = act_of(c_all[j], a_all[j]).astype(BF)
            pooled = pooled + jnp.dot(member, act, preferred_element_type=F32)
        averaged = (pooled / counts).astype(BF)
        x[...] = jnp.dot(averaged, win_ref[...], preferred_element_type=F32)

    def enter_second():
        j = TOK_DEVS - 1
        landed(c_all.at[j], c_recv.at[j])
        landed(a_all.at[j], a_recv.at[j])
        act = act_of(c_all[j], a_all[j])[ATOM_DEV - ROWS : ATOM_DEV]
        x[...] = jnp.dot(act.astype(BF), win_ref[...], preferred_element_type=F32)

    def conditions():
        @pl.when(core == 1)
        def _():
            @pl.loop(0, TOK_DEVS)
            def _(j):
                landed(d_all.at[j], d_recv.at[j])

            pltpu.make_async_remote_copy(
                src_ref=d_all, dst_ref=d_all, send_sem=p_send, recv_sem=p_recv,
                device_id=(sibling, t), device_id_type=MESH,
            ).start()

        @pl.when(core == 0)
        def _():
            landed(d_all, p_recv)

        landed(wada_ref, ada_sem)

        def rows_for(which, store):
            blocks = d_all[pl.ds(8 * which, 8)].astype(F32)
            norm[...] = jnp.concatenate(
                [blocks[:, :TOK_DEV].reshape(ROWS, KEYS), blocks[:, TOK_DEV:].reshape(ROWS, KEYS)],
                axis=1,
            ).astype(BF)
            for k in range(4):
                value = jnp.dot(
                    norm[...], wada_v[:, D * k : D * (k + 1)], preferred_element_type=F32
                )
                store(k, jax.nn.sigmoid(value) if k % 2 == 0 else value)

        def to_send(k, value):
            cond_tx[k] = value

        def to_keep(k, value):
            cond[core, k] = value

        rows_for(1 - core, to_send)
        pltpu.make_async_remote_copy(
            src_ref=cond_tx, dst_ref=cond.at[core], send_sem=m_send, recv_sem=m_recv,
            device_id=(sibling, t), device_id_type=MESH,
        ).start()
        rows_for(core, to_keep)

    mine, theirs = slice(0, ROWS), slice(ROWS, KEYS)

    def layer(lp):
        norm[...] = (normalise(x[...]) * cond[lp, 0] + cond[lp, 1]).astype(BF)

        def project(column, width):
            return jnp.dot(
                norm[...], wqkv_v[lp, :, column : column + width], preferred_element_type=F32
            ).astype(BF)

        for part in range(2):
            for j in range(3):
                kv[lp, part, j, mine, :] = project(D * (part + 1) + 256 * j, 256)
            pltpu.make_async_remote_copy(
                src_ref=kv.at[lp, part, :, mine], dst_ref=kv.at[lp, part, :, theirs],
                send_sem=kv_send.at[lp, part], recv_sem=kv_recv.at[lp, part],
                device_id=(sibling, t), device_id_type=MESH,
            ).start()
        for j in range(3):
            q[:, 256 * j : 256 * (j + 1)] = project(256 * j, 256)

        def spread_out(w):
            window = q[:, 256 * w : 256 * (w + 1)]
            lane = lax.broadcasted_iota(jnp.int32, (1, 256), 1) + 256 * w
            for k in range(6):
                low = HEAD_DIM * (5 * w + k)
                mask = jnp.where((lane >= low) & (lane < low + HEAD_DIM), 1.0, 0.0).astype(BF)
                spread[w, ROWS * k : ROWS * (k + 1)] = window * mask

        def score(w, first, stop):
            scores[w, :, first:stop] = lax.dot_general(
                spread[w], kv[lp, 0, w, first:stop], (((1,), (1,)), ((), ())),
                preferred_element_type=F32,
            )

        def soften(head):
            pair, e = head // 2, head % 2
            bias = b_all[lp, :, 48 * pair : 48 * (pair + 1), :].astype(F32)
            w = min(head // 5, 2)
            k = head - 5 * w
            raw = scores[w, ROWS * k : ROWS * (k + 1)]
            if k == 0 and w > 0:
                raw = raw + scores[w - 1, 5 * ROWS : 6 * ROWS]
            logits = raw * HEAD_DIM ** (-0.5) + bias[
                :, TOK_DEV * e : TOK_DEV * (e + 1)
            ].reshape(ROWS, KEYS)
            top = jnp.max(logits, axis=-1, keepdims=True)
            weight = jnp.exp(logits - top)
            total = jnp.sum(weight, axis=-1, keepdims=True)
            inverse[head] = jnp.broadcast_to(1.0 / total, (ROWS, 128))
            probs[ROWS * head : ROWS * (head + 1)] = weight.astype(BF)

        def gather(w):
            out = jnp.dot(
                probs[ROWS * 5 * w : ROWS * (5 * w + 6)], kv[lp, 1, w], preferred_element_type=F32
            )
            lane = lax.broadcasted_iota(jnp.int32, (1, 256), 1) + 256 * w
            whole = jnp.zeros((ROWS, 256), F32)
            for k in range(6):
                low = HEAD_DIM * (5 * w + k)
                factor = inverse[5 * w + k]
                piece = out[ROWS * k : ROWS * (k + 1)] * jnp.concatenate([factor, factor], axis=1)
                whole = jnp.where(lane >= low, piece, whole)
            att[:, 256 * w : 256 * (w + 1)] = whole.astype(BF)

        for w in range(3):
            spread_out(w)
            score(w, 0, 128)
        landed(kv.at[lp, 0, :, theirs], kv_recv.at[lp, 0])
        for w in range(3):
            score(w, 128, KEYS)
        landed(kv.at[lp, 1, :, theirs], kv_recv.at[lp, 1])
        landed(b_all.at[lp], b_recv.at[lp])
        for head in range(0, 6):
            soften(head)
        gather(0)
        for head in range(6, 11):
            soften(head)
        gather(1)
        for head in range(11, 16):
            soften(head)
        gather(2)

        for j in range(3):
            cols = slice(256 * j, 256 * (j + 1))
            x[:, cols] = x[:, cols] + jnp.dot(
                att[...], wout_v[lp, :, cols], preferred_element_type=F32
            )
        norm[...] = (normalise(x[...]) * cond[lp, 2] + cond[lp, 3]).astype(BF)
        for j in range(6):
            gate = jnp.dot(
                norm[...], wff_v[lp, :, 256 * j : 256 * (j + 1)], preferred_element_type=F32
            )
            up = jnp.dot(
                norm[...], wff_v[lp, :, FF + 256 * j : FF + 256 * (j + 1)],
                preferred_element_type=F32,
            )
            hid[:, 256 * j : 256 * (j + 1)] = (jax.nn.silu(gate) * up).astype(BF)
        for j in range(3):
            cols = slice(256 * j, 256 * (j + 1))
            x[:, cols] = x[:, cols] + jnp.dot(
                hid[...], wdown_v[lp, :, cols], preferred_element_type=F32
            )

    @pl.when(active)
    def _():
        conditions()

        @pl.when(s == 0)
        def _():
            enter_first()

        @pl.when(s == 1)
        def _():
            enter_second()

        for k, (src, dst) in enumerate(weights):
            for lp in range(2):
                landed(dst.at[lp], w_recv.at[lp, k])
        landed(cond.at[1 - core], m_recv)

        @pl.when(plane > 0)
        def _():
            landed(xin, x_recv)
            x[...] = xin[...].astype(F32)

        @pl.loop(0, 2)
        def _(lp):
            layer(lp)

        @pl.when(plane < 3)
        def _():
            xtx[...] = x[...].astype(BF)
            pltpu.make_async_remote_copy(
                src_ref=xtx, dst_ref=xin, send_sem=x_send, recv_sem=x_recv,
                device_id=(s + 2, t), device_id_type=MESH,
            ).start()

        @pl.when(plane == 3)
        def _():
            done = normalise(x[...]).reshape(8, TOK_DEV, D)
            fin_tx[...] = jnp.concatenate(
                [done, jnp.zeros((8, COND_PAD - TOK_DEV, D), F32)], axis=1
            ).astype(BF)

            @pl.loop(0, 8)
            def _(j):
                send(fin_tx.at[j], fin, f_send.at[j], f_recv, pose, 8 * core + j)

    landed(fin, f_recv)
    out_ref[...] = fin[...].astype(F32)[:TOK_DEV].astype(BF)

    sent(c_src, c_send.at[0], 0, chip_of(s))

    @pl.when(last)
    def _():
        sent(c_src, c_send.at[1], 1, chip_of(s))

    @pl.when((s == 0) | ((s == 1) & last))
    def _():
        @pl.loop(0, POSES)
        def _(p):
            sent(a_src, a_send.at[p], s, chip_of(p))

    @pl.when(core == 1)
    def _():
        @pl.loop(0, POSES)
        def _(p):
            sent(d_src, d_send.at[p], s, chip_of(p))

    @pl.when(active)
    def _():
        for k, (src, dst) in enumerate(weights):
            landed(src, w_send.at[k])
        landed(cond_tx, m_send)

        @pl.loop(0, 2)
        def _(lp):
            for part in range(2):
                landed(kv.at[lp, part, :, mine], kv_send.at[lp, part])

        @pl.when(core == 1)
        def _():
            landed(d_all, p_send)
            bias_out_gone()


        @pl.when(plane < 3)
        def _():
            landed(xtx, x_send)

        @pl.when(plane == 3)
        def _():
            @pl.loop(0, 8)
            def _(j):
                sent(fin_tx.at[j], f_send.at[j], pose, 8 * core + j)


def body(
    coords, atom_single, token_atoms, cond_single, pair_bias, w_coord, w_in,
    w_ada, w_qkv, w_out, w_ff, w_down,
):
    counts = token_atoms.reshape(1, TOK_DEV)
    points = jnp.transpose(coords, (1, 0, 2))
    bias = pair_bias[0].reshape(HEADS * TOK_DEV, KEYS)
    vmem = pl.BlockSpec(memory_space=pltpu.VMEM)
    hbm = pl.BlockSpec(memory_space=pl.ANY)
    dma = pltpu.SemaphoreType.DMA
    rows = pl.pallas_call(
        kernel,
        out_shape=jax.ShapeDtypeStruct((TOK_DEV, D), BF),
        in_specs=[hbm, vmem, hbm, vmem] + [hbm] * 8,
        out_specs=vmem,
        scratch_shapes=[
            pltpu.VMEM((3, 1, ATOM_DEV), F32),
            pltpu.VMEM((1, TOK_DEV), jnp.int32),
            pltpu.VMEM((3, 128), F32),
            pltpu.VMEM((128, D), BF),
            dma((5,)),
            pltpu.VMEM((8, 256), F32),
            pltpu.VMEM((ATOM_PAD, 128), BF),
            pltpu.VMEM((2 * TOK_DEV, KEYS), BF),
            pltpu.VMEM((8, 128), F32),
            pltpu.VMEM((TOK_DEVS, 8, 256), F32),
            pltpu.VMEM((TOK_DEVS, ATOM_PAD, 128), BF),
            pltpu.VMEM((TOK_DEVS, 2 * TOK_DEV, KEYS), BF),
            pltpu.VMEM((2, 8, HEADS * TOK_DEV, KEYS), BF),
            pltpu.VMEM((TOK_DEVS, QUARTER, KEYS), BF),
            pltpu.VMEM((D, 4 * D), BF),
            pltpu.VMEM((2, D, 3 * D), BF),
            pltpu.VMEM((2, D, D), BF),
            pltpu.VMEM((2, D, 2 * FF), BF),
            pltpu.VMEM((2, FF, D), BF),
            pltpu.VMEM((HEADS * TOK_DEV, KEYS), BF),
            pltpu.VMEM((HEADS * TOK_DEV, KEYS), BF),
            pltpu.VMEM((2, 4, ROWS, D), F32),
            pltpu.VMEM((4, ROWS, D), F32),
            pltpu.VMEM((ROWS, D), F32),
            pltpu.VMEM((ROWS, D), BF),
            pltpu.VMEM((ROWS, D), BF),
            pltpu.VMEM((ROWS, D), BF),
            pltpu.VMEM((ROWS, D), BF),
            pltpu.VMEM((2, 2, 3, KEYS, 256), BF),
            pltpu.VMEM((ROWS, D), BF),
            pltpu.VMEM((ROWS, FF), BF),
            pltpu.VMEM((8, COND_PAD, D), BF),
            pltpu.VMEM((COND_PAD, D), BF),
            pltpu.VMEM((3, 6 * ROWS, 256), BF),
            pltpu.VMEM((3, 6 * ROWS, KEYS), F32),
            pltpu.VMEM((HEADS * ROWS, KEYS), BF),
            pltpu.VMEM((HEADS, ROWS, 128), F32),
            dma((2,)), dma((TOK_DEVS,)),
            dma((POSES,)), dma((TOK_DEVS,)),
            dma((POSES,)), dma((TOK_DEVS,)),
            dma((8,)), dma((TOK_DEVS,)),
            dma((8, 4)), dma((2,)),
            pltpu.SemaphoreType.REGULAR,
            dma((4,)), dma((2, 4)),
            dma,
            dma, dma,
            dma, dma,
            dma((2, 2)), dma((2, 2)),
            dma, dma,
            dma((8,)), dma,
        ],
        compiler_params=pltpu.CompilerParams(
            collective_id=0, has_side_effects=True, vmem_limit_bytes=60 << 20
        ),
    )(
        points, atom_single, counts, cond_single, bias, w_coord, w_in,
        w_ada[0], w_qkv[0], w_out[0], w_ff[0], w_down[0],
    )
    return rows[None]


def solution(mesh):
    return jax.shard_map(
        body,
        mesh=mesh,
        in_specs=(
            P("section", None, "tok"),
            P("tok", None),
            P("tok"),
            P("tok", None),
            P("section", None, "tok", None),
            P(),
            P(),
            P("section", None, None),
            P("section", None, None),
            P("section", None, None),
            P("section", None, None),
            P("section", None, None),
        ),
        out_specs=P("section", "tok", None),
        check_vma=False,
    )
```

```python
import jax
import jax.numpy as jnp
from jax import lax
from jax.experimental import pallas as pl
from jax.experimental.pallas import tpu as pltpu
from jax.sharding import PartitionSpec as P

HEADS = 16
HEAD_DIM = 48
FF = 1536
D = 768
POSES = 8
TOK_DEVS = 16
SECTIONS = 8
ROWS = 192
TOK_DEV = 24
ATOM_DEV = 216
ATOM_PAD = 224
COND_PAD = 32
KEYS = 384
QUARTER = 96
MESH = pl.DeviceIdType.MESH
BF = jnp.bfloat16
F32 = jnp.float32


def chip_of(pose):
    x = pose // 2
    return 4 * x + 2 * (pose % 2) + x % 2


def normalise(v):
    centre = v - jnp.mean(v, axis=-1, keepdims=True)
    return centre * lax.rsqrt(jnp.mean(centre * centre, axis=-1, keepdims=True) + 1e-05)


def landed(ref, sem):
    pltpu.make_async_copy(ref, ref, sem).wait()


def kernel(
    coords_in, atom_ref, count_in, cond_ref, bias_in, wcoord_in, win_in,
    wada_ref, wqkv_ref, wout_ref, wff_ref, wdown_ref,
    out_ref,
    coords_ref, count_ref, wcoord_ref, win_ref, fetch,
    c_src, a_src, d_src, wc, c_all, a_all, d_all, b_all, relay,
    wada_v, wqkv_v, wout_v, wff_v, wdown_v, bias_v, bias_t,
    cond, cond_tx, x, xin, xtx, norm, q, kv, att, hid, fin_tx, fin,
    spread, scores, probs, inverse,
    c_send, c_recv, a_send, a_recv, d_send, d_recv, r_send, r_recv, b_send, b_recv, go,
    w_send, w_recv, ada_sem, p_send, p_recv, m_send, m_recv, kv_send, kv_recv, x_send, x_recv, f_send, f_recv,
):
    s = lax.axis_index("section")
    t = lax.axis_index("tok")
    plane = s // 2
    core = lax.rem(s, 2)
    sibling = s + 1 - 2 * core
    cx, cz = t // 4, lax.rem(t, 4)
    active = lax.rem(cx + cz, 2) == 0
    pose = 2 * cx + cz // 2
    half = t // 8

    fetched = (
        (coords_in, coords_ref), (count_in, count_ref),
        (wcoord_in, wcoord_ref), (win_in, win_ref), (bias_in, bias_v),
    )
    for k, (src, dst) in enumerate(fetched):
        pltpu.make_async_copy(src, dst, fetch.at[k]).start()

    weights = ((wqkv_ref, wqkv_v), (wout_ref, wout_v), (wff_ref, wff_v), (wdown_ref, wdown_v))

    @pl.when(active)
    def _():
        pltpu.make_async_copy(wada_ref, wada_v, ada_sem).start()
        for k, (src, dst) in enumerate(weights):
            pltpu.make_async_copy(src, dst.at[core], w_recv.at[core, k]).start()

    barrier = pltpu.get_barrier_semaphore()

    def greet(section, tok):
        pl.semaphore_signal(barrier, inc=1, device_id=(section, tok), device_id_type=MESH)

    @pl.loop(1, TOK_DEVS)
    def _(j):
        greet(s, lax.rem(t + j, TOK_DEVS))

    def beside(k):
        step = 1 + 2 * lax.rem(k, 2)
        return jnp.where(
            k < 2, 4 * lax.rem(cx + step, 4) + cz, 4 * cx + lax.rem(cz + step, 4)
        )

    @pl.when(active)
    def _():
        @pl.loop(0, 4)
        def _(k):
            greet(sibling, beside(k))

        @pl.when((s == 0) & (pose != 0))
        def _():
            @pl.loop(0, TOK_DEVS)
            def _(j):
                greet(pose, j)

        @pl.when((s == 1) & (pose != 1))
        def _():
            greet(pose, TOK_DEVS - 1)

        @pl.when(plane > 0)
        def _():
            greet(s - 2, t)

    greet(sibling, t)

    fin_section, fin_tok = 6 + half, chip_of(s)
    fin_self = (fin_section == s) & (fin_tok == t)

    @pl.when(jnp.logical_not(fin_self))
    def _():
        greet(fin_section, fin_tok)

    for k, (src, dst) in enumerate(fetched):
        pltpu.make_async_copy(src, dst, fetch.at[k]).wait()

    @pl.when(half == 0)
    def _():
        bias_t[...] = bias_v[...]

    @pl.when(half == 1)
    def _():
        straight = bias_v[...].astype(F32)
        bias_t[...] = jnp.concatenate([straight[:, ROWS:], straight[:, :ROWS]], axis=1).astype(BF)

    c_src[...] = jnp.zeros_like(c_src)
    c_src[0:3, 0:ATOM_DEV] = coords_ref[...].reshape(3, ATOM_DEV)
    c_src[3:4, 0:TOK_DEV] = count_ref[...].astype(F32)
    wc[...] = jnp.zeros_like(wc)
    wc[0:3] = wcoord_ref[...]
    a_src[...] = jnp.concatenate(
        [atom_ref[...].astype(F32), jnp.zeros((ATOM_PAD - ATOM_DEV, 128), F32)], axis=0
    ).astype(BF)
    single = cond_ref[...].astype(F32)
    d_src[...] = jnp.concatenate([single[:, :KEYS], single[:, KEYS:]], axis=0).astype(BF)

    one = lambda flag: flag.astype(jnp.int32)
    last = t == TOK_DEVS - 1
    expected = 15 + 1 + 4 * (1 - one(active))
    expected += one(s != 0) + one(last & (s != 1))
    expected += one(active & (plane < 3))
    fin_here = active & (plane == 3)
    fin_own = fin_here & (pose == s) & (half == core)
    expected += 8 * one(fin_here) - one(fin_own)
    pl.semaphore_wait(barrier, expected)

    def send(src, dst, send_sem, recv_sem, section, tok):
        own = (section == s) & (tok == t)

        @pl.when(own)
        def _():
            pltpu.make_async_copy(src, dst, recv_sem).start()

        @pl.when(jnp.logical_not(own))
        def _():
            pltpu.make_async_remote_copy(
                src_ref=src, dst_ref=dst, send_sem=send_sem, recv_sem=recv_sem,
                device_id=(section, tok), device_id_type=MESH,
            ).start()

    def sent(src, send_sem, section, tok):
        @pl.when(jnp.logical_not((section == s) & (tok == t)))
        def _():
            landed(src, send_sem)

    send(c_src, c_all.at[t], c_send.at[0], c_recv.at[t], 0, chip_of(s))

    @pl.when(last)
    def _():
        send(c_src, c_all.at[t], c_send.at[1], c_recv.at[t], 1, chip_of(s))

    quarter = 2 * lax.rem(cx, 2) + lax.rem(cz + 2 * (cx // 2), 4) // 2

    def bias_part(k):
        return bias_t.at[pl.ds(pl.multiple_of(QUARTER * k, QUARTER), QUARTER)]

    def relay_chip(k, e):
        first = k // 2
        return 4 * (first + 2 * e) + lax.rem(2 * lax.rem(k, 2) + 1 - first + 2 * e, 4)

    def bias_out():
        @pl.loop(0, 8)
        def _(j):
            k, e = lax.rem(j, 4), j // 4
            send(bias_part(k), relay.at[t], r_send.at[j], r_recv.at[t], s, relay_chip(k, e))

    def bias_out_gone():
        @pl.loop(0, 8)
        def _(j):
            k, e = lax.rem(j, 4), j // 4
            sent(bias_part(k), r_send.at[j], s, relay_chip(k, e))

    def bias_on():
        @pl.loop(0, 8)
        def _(j):
            pair = lax.rem(t // 2 + j, 8)
            for e in range(2):
                landed(relay.at[2 * pair + e], r_recv.at[2 * pair + e])

            @pl.loop(0, 4)
            def _(k):
                pltpu.make_async_remote_copy(
                    src_ref=relay.at[pl.ds(2 * pair, 2)],
                    dst_ref=b_all.at[
                        core, pl.ds(2 * lax.rem(pair, 4), 2),
                        pl.ds(pl.multiple_of(QUARTER * quarter, QUARTER), QUARTER),
                    ],
                    send_sem=b_send.at[j, k], recv_sem=b_recv.at[core],
                    device_id=(2 * plane + pair // 4, beside(k)), device_id_type=MESH,
                ).start()

    def bias_gone(low, high):
        @pl.loop(low, high)
        def _(j):
            @pl.loop(0, 4)
            def _(k):
                landed(relay.at[pl.ds(0, 2)], b_send.at[j, k])

    def tell():
        pl.semaphore_signal(go, inc=1, device_id=(sibling, t), device_id_type=MESH)

    @pl.when(core == 0)
    def _():
        bias_out()

    @pl.when((s == 0) | ((s == 1) & last))
    def _():
        @pl.loop(0, POSES)
        def _(p):
            send(a_src, a_all.at[t], a_send.at[p], a_recv.at[t], s, chip_of(p))

    @pl.when(core == 1)
    def _():
        @pl.loop(0, POSES)
        def _(p):
            send(d_src, d_all.at[t], d_send.at[p], d_recv.at[t], s, chip_of(p))

    @pl.when(active)
    def _():
        for k, (src, dst) in enumerate(weights):
            pltpu.make_async_remote_copy(
                src_ref=src, dst_ref=dst.at[core], send_sem=w_send.at[k],
                recv_sem=w_recv.at[core, k], device_id=(sibling, t), device_id_type=MESH,
            ).start()

    @pl.when(core == 0)
    def _():
        bias_out_gone()
        tell()

    @pl.when(core == 1)
    def _():
        pl.semaphore_wait(go, 1)
        bias_out()

    @pl.when((core == 0) & jnp.logical_not(active))
    def _():
        bias_on()
        bias_gone(0, 6)
        tell()
        bias_gone(6, 8)

    @pl.when((core == 1) & jnp.logical_not(active))
    def _():
        pl.semaphore_wait(go, 1)
        bias_on()
        bias_out_gone()
        bias_gone(0, 8)

    def act_of(points, single):
        moved = lax.dot_general(
            points, wc[...], (((0,), (0,)), ((), ())),
            precision=lax.Precision.HIGHEST, preferred_element_type=F32,
        )
        return jnp.maximum(single.astype(F32) + moved[:ATOM_PAD], 0.0)

    def enter_first():
        @pl.loop(0, TOK_DEVS)
        def _(j):
            landed(c_all.at[j], c_recv.at[j])

        lane8 = lax.broadcasted_iota(jnp.int32, (TOK_DEV, 128), 1)
        place8 = lax.broadcasted_iota(jnp.int32, (TOK_DEV, 128), 0)
        count_blocks, start_blocks = [], []
        total = jnp.zeros((TOK_DEV, 1), F32)
        for j in range(8):
            row = jnp.broadcast_to(c_all[j, 3:4, 0:128], (TOK_DEV, 128))
            mine = jnp.where(lane8 == place8, row, 0.0)
            ahead = jnp.where(lane8 < place8, row, 0.0)
            count_blocks.append(jnp.sum(mine, axis=1, keepdims=True))
            start_blocks.append(total + jnp.sum(ahead, axis=1, keepdims=True))
            total = total + jnp.sum(row, axis=1, keepdims=True)
        counts = jnp.broadcast_to(jnp.concatenate(count_blocks, axis=0), (ROWS, 128))
        starts = jnp.broadcast_to(jnp.concatenate(start_blocks, axis=0), (ROWS, 128))
        ends = starts + counts
        lower = jnp.concatenate([starts, starts], axis=1)[:, :ATOM_PAD]
        upper = jnp.concatenate([ends, ends], axis=1)[:, :ATOM_PAD]
        lane = lax.broadcasted_iota(jnp.int32, (ROWS, ATOM_PAD), 1)

        @pl.loop(0, TOK_DEVS)
        def _(j):
            landed(a_all.at[j], a_recv.at[j])

        pooled = jnp.zeros((ROWS, 128), F32)
        for j in range(TOK_DEVS):
            place = (lane + j * ATOM_DEV).astype(F32)
            inside = (place >= lower) & (place < upper) & (lane < ATOM_DEV)
            member = jnp.where(inside, 1.0, 0.0).astype(BF)
            act = act_of(c_all[j], a_all[j]).astype(BF)
            pooled = pooled + jnp.dot(member, act, preferred_element_type=F32)
        averaged = (pooled / counts).astype(BF)
        x[...] = jnp.dot(averaged, win_ref[...], preferred_element_type=F32)

    def enter_second():
        j = TOK_DEVS - 1
        landed(c_all.at[j], c_recv.at[j])
        landed(a_all.at[j], a_recv.at[j])
        act = act_of(c_all[j], a_all[j])[ATOM_DEV - ROWS : ATOM_DEV]
        x[...] = jnp.dot(act.astype(BF), win_ref[...], preferred_element_type=F32)

    def conditions():
        @pl.when(core == 1)
        def _():
            @pl.loop(0, TOK_DEVS)
            def _(j):
                landed(d_all.at[j], d_recv.at[j])

            pltpu.make_async_remote_copy(
                src_ref=d_all, dst_ref=d_all, send_sem=p_send, recv_sem=p_recv,
                device_id=(sibling, t), device_id_type=MESH,
            ).start()

        @pl.when(core == 0)
        def _():
            landed(d_all, p_recv)

        landed(wada_ref, ada_sem)

        def rows_for(which, store):
            blocks = d_all[pl.ds(8 * which, 8)].astype(F32)
            norm[...] = jnp.concatenate(
                [blocks[:, :TOK_DEV].reshape(ROWS, KEYS), blocks[:, TOK_DEV:].reshape(ROWS, KEYS)],
                axis=1,
            ).astype(BF)
            for k in range(4):
                value = jnp.dot(
                    norm[...], wada_v[:, D * k : D * (k + 1)], preferred_element_type=F32
                )
                store(k, jax.nn.sigmoid(value) if k % 2 == 0 else value)

        def to_send(k, value):
            cond_tx[k] = value

        def to_keep(k, value):
            cond[core, k] = value

        rows_for(1 - core, to_send)
        pltpu.make_async_remote_copy(
            src_ref=cond_tx, dst_ref=cond.at[core], send_sem=m_send, recv_sem=m_recv,
            device_id=(sibling, t), device_id_type=MESH,
        ).start()
        rows_for(core, to_keep)

    mine, theirs = slice(0, ROWS), slice(ROWS, KEYS)

    def layer(lp):
        norm[...] = (normalise(x[...]) * cond[lp, 0] + cond[lp, 1]).astype(BF)

        def project(column, width):
            return jnp.dot(
                norm[...], wqkv_v[lp, :, column : column + width], preferred_element_type=F32
            ).astype(BF)

        for part in range(2):
            for j in range(3):
                kv[lp, part, j, mine, :] = project(D * (part + 1) + 256 * j, 256)
            pltpu.make_async_remote_copy(
                src_ref=kv.at[lp, part, :, mine], dst_ref=kv.at[lp, part, :, theirs],
                send_sem=kv_send.at[lp, part], recv_sem=kv_recv.at[lp, part],
                device_id=(sibling, t), device_id_type=MESH,
            ).start()
        for j in range(3):
            q[:, 256 * j : 256 * (j + 1)] = project(256 * j, 256)

        def spread_out(w):
            window = q[:, 256 * w : 256 * (w + 1)]
            lane = lax.broadcasted_iota(jnp.int32, (1, 256), 1) + 256 * w
            for k in range(6):
                low = HEAD_DIM * (5 * w + k)
                mask = jnp.where((lane >= low) & (lane < low + HEAD_DIM), 1.0, 0.0).astype(BF)
                spread[w, ROWS * k : ROWS * (k + 1)] = window * mask

        def score(w, first, stop):
            scores[w, :, first:stop] = lax.dot_general(
                spread[w], kv[lp, 0, w, first:stop], (((1,), (1,)), ((), ())),
                preferred_element_type=F32,
            )

        def soften(head):
            pair, e = head // 2, head % 2
            bias = b_all[lp, :, 48 * pair : 48 * (pair + 1), :].astype(F32)
            w = min(head // 5, 2)
            k = head - 5 * w
            raw = scores[w, ROWS * k : ROWS * (k + 1)]
            if k == 0 and w > 0:
                raw = raw + scores[w - 1, 5 * ROWS : 6 * ROWS]
            logits = raw * HEAD_DIM ** (-0.5) + bias[
                :, TOK_DEV * e : TOK_DEV * (e + 1)
            ].reshape(ROWS, KEYS)
            top = jnp.max(logits, axis=-1, keepdims=True)
            weight = jnp.exp(logits - top)
            total = jnp.sum(weight, axis=-1, keepdims=True)
            inverse[head] = jnp.broadcast_to(1.0 / total, (ROWS, 128))
            probs[ROWS * head : ROWS * (head + 1)] = weight.astype(BF)

        def gather(w):
            out = jnp.dot(
                probs[ROWS * 5 * w : ROWS * (5 * w + 6)], kv[lp, 1, w], preferred_element_type=F32
            )
            lane = lax.broadcasted_iota(jnp.int32, (1, 256), 1) + 256 * w
            whole = jnp.zeros((ROWS, 256), F32)
            for k in range(6):
                low = HEAD_DIM * (5 * w + k)
                factor = inverse[5 * w + k]
                piece = out[ROWS * k : ROWS * (k + 1)] * jnp.concatenate([factor, factor], axis=1)
                whole = jnp.where(lane >= low, piece, whole)
            att[:, 256 * w : 256 * (w + 1)] = whole.astype(BF)

        for w in range(3):
            spread_out(w)
            score(w, 0, 128)
        landed(kv.at[lp, 0, :, theirs], kv_recv.at[lp, 0])
        landed(kv.at[lp, 1, :, theirs], kv_recv.at[lp, 1])
        landed(b_all.at[lp], b_recv.at[lp])
        for w in range(3):
            score(w, 128, KEYS)
        for head in range(0, 6):
            soften(head)
        gather(0)
        for head in range(6, 11):
            soften(head)
        gather(1)
        for head in range(11, 16):
            soften(head)
        gather(2)

        for j in range(3):
            cols = slice(256 * j, 256 * (j + 1))
            x[:, cols] = x[:, cols] + jnp.dot(
                att[...], wout_v[lp, :, cols], preferred_element_type=F32
            )
        norm[...] = (normalise(x[...]) * cond[lp, 2] + cond[lp, 3]).astype(BF)
        for j in range(6):
            gate = jnp.dot(
                norm[...], wff_v[lp, :, 256 * j : 256 * (j + 1)], preferred_element_type=F32
            )
            up = jnp.dot(
                norm[...], wff_v[lp, :, FF + 256 * j : FF + 256 * (j + 1)],
                preferred_element_type=F32,
            )
            hid[:, 256 * j : 256 * (j + 1)] = (jax.nn.silu(gate) * up).astype(BF)
        for j in range(3):
            cols = slice(256 * j, 256 * (j + 1))
            x[:, cols] = x[:, cols] + jnp.dot(
                hid[...], wdown_v[lp, :, cols], preferred_element_type=F32
            )

    @pl.when(active)
    def _():
        conditions()

        @pl.when(s == 0)
        def _():
            enter_first()

        @pl.when(s == 1)
        def _():
            enter_second()

        for k, (src, dst) in enumerate(weights):
            for lp in range(2):
                landed(dst.at[lp], w_recv.at[lp, k])
        landed(cond.at[1 - core], m_recv)

        @pl.when(plane > 0)
        def _():
            landed(xin, x_recv)
            x[...] = xin[...].astype(F32)

        @pl.loop(0, 2)
        def _(lp):
            layer(lp)

        @pl.when(plane < 3)
        def _():
            xtx[...] = x[...].astype(BF)
            pltpu.make_async_remote_copy(
                src_ref=xtx, dst_ref=xin, send_sem=x_send, recv_sem=x_recv,
                device_id=(s + 2, t), device_id_type=MESH,
            ).start()

        @pl.when(plane == 3)
        def _():
            done = normalise(x[...]).reshape(8, TOK_DEV, D)
            fin_tx[...] = jnp.concatenate(
                [done, jnp.zeros((8, COND_PAD - TOK_DEV, D), F32)], axis=1
            ).astype(BF)

            @pl.loop(0, 8)
            def _(j):
                send(fin_tx.at[j], fin, f_send.at[j], f_recv, pose, 8 * core + j)

    landed(fin, f_recv)
    out_ref[...] = fin[...].astype(F32)[:TOK_DEV].astype(BF)

    sent(c_src, c_send.at[0], 0, chip_of(s))

    @pl.when(last)
    def _():
        sent(c_src, c_send.at[1], 1, chip_of(s))

    @pl.when((s == 0) | ((s == 1) & last))
    def _():
        @pl.loop(0, POSES)
        def _(p):
            sent(a_src, a_send.at[p], s, chip_of(p))

    @pl.when(core == 1)
    def _():
        @pl.loop(0, POSES)
        def _(p):
            sent(d_src, d_send.at[p], s, chip_of(p))

    @pl.when(active)
    def _():
        for k, (src, dst) in enumerate(weights):
            landed(src, w_send.at[k])
        landed(cond_tx, m_send)

        @pl.loop(0, 2)
        def _(lp):
            for part in range(2):
                landed(kv.at[lp, part, :, mine], kv_send.at[lp, part])

        @pl.when(core == 1)
        def _():
            landed(d_all, p_send)
            bias_out_gone()


        @pl.when(plane < 3)
        def _():
            landed(xtx, x_send)

        @pl.when(plane == 3)
        def _():
            @pl.loop(0, 8)
            def _(j):
                sent(fin_tx.at[j], f_send.at[j], pose, 8 * core + j)


def body(
    coords, atom_single, token_atoms, cond_single, pair_bias, w_coord, w_in,
    w_ada, w_qkv, w_out, w_ff, w_down,
):
    counts = token_atoms.reshape(1, TOK_DEV)
    points = jnp.transpose(coords, (1, 0, 2))
    bias = pair_bias[0].reshape(HEADS * TOK_DEV, KEYS)
    vmem = pl.BlockSpec(memory_space=pltpu.VMEM)
    hbm = pl.BlockSpec(memory_space=pl.ANY)
    dma = pltpu.SemaphoreType.DMA
    rows = pl.pallas_call(
        kernel,
        out_shape=jax.ShapeDtypeStruct((TOK_DEV, D), BF),
        in_specs=[hbm, vmem, hbm, vmem] + [hbm] * 8,
        out_specs=vmem,
        scratch_shapes=[
            pltpu.VMEM((3, 1, ATOM_DEV), F32),
            pltpu.VMEM((1, TOK_DEV), jnp.int32),
            pltpu.VMEM((3, 128), F32),
            pltpu.VMEM((128, D), BF),
            dma((5,)),
            pltpu.VMEM((8, 256), F32),
            pltpu.VMEM((ATOM_PAD, 128), BF),
            pltpu.VMEM((2 * TOK_DEV, KEYS), BF),
            pltpu.VMEM((8, 128), F32),
            pltpu.VMEM((TOK_DEVS, 8, 256), F32),
            pltpu.VMEM((TOK_DEVS, ATOM_PAD, 128), BF),
            pltpu.VMEM((TOK_DEVS, 2 * TOK_DEV, KEYS), BF),
            pltpu.VMEM((2, 8, HEADS * TOK_DEV, KEYS), BF),
            pltpu.VMEM((TOK_DEVS, QUARTER, KEYS), BF),
            pltpu.VMEM((D, 4 * D), BF),
            pltpu.VMEM((2, D, 3 * D), BF),
            pltpu.VMEM((2, D, D), BF),
            pltpu.VMEM((2, D, 2 * FF), BF),
            pltpu.VMEM((2, FF, D), BF),
            pltpu.VMEM((HEADS * TOK_DEV, KEYS), BF),
            pltpu.VMEM((HEADS * TOK_DEV, KEYS), BF),
            pltpu.VMEM((2, 4, ROWS, D), F32),
            pltpu.VMEM((4, ROWS, D), F32),
            pltpu.VMEM((ROWS, D), F32),
            pltpu.VMEM((ROWS, D), BF),
            pltpu.VMEM((ROWS, D), BF),
            pltpu.VMEM((ROWS, D), BF),
            pltpu.VMEM((ROWS, D), BF),
            pltpu.VMEM((2, 2, 3, KEYS, 256), BF),
            pltpu.VMEM((ROWS, D), BF),
            pltpu.VMEM((ROWS, FF), BF),
            pltpu.VMEM((8, COND_PAD, D), BF),
            pltpu.VMEM((COND_PAD, D), BF),
            pltpu.VMEM((3, 6 * ROWS, 256), BF),
            pltpu.VMEM((3, 6 * ROWS, KEYS), F32),
            pltpu.VMEM((HEADS * ROWS, KEYS), BF),
            pltpu.VMEM((HEADS, ROWS, 128), F32),
            dma((2,)), dma((TOK_DEVS,)),
            dma((POSES,)), dma((TOK_DEVS,)),
            dma((POSES,)), dma((TOK_DEVS,)),
            dma((8,)), dma((TOK_DEVS,)),
            dma((8, 4)), dma((2,)),
            pltpu.SemaphoreType.REGULAR,
            dma((4,)), dma((2, 4)),
            dma,
            dma, dma,
            dma, dma,
            dma((2, 2)), dma((2, 2)),
            dma, dma,
            dma((8,)), dma,
        ],
        compiler_params=pltpu.CompilerParams(
            collective_id=0, has_side_effects=True, vmem_limit_bytes=60 << 20
        ),
    )(
        points, atom_single, counts, cond_single, bias, w_coord, w_in,
        w_ada[0], w_qkv[0], w_out[0], w_ff[0], w_down[0],
    )
    return rows[None]


def solution(mesh):
    return jax.shard_map(
        body,
        mesh=mesh,
        in_specs=(
            P("section", None, "tok"),
            P("tok", None),
            P("tok"),
            P("tok", None),
            P("section", None, "tok", None),
            P(),
            P(),
            P("section", None, None),
            P("section", None, None),
            P("section", None, None),
            P("section", None, None),
            P("section", None, None),
        ),
        out_specs=P("section", "tok", None),
        check_vma=False,
    )
```

```python
import jax
import jax.numpy as jnp
from jax import lax
from jax.experimental import pallas as pl
from jax.experimental.pallas import tpu as pltpu
from jax.sharding import PartitionSpec as P

HEADS = 16
HEAD_DIM = 48
FF = 1536
D = 768
POSES = 8
TOK_DEVS = 16
SECTIONS = 8
ROWS = 192
TOK_DEV = 24
ATOM_DEV = 216
ATOM_PAD = 224
COND_PAD = 32
KEYS = 384
QUARTER = 96
MESH = pl.DeviceIdType.MESH
BF = jnp.bfloat16
F32 = jnp.float32


def chip_of(pose):
    x = pose // 2
    return 4 * x + 2 * (pose % 2) + x % 2


def normalise(v):
    centre = v - jnp.mean(v, axis=-1, keepdims=True)
    return centre * lax.rsqrt(jnp.mean(centre * centre, axis=-1, keepdims=True) + 1e-05)


def landed(ref, sem):
    pltpu.make_async_copy(ref, ref, sem).wait()


def kernel(
    coords_in, atom_ref, count_in, cond_ref, bias_in, wcoord_in, win_in,
    wada_ref, wqkv_ref, wout_ref, wff_ref, wdown_ref,
    out_ref,
    coords_ref, count_ref, wcoord_ref, win_ref, fetch,
    c_src, a_src, d_src, wc, c_all, a_all, d_all, b_all, relay,
    wada_v, wqkv_v, wout_v, wff_v, wdown_v, bias_v, bias_t,
    cond, cond_tx, x, xin, xtx, norm, q, kv, att, hid, fin_tx, fin,
    spread, scores, probs, inverse,
    c_send, c_recv, a_send, a_recv, d_send, d_recv, r_send, r_recv, b_send, b_recv, go,
    w_send, w_recv, ada_sem, p_send, p_recv, m_send, m_recv, kv_send, kv_recv, x_send, x_recv, f_send, f_recv,
):
    s = lax.axis_index("section")
    t = lax.axis_index("tok")
    plane = s // 2
    core = lax.rem(s, 2)
    sibling = s + 1 - 2 * core
    cx, cz = t // 4, lax.rem(t, 4)
    active = lax.rem(cx + cz, 2) == 0
    pose = 2 * cx + cz // 2
    half = t // 8

    fetched = (
        (coords_in, coords_ref), (count_in, count_ref),
        (wcoord_in, wcoord_ref), (win_in, win_ref), (bias_in, bias_v),
    )
    for k, (src, dst) in enumerate(fetched):
        pltpu.make_async_copy(src, dst, fetch.at[k]).start()

    weights = ((wqkv_ref, wqkv_v), (wout_ref, wout_v), (wff_ref, wff_v), (wdown_ref, wdown_v))

    @pl.when(active)
    def _():
        pltpu.make_async_copy(wada_ref, wada_v, ada_sem).start()
        for k, (src, dst) in enumerate(weights):
            pltpu.make_async_copy(src, dst.at[core], w_recv.at[core, k]).start()

    barrier = pltpu.get_barrier_semaphore()

    def greet(section, tok):
        pl.semaphore_signal(barrier, inc=1, device_id=(section, tok), device_id_type=MESH)

    @pl.loop(1, TOK_DEVS)
    def _(j):
        greet(s, lax.rem(t + j, TOK_DEVS))

    def beside(k):
        step = 1 + 2 * lax.rem(k, 2)
        return jnp.where(
            k < 2, 4 * lax.rem(cx + step, 4) + cz, 4 * cx + lax.rem(cz + step, 4)
        )

    @pl.when(active)
    def _():
        @pl.loop(0, 4)
        def _(k):
            greet(sibling, beside(k))

        @pl.when((s == 0) & (pose != 0))
        def _():
            @pl.loop(0, TOK_DEVS)
            def _(j):
                greet(pose, j)

        @pl.when((s == 1) & (pose != 1))
        def _():
            greet(pose, TOK_DEVS - 1)

        @pl.when(plane > 0)
        def _():
            greet(s - 2, t)

    greet(sibling, t)

    fin_section, fin_tok = 6 + half, chip_of(s)
    fin_self = (fin_section == s) & (fin_tok == t)

    @pl.when(jnp.logical_not(fin_self))
    def _():
        greet(fin_section, fin_tok)

    for k, (src, dst) in enumerate(fetched):
        pltpu.make_async_copy(src, dst, fetch.at[k]).wait()

    @pl.when(half == 0)
    def _():
        bias_t[...] = bias_v[...]

    @pl.when(half == 1)
    def _():
        straight = bias_v[...].astype(F32)
        bias_t[...] = jnp.concatenate([straight[:, ROWS:], straight[:, :ROWS]], axis=1).astype(BF)

    c_src[...] = jnp.zeros_like(c_src)
    c_src[0:3, 0:ATOM_DEV] = coords_ref[...].reshape(3, ATOM_DEV)
    c_src[3:4, 0:TOK_DEV] = count_ref[...].astype(F32)
    wc[...] = jnp.zeros_like(wc)
    wc[0:3] = wcoord_ref[...]
    a_src[...] = jnp.concatenate(
        [atom_ref[...].astype(F32), jnp.zeros((ATOM_PAD - ATOM_DEV, 128), F32)], axis=0
    ).astype(BF)
    single = cond_ref[...].astype(F32)
    d_src[...] = jnp.concatenate([single[:, :KEYS], single[:, KEYS:]], axis=0).astype(BF)

    one = lambda flag: flag.astype(jnp.int32)
    last = t == TOK_DEVS - 1
    expected = 15 + 1 + 4 * (1 - one(active))
    expected += one(s != 0) + one(last & (s != 1))
    expected += one(active & (plane < 3))
    fin_here = active & (plane == 3)
    fin_own = fin_here & (pose == s) & (half == core)
    expected += 8 * one(fin_here) - one(fin_own)
    pl.semaphore_wait(barrier, expected)

    def send(src, dst, send_sem, recv_sem, section, tok):
        own = (section == s) & (tok == t)

        @pl.when(own)
        def _():
            pltpu.make_async_copy(src, dst, recv_sem).start()

        @pl.when(jnp.logical_not(own))
        def _():
            pltpu.make_async_remote_copy(
                src_ref=src, dst_ref=dst, send_sem=send_sem, recv_sem=recv_sem,
                device_id=(section, tok), device_id_type=MESH,
            ).start()

    def sent(src, send_sem, section, tok):
        @pl.when(jnp.logical_not((section == s) & (tok == t)))
        def _():
            landed(src, send_sem)

    send(c_src, c_all.at[t], c_send.at[0], c_recv.at[t], 0, chip_of(s))

    @pl.when(last)
    def _():
        send(c_src, c_all.at[t], c_send.at[1], c_recv.at[t], 1, chip_of(s))

    quarter = 2 * lax.rem(cx, 2) + lax.rem(cz + 2 * (cx // 2), 4) // 2

    def bias_part(k):
        return bias_t.at[pl.ds(pl.multiple_of(QUARTER * k, QUARTER), QUARTER)]

    def relay_chip(k, e):
        first = k // 2
        return 4 * (first + 2 * e) + lax.rem(2 * lax.rem(k, 2) + 1 - first + 2 * e, 4)

    def bias_out():
        @pl.loop(0, 8)
        def _(j):
            k, e = lax.rem(j, 4), j // 4
            send(bias_part(k), relay.at[t], r_send.at[j], r_recv.at[t], s, relay_chip(k, e))

    def bias_out_gone():
        @pl.loop(0, 8)
        def _(j):
            k, e = lax.rem(j, 4), j // 4
            sent(bias_part(k), r_send.at[j], s, relay_chip(k, e))

    def bias_on():
        @pl.loop(0, 8)
        def _(j):
            pair = lax.rem(t // 2 + j, 8)
            for e in range(2):
                landed(relay.at[2 * pair + e], r_recv.at[2 * pair + e])

            @pl.loop(0, 4)
            def _(k):
                pltpu.make_async_remote_copy(
                    src_ref=relay.at[pl.ds(2 * pair, 2)],
                    dst_ref=b_all.at[
                        core, pl.ds(2 * lax.rem(pair, 4), 2),
                        pl.ds(pl.multiple_of(QUARTER * quarter, QUARTER), QUARTER),
                    ],
                    send_sem=b_send.at[j, k], recv_sem=b_recv.at[core],
                    device_id=(2 * plane + pair // 4, beside(k)), device_id_type=MESH,
                ).start()

    def bias_gone(low, high):
        @pl.loop(low, high)
        def _(j):
            @pl.loop(0, 4)
            def _(k):
                landed(relay.at[pl.ds(0, 2)], b_send.at[j, k])

    def tell():
        pl.semaphore_signal(go, inc=1, device_id=(sibling, t), device_id_type=MESH)

    @pl.when(core == 0)
    def _():
        bias_out()

    @pl.when((s == 0) | ((s == 1) & last))
    def _():
        @pl.loop(0, POSES)
        def _(p):
            send(a_src, a_all.at[t], a_send.at[p], a_recv.at[t], s, chip_of(p))

    @pl.when(core == 1)
    def _():
        @pl.loop(0, POSES)
        def _(p):
            send(d_src, d_all.at[t], d_send.at[p], d_recv.at[t], s, chip_of(p))

    @pl.when(active)
    def _():
        for k, (src, dst) in enumerate(weights):
            pltpu.make_async_remote_copy(
                src_ref=src, dst_ref=dst.at[core], send_sem=w_send.at[k],
                recv_sem=w_recv.at[core, k], device_id=(sibling, t), device_id_type=MESH,
            ).start()

    @pl.when(core == 0)
    def _():
        bias_out_gone()
        tell()

    @pl.when(core == 1)
    def _():
        pl.semaphore_wait(go, 1)
        bias_out()

    @pl.when((core == 0) & jnp.logical_not(active))
    def _():
        bias_on()
        bias_gone(0, 6)
        tell()
        bias_gone(6, 8)

    @pl.when((core == 1) & jnp.logical_not(active))
    def _():
        pl.semaphore_wait(go, 1)
        bias_on()
        bias_out_gone()
        bias_gone(0, 8)

    def act_of(points, single):
        moved = lax.dot_general(
            points, wc[...], (((0,), (0,)), ((), ())),
            precision=lax.Precision.HIGHEST, preferred_element_type=F32,
        )
        return jnp.maximum(single.astype(F32) + moved[:ATOM_PAD], 0.0)

    def enter_first():
        @pl.loop(0, TOK_DEVS)
        def _(j):
            landed(c_all.at[j], c_recv.at[j])

        lane8 = lax.broadcasted_iota(jnp.int32, (TOK_DEV, 128), 1)
        place8 = lax.broadcasted_iota(jnp.int32, (TOK_DEV, 128), 0)
        count_blocks, start_blocks = [], []
        total = jnp.zeros((TOK_DEV, 1), F32)
        for j in range(8):
            row = jnp.broadcast_to(c_all[j, 3:4, 0:128], (TOK_DEV, 128))
            mine = jnp.where(lane8 == place8, row, 0.0)
            ahead = jnp.where(lane8 < place8, row, 0.0)
            count_blocks.append(jnp.sum(mine, axis=1, keepdims=True))
            start_blocks.append(total + jnp.sum(ahead, axis=1, keepdims=True))
            total = total + jnp.sum(row, axis=1, keepdims=True)
        counts = jnp.broadcast_to(jnp.concatenate(count_blocks, axis=0), (ROWS, 128))
        starts = jnp.broadcast_to(jnp.concatenate(start_blocks, axis=0), (ROWS, 128))
        ends = starts + counts
        lower = jnp.concatenate([starts, starts], axis=1)[:, :ATOM_PAD]
        upper = jnp.concatenate([ends, ends], axis=1)[:, :ATOM_PAD]
        lane = lax.broadcasted_iota(jnp.int32, (ROWS, ATOM_PAD), 1)

        @pl.loop(0, TOK_DEVS)
        def _(j):
            landed(a_all.at[j], a_recv.at[j])

        pooled = jnp.zeros((ROWS, 128), F32)
        for j in range(TOK_DEVS):
            place = (lane + j * ATOM_DEV).astype(F32)
            inside = (place >= lower) & (place < upper) & (lane < ATOM_DEV)
            member = jnp.where(inside, 1.0, 0.0).astype(BF)
            act = act_of(c_all[j], a_all[j]).astype(BF)
            pooled = pooled + jnp.dot(member, act, preferred_element_type=F32)
        averaged = (pooled / counts).astype(BF)
        x[...] = jnp.dot(averaged, win_ref[...], preferred_element_type=F32)

    def enter_second():
        j = TOK_DEVS - 1
        landed(c_all.at[j], c_recv.at[j])
        landed(a_all.at[j], a_recv.at[j])
        act = act_of(c_all[j], a_all[j])[ATOM_DEV - ROWS : ATOM_DEV]
        x[...] = jnp.dot(act.astype(BF), win_ref[...], preferred_element_type=F32)

    def conditions():
        @pl.when(core == 1)
        def _():
            @pl.loop(0, TOK_DEVS)
            def _(j):
                landed(d_all.at[j], d_recv.at[j])

            pltpu.make_async_remote_copy(
                src_ref=d_all, dst_ref=d_all, send_sem=p_send, recv_sem=p_recv,
                device_id=(sibling, t), device_id_type=MESH,
            ).start()

        @pl.when(core == 0)
        def _():
            landed(d_all, p_recv)

        landed(wada_ref, ada_sem)

        def rows_for(which, store):
            blocks = d_all[pl.ds(8 * which, 8)].astype(F32)
            norm[...] = jnp.concatenate(
                [blocks[:, :TOK_DEV].reshape(ROWS, KEYS), blocks[:, TOK_DEV:].reshape(ROWS, KEYS)],
                axis=1,
            ).astype(BF)
            for k in range(4):
                value = jnp.dot(
                    norm[...], wada_v[:, D * k : D * (k + 1)], preferred_element_type=F32
                )
                store(k, jax.nn.sigmoid(value) if k % 2 == 0 else value)

        def to_send(k, value):
            cond_tx[k] = value

        def to_keep(k, value):
            cond[core, k] = value

        rows_for(1 - core, to_send)
        pltpu.make_async_remote_copy(
            src_ref=cond_tx, dst_ref=cond.at[core], send_sem=m_send, recv_sem=m_recv,
            device_id=(sibling, t), device_id_type=MESH,
        ).start()
        rows_for(core, to_keep)

    mine, theirs = slice(0, ROWS), slice(ROWS, KEYS)

    def layer(lp):
        norm[...] = (normalise(x[...]) * cond[lp, 0] + cond[lp, 1]).astype(BF)

        def project(column, width):
            return jnp.dot(
                norm[...], wqkv_v[lp, :, column : column + width], preferred_element_type=F32
            ).astype(BF)

        for part in range(2):
            for j in range(3):
                kv[lp, part, j, mine, :] = project(D * (part + 1) + 256 * j, 256)
        pltpu.make_async_remote_copy(
            src_ref=kv.at[lp, :, :, mine], dst_ref=kv.at[lp, :, :, theirs],
            send_sem=kv_send.at[lp], recv_sem=kv_recv.at[lp],
            device_id=(sibling, t), device_id_type=MESH,
        ).start()
        for j in range(3):
            q[:, 256 * j : 256 * (j + 1)] = project(256 * j, 256)

        def spread_out(w):
            window = q[:, 256 * w : 256 * (w + 1)]
            lane = lax.broadcasted_iota(jnp.int32, (1, 256), 1) + 256 * w
            for k in range(6):
                low = HEAD_DIM * (5 * w + k)
                mask = jnp.where((lane >= low) & (lane < low + HEAD_DIM), 1.0, 0.0).astype(BF)
                spread[w, ROWS * k : ROWS * (k + 1)] = window * mask

        def score(w, first, stop):
            scores[w, :, first:stop] = lax.dot_general(
                spread[w], kv[lp, 0, w, first:stop], (((1,), (1,)), ((), ())),
                preferred_element_type=F32,
            )

        def soften(head):
            pair, e = head // 2, head % 2
            bias = b_all[lp, :, 48 * pair : 48 * (pair + 1), :].astype(F32)
            w = min(head // 5, 2)
            k = head - 5 * w
            raw = scores[w, ROWS * k : ROWS * (k + 1)]
            if k == 0 and w > 0:
                raw = raw + scores[w - 1, 5 * ROWS : 6 * ROWS]
            logits = raw * HEAD_DIM ** (-0.5) + bias[
                :, TOK_DEV * e : TOK_DEV * (e + 1)
            ].reshape(ROWS, KEYS)
            top = jnp.max(logits, axis=-1, keepdims=True)
            weight = jnp.exp(logits - top)
            total = jnp.sum(weight, axis=-1, keepdims=True)
            inverse[head] = jnp.broadcast_to(1.0 / total, (ROWS, 128))
            probs[ROWS * head : ROWS * (head + 1)] = weight.astype(BF)

        def gather(w):
            out = jnp.dot(
                probs[ROWS * 5 * w : ROWS * (5 * w + 6)], kv[lp, 1, w], preferred_element_type=F32
            )
            lane = lax.broadcasted_iota(jnp.int32, (1, 256), 1) + 256 * w
            whole = jnp.zeros((ROWS, 256), F32)
            for k in range(6):
                low = HEAD_DIM * (5 * w + k)
                factor = inverse[5 * w + k]
                piece = out[ROWS * k : ROWS * (k + 1)] * jnp.concatenate([factor, factor], axis=1)
                whole = jnp.where(lane >= low, piece, whole)
            att[:, 256 * w : 256 * (w + 1)] = whole.astype(BF)

        for w in range(3):
            spread_out(w)
            score(w, 0, 128)
        landed(kv.at[lp, :, :, theirs], kv_recv.at[lp])
        landed(b_all.at[lp], b_recv.at[lp])
        for w in range(3):
            score(w, 128, KEYS)
        for head in range(0, 6):
            soften(head)
        gather(0)
        for head in range(6, 11):
            soften(head)
        gather(1)
        for head in range(11, 16):
            soften(head)
        gather(2)

        for j in range(3):
            cols = slice(256 * j, 256 * (j + 1))
            x[:, cols] = x[:, cols] + jnp.dot(
                att[...], wout_v[lp, :, cols], preferred_element_type=F32
            )
        norm[...] = (normalise(x[...]) * cond[lp, 2] + cond[lp, 3]).astype(BF)
        for j in range(6):
            gate = jnp.dot(
                norm[...], wff_v[lp, :, 256 * j : 256 * (j + 1)], preferred_element_type=F32
            )
            up = jnp.dot(
                norm[...], wff_v[lp, :, FF + 256 * j : FF + 256 * (j + 1)],
                preferred_element_type=F32,
            )
            hid[:, 256 * j : 256 * (j + 1)] = (jax.nn.silu(gate) * up).astype(BF)
        for j in range(3):
            cols = slice(256 * j, 256 * (j + 1))
            state = x[:, cols] + jnp.dot(
                hid[...], wdown_v[lp, :, cols], preferred_element_type=F32
            )
            x[:, cols] = state
            xtx[:, cols] = state.astype(BF)

    @pl.when(active)
    def _():
        conditions()

        @pl.when(s == 0)
        def _():
            enter_first()

        @pl.when(s == 1)
        def _():
            enter_second()

        for k, (src, dst) in enumerate(weights):
            for lp in range(2):
                landed(dst.at[lp], w_recv.at[lp, k])
        landed(cond.at[1 - core], m_recv)

        @pl.when(plane > 0)
        def _():
            landed(xin, x_recv)
            x[...] = xin[...].astype(F32)

        @pl.loop(0, 2)
        def _(lp):
            layer(lp)

        @pl.when(plane < 3)
        def _():
            pltpu.make_async_remote_copy(
                src_ref=xtx, dst_ref=xin, send_sem=x_send, recv_sem=x_recv,
                device_id=(s + 2, t), device_id_type=MESH,
            ).start()

        @pl.when(plane == 3)
        def _():
            done = normalise(x[...]).reshape(8, TOK_DEV, D)
            fin_tx[...] = jnp.concatenate(
                [done, jnp.zeros((8, COND_PAD - TOK_DEV, D), F32)], axis=1
            ).astype(BF)

            @pl.loop(0, 8)
            def _(j):
                send(fin_tx.at[j], fin, f_send.at[j], f_recv, pose, 8 * core + j)

    landed(fin, f_recv)
    out_ref[...] = fin[...].astype(F32)[:TOK_DEV].astype(BF)

    sent(c_src, c_send.at[0], 0, chip_of(s))

    @pl.when(last)
    def _():
        sent(c_src, c_send.at[1], 1, chip_of(s))

    @pl.when((s == 0) | ((s == 1) & last))
    def _():
        @pl.loop(0, POSES)
        def _(p):
            sent(a_src, a_send.at[p], s, chip_of(p))

    @pl.when(core == 1)
    def _():
        @pl.loop(0, POSES)
        def _(p):
            sent(d_src, d_send.at[p], s, chip_of(p))

    @pl.when(active)
    def _():
        for k, (src, dst) in enumerate(weights):
            landed(src, w_send.at[k])
        landed(cond_tx, m_send)

        @pl.loop(0, 2)
        def _(lp):
            landed(kv.at[lp, :, :, mine], kv_send.at[lp])

        @pl.when(core == 1)
        def _():
            landed(d_all, p_send)
            bias_out_gone()


        @pl.when(plane < 3)
        def _():
            landed(xtx, x_send)

        @pl.when(plane == 3)
        def _():
            @pl.loop(0, 8)
            def _(j):
                sent(fin_tx.at[j], f_send.at[j], pose, 8 * core + j)


def body(
    coords, atom_single, token_atoms, cond_single, pair_bias, w_coord, w_in,
    w_ada, w_qkv, w_out, w_ff, w_down,
):
    counts = token_atoms.reshape(1, TOK_DEV)
    points = jnp.transpose(coords, (1, 0, 2))
    bias = pair_bias[0].reshape(HEADS * TOK_DEV, KEYS)
    vmem = pl.BlockSpec(memory_space=pltpu.VMEM)
    hbm = pl.BlockSpec(memory_space=pl.ANY)
    dma = pltpu.SemaphoreType.DMA
    rows = pl.pallas_call(
        kernel,
        out_shape=jax.ShapeDtypeStruct((TOK_DEV, D), BF),
        in_specs=[hbm, vmem, hbm, vmem] + [hbm] * 8,
        out_specs=vmem,
        scratch_shapes=[
            pltpu.VMEM((3, 1, ATOM_DEV), F32),
            pltpu.VMEM((1, TOK_DEV), jnp.int32),
            pltpu.VMEM((3, 128), F32),
            pltpu.VMEM((128, D), BF),
            dma((5,)),
            pltpu.VMEM((8, 256), F32),
            pltpu.VMEM((ATOM_PAD, 128), BF),
            pltpu.VMEM((2 * TOK_DEV, KEYS), BF),
            pltpu.VMEM((8, 128), F32),
            pltpu.VMEM((TOK_DEVS, 8, 256), F32),
            pltpu.VMEM((TOK_DEVS, ATOM_PAD, 128), BF),
            pltpu.VMEM((TOK_DEVS, 2 * TOK_DEV, KEYS), BF),
            pltpu.VMEM((2, 8, HEADS * TOK_DEV, KEYS), BF),
            pltpu.VMEM((TOK_DEVS, QUARTER, KEYS), BF),
            pltpu.VMEM((D, 4 * D), BF),
            pltpu.VMEM((2, D, 3 * D), BF),
            pltpu.VMEM((2, D, D), BF),
            pltpu.VMEM((2, D, 2 * FF), BF),
            pltpu.VMEM((2, FF, D), BF),
            pltpu.VMEM((HEADS * TOK_DEV, KEYS), BF),
            pltpu.VMEM((HEADS * TOK_DEV, KEYS), BF),
            pltpu.VMEM((2, 4, ROWS, D), F32),
            pltpu.VMEM((4, ROWS, D), F32),
            pltpu.VMEM((ROWS, D), F32),
            pltpu.VMEM((ROWS, D), BF),
            pltpu.VMEM((ROWS, D), BF),
            pltpu.VMEM((ROWS, D), BF),
            pltpu.VMEM((ROWS, D), BF),
            pltpu.VMEM((2, 2, 3, KEYS, 256), BF),
            pltpu.VMEM((ROWS, D), BF),
            pltpu.VMEM((ROWS, FF), BF),
            pltpu.VMEM((8, COND_PAD, D), BF),
            pltpu.VMEM((COND_PAD, D), BF),
            pltpu.VMEM((3, 6 * ROWS, 256), BF),
            pltpu.VMEM((3, 6 * ROWS, KEYS), F32),
            pltpu.VMEM((HEADS * ROWS, KEYS), BF),
            pltpu.VMEM((HEADS, ROWS, 128), F32),
            dma((2,)), dma((TOK_DEVS,)),
            dma((POSES,)), dma((TOK_DEVS,)),
            dma((POSES,)), dma((TOK_DEVS,)),
            dma((8,)), dma((TOK_DEVS,)),
            dma((8, 4)), dma((2,)),
            pltpu.SemaphoreType.REGULAR,
            dma((4,)), dma((2, 4)),
            dma,
            dma, dma,
            dma, dma,
            dma((2,)), dma((2,)),
            dma, dma,
            dma((8,)), dma,
        ],
        compiler_params=pltpu.CompilerParams(
            collective_id=0, has_side_effects=True, vmem_limit_bytes=60 << 20
        ),
    )(
        points, atom_single, counts, cond_single, bias, w_coord, w_in,
        w_ada[0], w_qkv[0], w_out[0], w_ff[0], w_down[0],
    )
    return rows[None]


def solution(mesh):
    return jax.shard_map(
        body,
        mesh=mesh,
        in_specs=(
            P("section", None, "tok"),
            P("tok", None),
            P("tok"),
            P("tok", None),
            P("section", None, "tok", None),
            P(),
            P(),
            P("section", None, None),
            P("section", None, None),
            P("section", None, None),
            P("section", None, None),
            P("section", None, None),
        ),
        out_specs=P("section", "tok", None),
        check_vma=False,
    )
```
